32 devices in a mesh: dp: 8 (over y, x, core), mp: 4 (over z).
Axes of the slice: x: 2, y: 2, z: 4, core: 2. Of those that a mesh axis runs over, the one named last changes fastest.
Arguments:
- tokens: bfloat16 [3, 8192, 1024], P(None, ('dp', 'mp')), may hold values from -6 to 6
- first_values: bfloat16 [3, 8192, 1024], P(None, ('dp', 'mp')), may hold values from -6 to 6
- sequences: int32 [3, 8], P(None, 'dp'), may hold values from 1 to 2
- w_query: bfloat16 [1024, 1024], P('dp', 'mp'), may hold values from -0.1875 to 0.1875
- w_key: bfloat16 [1024, 1024], P('dp', 'mp'), may hold values from -0.1875 to 0.1875
- w_value: bfloat16 [1024, 1024], P('dp', 'mp'), may hold values from -0.1875 to 0.1875
- w_out: bfloat16 [1024, 1024], P('dp', 'mp'), may hold values from -4 to 4
- w_gate: bfloat16 [1024, 2816], P('dp', 'mp'), may hold values from -0.1875 to 0.1875
- w_up: bfloat16 [1024, 2816], P('dp', 'mp'), may hold values from -0.1875 to 0.1875
- w_down: bfloat16 [1024, 2816], P('dp', 'mp'), may hold values from -0.109375 to 0.109375
- gain_attn: bfloat16 [1024], P('dp'), may hold values from 0.5 to 1.5
- gain_mlp: bfloat16 [1024], P('dp'), may hold values from 0.5 to 1.5
- cotangent: bfloat16 [3, 8192, 1024], P(None, ('dp', 'mp')), may hold values from -6 to 6
Outputs:
- layer_out: bfloat16 [3, 8192, 1024], P(None, ('dp', 'mp'))
- grad_tokens: float32 [3, 8192, 1024], P(None, ('dp', 'mp'))
- grad_first_values: float32 [3, 8192, 1024], P(None, ('dp', 'mp'))
- grad_w_query: float32 [1024, 1024], P('dp', 'mp')
- grad_w_key: float32 [1024, 1024], P('dp', 'mp')
- grad_w_value: float32 [1024, 1024], P('dp', 'mp')
- grad_w_out: float32 [1024, 1024], P('dp', 'mp')
- grad_w_gate: float32 [1024, 2816], P('dp', 'mp')
- grad_w_up: float32 [1024, 2816], P('dp', 'mp')
- grad_w_down: float32 [1024, 2816], P('dp', 'mp')
- grad_gain_attn: float32 [1024], P(('dp', 'mp'))
- grad_gain_mlp: float32 [1024], P(('dp', 'mp'))
The draws below stay inside these ranges and needn't reach their ends.
Inputs may be any that keep to these rules, and one draw needn't show every extreme that they name: A block with 1 holds one sequence of 1024 tokens; a block with 2 holds two sequences of 512 tokens, the second starting at the block's middle.
All inputs are finite; a program needn't handle non-finite values.
Results may differ from the reference program's by a relative error of at most 0.023.
Values may be sent and summed in bfloat16 or wider, within the bound.
A program may use at most 320 MiB of HBM per device.

```python
import jax
import jax.numpy as jnp
from jax import lax

HEADS = 16
HEAD_DIM = 64
D = 1024
FF = 2816
SEQ = 1024
MICRO = 3
ROWS = 8192
N_DP = 8


def plant(entries, own_key, smallest, top_value):
    extent = entries.shape
    spot = [jax.random.randint(jax.random.fold_in(own_key, axis), (), 0, extent[axis]) for axis in range(len(extent))]
    entries = entries.at[tuple(spot)].set(smallest)
    longest = extent.index(max(extent))
    spot[longest] = (spot[longest] + 1) % extent[longest]
    return entries.at[tuple(spot)].set(top_value)


def strengthened(entries, rng, source, target, blocks, factor):
    def block_of(axis_at):
        return (jnp.arange(entries.shape[axis_at]) // (entries.shape[axis_at] // blocks)).reshape((-1,) + (1,) * (entries.ndim - 1 - axis_at))

    one_side = jax.random.permutation(rng, blocks)[block_of(target)]
    far = (block_of(target) + blocks // 2) % blocks
    return jnp.where((block_of(source) == one_side) | (block_of(source) == far), factor * entries, entries)


def block_scale(own_key, shape, pieces, low, largest):
    factor_of, own = 1.0, jax.random.fold_in(own_key, 6)
    for dim, blocks in pieces:
        steps = jnp.exp(jax.random.uniform(jax.random.fold_in(own, dim), (blocks,), jnp.float32, low / len(pieces), largest / len(pieces)))
        factor_of = factor_of * jnp.repeat(steps, shape[dim] // blocks).reshape([-1 if axis == dim else 1 for axis in range(len(shape))])
    return factor_of


def scatter_about(stream_key, extent, spread, bound, cuts=(), kind=jnp.bfloat16):
    result = jax.random.normal(stream_key, extent, jnp.float32) * spread
    if len(cuts) > 0:
        result = block_scale(stream_key, extent, cuts, -0.22, 0.18) * result
    return jnp.clip(result, min=-bound, max=bound).astype(kind)


def noise_with(rng, shape, spread, reach, cuts, heavy, held_as=jnp.bfloat16):
    result = spread * jax.random.normal(rng, shape, jnp.float32)
    if cuts:
        result = result * block_scale(rng, shape, cuts, -0.22, 0.18)
    return jnp.clip(strengthened(result, jax.random.fold_in(rng, 3), *heavy), -reach, reach).astype(held_as)


def setup_inputs(seed: int = 0) -> dict:
    streams_of = jax.random.split(jax.random.key(seed), 14)
    tokens = scatter_about(streams_of[0], (MICRO, ROWS, D), 1.0, 6.0, ((1, 32),))
    first_values = scatter_about(streams_of[1], (MICRO, ROWS, D), 1.0, 6.0, ((1, 32),))
    sequences = plant(jax.random.randint(streams_of[2], (MICRO, N_DP), 1, 3), jax.random.fold_in(streams_of[2], 1), 1, 2).astype(jnp.int32)
    w_query = scatter_about(streams_of[3], (D, D), D ** -0.5, 0.1875, ((0, 8), (1, 4)))
    w_key = scatter_about(streams_of[4], (D, D), D ** -0.5, 0.1875, ((0, 8), (1, 4)))
    w_value = scatter_about(streams_of[5], (D, D), D ** -0.5, 0.1875, ((0, 8), (1, 4)))
    w_out = scatter_about(streams_of[6], (D, D), (max(1, 2 * D // SEQ)) ** -0.5, 4.0, ((0, 8), (1, 4)))
    w_gate = scatter_about(streams_of[7], (D, FF), D ** -0.5, 0.1875, ((0, 8), (1, 4)))
    w_up = scatter_about(streams_of[8], (D, FF), D ** -0.5, 0.1875, ((0, 8), (1, 4)))
    w_down = scatter_about(streams_of[9], (D, FF), FF ** -0.5, 0.109375, ((0, 8), (1, 4)))
    gain_attn = jnp.clip(1.0 + 0.1 * jax.random.normal(streams_of[10], (D,), jnp.float32), 0.5, 1.5).astype(jnp.bfloat16)
    gain_mlp = jnp.clip(1.0 + 0.1 * jax.random.normal(streams_of[11], (D,), jnp.float32), 0.5, 1.5).astype(jnp.bfloat16)
    cotangent = noise_with(streams_of[12], (MICRO, ROWS, D), 1.0, 6.0, ((1, 32),), (1, 2, 32, 2.75))
    return dict(tokens=tokens, first_values=first_values, sequences=sequences, w_query=w_query, w_key=w_key, w_value=w_value, w_out=w_out, w_gate=w_gate, w_up=w_up, w_down=w_down, gain_attn=gain_attn, gain_mlp=gain_mlp, cotangent=cotangent)


@jax.custom_vjp
def low(v):
    return lax.optimization_barrier(v.astype(jnp.bfloat16)).astype(jnp.float32)

@jax.custom_vjp
def low_back(v):
    return v

def low_keep(v):
    return (low(v), None)

def low_pass(kept, grad):
    return (grad,)

def back_keep(v):
    return (v, None)

def back_low(kept, grad):
    return (low(grad),)
low.defvjp(low_keep, low_pass)
low_back.defvjp(back_keep, back_low)
EPSILON = 1e-06
THETA = 10000.0

def matmul(left, right):
    return jnp.dot(left, right, precision=lax.Precision.HIGHEST, preferred_element_type=jnp.float32)

def normalize(rows):
    return rows * lax.rsqrt(lax.optimization_barrier(jnp.mean(rows * rows, axis=-1, keepdims=True)) + EPSILON)

def rotary_tables(position, head_size):
    halfway = head_size // 2
    inverse = THETA ** (-2.0 * jnp.arange(halfway, dtype=jnp.float32) / head_size)
    angles = position.astype(jnp.float32)[:, None] * inverse[None, :]
    return (jnp.cos(angles), jnp.sin(angles))

def rotate(values, cosine, sine, direction):
    halfway = values.shape[-1] // 2
    former = values[..., :halfway]
    latter = values[..., halfway:]
    cos_rows = cosine[:, None, :]
    sin_rows = direction * sine[:, None, :]
    return jnp.concatenate([former * cos_rows - latter * sin_rows, latter * cos_rows + former * sin_rows], axis=-1)

def layout(packed, length):
    index_rows = jnp.arange(length, dtype=jnp.int32)
    second = jnp.where((packed == 2) & (index_rows >= length // 2), 1, 0).astype(jnp.int32)
    return (second, index_rows - second * (length // 2))

def layer(weights, x_rows, first_rows, packed):
    w_query, w_key, w_value, w_out, w_gate, w_up, w_down, gain_attn, gain_mlp = weights
    second, position = layout(packed, SEQ)
    cosine, sine = rotary_tables(position, HEAD_DIM)
    input_one = low(normalize(x_rows) * gain_attn[None, :])
    query = low_back(matmul(input_one, w_query)).reshape(SEQ, HEADS, HEAD_DIM)
    key_rows = low_back(matmul(input_one, w_key)).reshape(SEQ, HEADS, HEAD_DIM)
    value_rows = matmul(input_one, w_value)
    query = low(rotate(query, cosine, sine, 1.0))
    key_rows = low(rotate(key_rows, cosine, sine, 1.0))
    mixed = low(low_back(0.5 * (value_rows + first_rows))).reshape(SEQ, HEADS, HEAD_DIM)
    scores = jnp.einsum('qhd,khd->hqk', query, key_rows, precision=lax.Precision.HIGHEST) * HEAD_DIM ** (-0.5)
    scores = low_back(scores)
    row_ids = jnp.arange(SEQ, dtype=jnp.int32)
    allowed = (row_ids[None, :] <= row_ids[:, None]) & (second[:, None] == second[None, :])
    scores = jnp.where(allowed[None], scores, -1e+30)
    highest = lax.optimization_barrier(jnp.max(scores, axis=-1, keepdims=True))
    powers = jnp.exp(scores - highest)
    probs = low(powers / lax.optimization_barrier(jnp.sum(powers, axis=-1, keepdims=True)))
    attended = jnp.einsum('hqk,khd->qhd', probs, mixed, precision=lax.Precision.HIGHEST)
    attended = low(low_back(attended)).reshape(SEQ, HEADS * HEAD_DIM)
    mid_rows = x_rows + low_back(matmul(attended, w_out.T))
    input_two = low(normalize(mid_rows) * gain_mlp[None, :])
    gate = low_back(matmul(input_two, w_gate))
    upward = low_back(matmul(input_two, w_up))
    hidden = low(jax.nn.silu(gate) * upward)
    return mid_rows + low_back(matmul(hidden, w_down.T))

def reference(tokens, first_values, sequences, w_query, w_key, w_value, w_out, w_gate, w_up, w_down, gain_attn, gain_mlp, cotangent):
    weights = tuple((item.astype(jnp.float32) for item in (w_query, w_key, w_value, w_out, w_gate, w_up, w_down, gain_attn, gain_mlp)))
    blocks = MICRO * N_DP
    x_blocks = tokens.astype(jnp.float32).reshape(blocks, SEQ, D)
    first_blocks = first_values.astype(jnp.float32).reshape(blocks, SEQ, D)
    packed_blocks = sequences.reshape(blocks).astype(jnp.int32)
    step = jax.checkpoint(layer)

    def forward(weights, x_blocks, first_blocks):

        def visit(carry, item):
            return (carry, step(weights, item[0], item[1], item[2]))
        _, outputs = lax.scan(visit, jnp.zeros((), jnp.float32), (x_blocks, first_blocks, packed_blocks))
        return outputs
    outputs, pullback = jax.vjp(forward, weights, x_blocks, first_blocks)
    grad_weights, grad_x, grad_first = pullback(cotangent.astype(jnp.float32).reshape(blocks, SEQ, D))
    return (outputs.reshape(MICRO, ROWS, D).astype(jnp.bfloat16), grad_x.reshape(MICRO, ROWS, D), grad_first.reshape(MICRO, ROWS, D), grad_weights[0], grad_weights[1], grad_weights[2], grad_weights[3], grad_weights[4], grad_weights[5], grad_weights[6], grad_weights[7], grad_weights[8])
```

```python
import jax
import jax.numpy as jnp
import numpy as np
from jax import lax
from jax.experimental import pallas as pl
from jax.experimental.pallas import tpu as pltpu
from jax.sharding import PartitionSpec as P

HEAD_DIM = 64


EPSILON = 1e-06
THETA = 10000.0


def normalize(rows):
    factor = lax.rsqrt(jnp.mean(rows * rows, axis=-1, keepdims=True) + EPSILON)
    return (rows * factor, factor)


def norm_back(grad_normed, normed, factor):
    return factor * (grad_normed - normed * jnp.mean(grad_normed * normed, axis=-1, keepdims=True))


def rotary_tables(position, head_size):
    halfway = head_size // 2
    inverse = THETA ** (-2.0 * jnp.arange(halfway, dtype=jnp.float32) / head_size)
    angles = position.astype(jnp.float32)[:, None] * inverse[None, :]
    return (jnp.cos(angles), jnp.sin(angles))


def rotate(values, cosine, sine, direction):
    halfway = values.shape[-1] // 2
    former = values[..., :halfway]
    latter = values[..., halfway:]
    cos_rows = cosine[:, None, :]
    sin_rows = direction * sine[:, None, :]
    return jnp.concatenate(
        [former * cos_rows - latter * sin_rows, latter * cos_rows + former * sin_rows], axis=-1
    )


def layout(packed, length):
    index_rows = jnp.arange(length, dtype=jnp.int32)
    second = jnp.where((packed == 2) & (index_rows >= length // 2), 1, 0).astype(jnp.int32)
    return (second, index_rows - second * (length // 2))


def block_scores(query, key_rows, second, offset, block_rows, key_end, scale):
    raw = (
        jnp.einsum(
            "qhd,khd->hqk",
            query[offset : offset + block_rows],
            key_rows,
            preferred_element_type=jnp.float32,
        )
        * scale
    )
    row_ids = offset + jnp.arange(block_rows, dtype=jnp.int32)
    col_ids = jnp.arange(key_end, dtype=jnp.int32)
    allowed = (col_ids[None, :] <= row_ids[:, None]) & (
        second[offset : offset + block_rows][:, None] == second[None, :]
    )
    return jnp.where(allowed[None], raw, -1e30)


def whole_rows(part):
    return lax.all_gather(part, "mp", axis=0, tiled=True)


def summed_rows(term, local_rows):
    return lax.psum_scatter(
        term(jnp.int32(0), local_rows * lax.axis_size("mp")).astype(jnp.bfloat16),
        "mp",
        scatter_dimension=0,
        tiled=True,
    ).astype(jnp.float32)


def fetch(w_query, w_key, w_value, w_out, w_gate, w_up, w_down, gain_attn, gain_mlp):
    return (
        lax.all_gather(w_query, "dp", axis=0, tiled=True),
        lax.all_gather(w_key, "dp", axis=0, tiled=True),
        lax.all_gather(w_value, "dp", axis=0, tiled=True),
        lax.all_gather(w_out, "dp", axis=0, tiled=True),
        lax.all_gather(w_gate, "dp", axis=0, tiled=True),
        lax.all_gather(w_up, "dp", axis=0, tiled=True),
        lax.all_gather(w_down, "dp", axis=0, tiled=True),
        lax.all_gather(gain_attn, "dp", axis=0, tiled=True),
        lax.all_gather(gain_mlp, "dp", axis=0, tiled=True),
    )


def project_back(left, right):
    return jnp.einsum("rc,dc->rd", left, right, preferred_element_type=jnp.float32)


def outer_sum(left, right):
    return jnp.einsum("td,tc->dc", left, right, preferred_element_type=jnp.float32)


def body(
    tokens,
    first_values,
    sequences,
    w_query,
    w_key,
    w_value,
    w_out,
    w_gate,
    w_up,
    w_down,
    gain_attn,
    gain_mlp,
    cotangent,
):
    micro = tokens.shape[0]
    local_rows = tokens.shape[1]
    length = local_rows * lax.axis_size("mp")
    heads_here = w_query.shape[1] // HEAD_DIM
    block_rows = min(512, length)
    scale = HEAD_DIM ** (-0.5)
    saved = []
    outputs = []
    for batch in range(micro):
        full = fetch(w_query, w_key, w_value, w_out, w_gate, w_up, w_down, gain_attn, gain_mlp)
        q_full, k_full, v_full, o_full, gate_full, up_full, down_full, gain_one, gain_two = full
        gain_one = gain_one.astype(jnp.float32)
        gain_two = gain_two.astype(jnp.float32)
        x_rows = tokens[batch].astype(jnp.float32)
        normed_one, factor_one = normalize(x_rows)
        input_one = whole_rows((normed_one * gain_one[None, :]).astype(jnp.bfloat16))
        second, position = layout(sequences[batch, 0], length)
        cosine, sine = rotary_tables(position, HEAD_DIM)
        query = jnp.dot(input_one, q_full, preferred_element_type=jnp.float32).reshape(
            length, heads_here, HEAD_DIM
        )
        query = rotate(query, cosine, sine, 1.0).astype(jnp.bfloat16)
        key_rows = jnp.dot(input_one, k_full, preferred_element_type=jnp.float32).reshape(
            length, heads_here, HEAD_DIM
        )
        key_rows = rotate(key_rows, cosine, sine, 1.0).astype(jnp.bfloat16)
        first_here = lax.all_to_all(
            first_values[batch], "mp", split_axis=1, concat_axis=0, tiled=True
        )
        mixed = 0.5 * (
            jnp.dot(input_one, v_full, preferred_element_type=jnp.float32)
            + first_here.astype(jnp.float32)
        )
        mixed = mixed.astype(jnp.bfloat16).reshape(length, heads_here, HEAD_DIM)
        pieces = []
        logsums = []
        for offset in range(0, length, block_rows):
            key_end = length
            scores = block_scores(query, key_rows, second, offset, block_rows, key_end, scale)
            highest = jnp.max(scores, axis=-1, keepdims=True)
            powers = jnp.exp(scores - highest)
            denominator = jnp.sum(powers, axis=-1, keepdims=True)
            probs_low = (powers / denominator).astype(jnp.bfloat16)
            logsums.append(highest + jnp.log(denominator))
            pieces.append(
                jnp.einsum("hqk,khd->qhd", probs_low, mixed, preferred_element_type=jnp.float32)
            )
        attended = (
            jnp.concatenate(pieces, axis=0)
            .reshape(length, heads_here * HEAD_DIM)
            .astype(jnp.bfloat16)
        )

        def attn_term(offset, amount):
            return project_back(attended, o_full)

        mid_rows = x_rows + summed_rows(attn_term, local_rows)
        normed_two, factor_two = normalize(mid_rows)
        input_two = whole_rows((normed_two * gain_two[None, :]).astype(jnp.bfloat16))
        gate = jnp.dot(input_two, gate_full, preferred_element_type=jnp.float32)
        upward = jnp.dot(input_two, up_full, preferred_element_type=jnp.float32)
        sigma = jax.nn.sigmoid(gate)
        hidden = (gate * sigma * upward).astype(jnp.bfloat16)

        def mlp_term(offset, amount):
            return project_back(hidden, down_full)

        mlp_rows = summed_rows(mlp_term, local_rows)
        outputs.append((mid_rows + mlp_rows).astype(jnp.bfloat16))
        saved.append(
            (
                normed_one,
                factor_one,
                input_one,
                second,
                cosine,
                sine,
                query,
                key_rows,
                mixed,
                logsums,
                attended,
                normed_two,
                factor_two,
                input_two,
                gate,
                sigma,
                upward,
                hidden,
            )
        )
    grad_sum = None
    gain_grad_one = jnp.zeros((tokens.shape[2],), jnp.float32)
    gain_grad_two = jnp.zeros((tokens.shape[2],), jnp.float32)
    grad_tokens = []
    grad_first = []
    for batch in range(micro):
        (
            normed_one,
            factor_one,
            input_one,
            second,
            cosine,
            sine,
            query,
            key_rows,
            mixed,
            logsums,
            attended,
            normed_two,
            factor_two,
            input_two,
            gate,
            sigma,
            upward,
            hidden,
        ) = saved[batch]
        full = fetch(w_query, w_key, w_value, w_out, w_gate, w_up, w_down, gain_attn, gain_mlp)
        q_full, k_full, v_full, o_full, gate_full, up_full, down_full, gain_one, gain_two = full
        gain_one = gain_one.astype(jnp.float32)
        gain_two = gain_two.astype(jnp.float32)
        grad_rows = cotangent[batch]
        grad_full = whole_rows(grad_rows)
        grad_down = outer_sum(grad_full, hidden)
        grad_hidden = jnp.dot(grad_full, down_full, preferred_element_type=jnp.float32)
        grad_gate = (grad_hidden * upward * sigma * (1.0 + gate * (1.0 - sigma))).astype(
            jnp.bfloat16
        )
        grad_up = (grad_hidden * gate * sigma).astype(jnp.bfloat16)
        grad_gate_w = outer_sum(input_two, grad_gate)
        grad_up_w = outer_sum(input_two, grad_up)

        def mlp_back(offset, amount):
            return project_back(grad_gate, gate_full) + project_back(grad_up, up_full)

        grad_input_two = summed_rows(mlp_back, local_rows)
        gain_grad_two = gain_grad_two + jnp.sum(grad_input_two * normed_two, axis=0)
        grad_mid = grad_rows.astype(jnp.float32) + norm_back(
            grad_input_two * gain_two[None, :], normed_two, factor_two
        )
        grad_attn = whole_rows(grad_mid.astype(jnp.bfloat16))
        grad_out_w = outer_sum(grad_attn, attended)
        grad_attended = jnp.dot(grad_attn, o_full, preferred_element_type=jnp.float32)
        grad_attended = grad_attended.astype(jnp.bfloat16).reshape(length, heads_here, HEAD_DIM)
        grad_mixed = jnp.zeros((length, heads_here, HEAD_DIM), jnp.float32)
        grad_key = jnp.zeros((length, heads_here, HEAD_DIM), jnp.float32)
        query_parts = []
        for turn, offset in enumerate(range(0, length, block_rows)):
            key_end = length
            scores = block_scores(query, key_rows, second, offset, block_rows, key_end, scale)
            probs = jnp.exp(scores - logsums[turn])
            grad_block = grad_attended[offset : offset + block_rows]
            grad_probs = jnp.einsum(
                "qhd,khd->hqk", grad_block, mixed, preferred_element_type=jnp.float32
            )
            grad_mixed = grad_mixed.at[:key_end].add(
                jnp.einsum(
                    "hqk,qhd->khd",
                    probs.astype(jnp.bfloat16),
                    grad_block,
                    preferred_element_type=jnp.float32,
                )
            )
            grad_scores = probs * (grad_probs - jnp.sum(probs * grad_probs, axis=-1, keepdims=True))
            grad_scores = grad_scores.astype(jnp.bfloat16)
            query_parts.append(
                jnp.einsum(
                    "hqk,khd->qhd", grad_scores, key_rows, preferred_element_type=jnp.float32
                )
                * scale
            )
            grad_key = grad_key.at[:key_end].add(
                jnp.einsum(
                    "hqk,qhd->khd",
                    grad_scores,
                    query[offset : offset + block_rows],
                    preferred_element_type=jnp.float32,
                )
                * scale
            )
        grad_mixed_low = grad_mixed.reshape(length, heads_here * HEAD_DIM).astype(jnp.bfloat16)
        grad_value = (0.5 * grad_mixed_low.astype(jnp.float32)).astype(jnp.bfloat16)
        grad_query = rotate(jnp.concatenate(query_parts, axis=0), cosine, sine, -1.0)
        grad_query = grad_query.reshape(length, heads_here * HEAD_DIM).astype(jnp.bfloat16)
        grad_key_low = (
            rotate(grad_key, cosine, sine, -1.0)
            .reshape(length, heads_here * HEAD_DIM)
            .astype(jnp.bfloat16)
        )
        grad_query_w = outer_sum(input_one, grad_query)
        grad_key_w = outer_sum(input_one, grad_key_low)
        grad_value_w = outer_sum(input_one, grad_value)

        def attn_back(offset, amount):
            return (
                project_back(grad_query, q_full)
                + project_back(grad_key_low, k_full)
                + project_back(grad_value, v_full)
            )

        grad_input_one = summed_rows(attn_back, local_rows)
        gain_grad_one = gain_grad_one + jnp.sum(grad_input_one * normed_one, axis=0)
        grad_tokens.append(
            grad_mid + norm_back(grad_input_one * gain_one[None, :], normed_one, factor_one)
        )
        returned = lax.all_to_all(grad_mixed_low, "mp", split_axis=0, concat_axis=1, tiled=True)
        grad_first.append(0.5 * returned.astype(jnp.float32))
        shared = (
            lax.psum_scatter(
                grad_query_w.astype(jnp.bfloat16), "dp", scatter_dimension=0, tiled=True
            ).astype(jnp.float32),
            lax.psum_scatter(
                grad_key_w.astype(jnp.bfloat16), "dp", scatter_dimension=0, tiled=True
            ).astype(jnp.float32),
            lax.psum_scatter(
                grad_value_w.astype(jnp.bfloat16), "dp", scatter_dimension=0, tiled=True
            ).astype(jnp.float32),
            lax.psum_scatter(
                grad_out_w.astype(jnp.bfloat16), "dp", scatter_dimension=0, tiled=True
            ).astype(jnp.float32),
            lax.psum_scatter(
                grad_gate_w.astype(jnp.bfloat16), "dp", scatter_dimension=0, tiled=True
            ).astype(jnp.float32),
            lax.psum_scatter(
                grad_up_w.astype(jnp.bfloat16), "dp", scatter_dimension=0, tiled=True
            ).astype(jnp.float32),
            lax.psum_scatter(
                grad_down.astype(jnp.bfloat16), "dp", scatter_dimension=0, tiled=True
            ).astype(jnp.float32),
        )
        grad_sum = shared if grad_sum is None else jax.tree.map(jnp.add, grad_sum, shared)
    gain_parts = (
        lax.psum_scatter(gain_grad_one, ("dp", "mp"), scatter_dimension=0, tiled=True),
        lax.psum_scatter(gain_grad_two, ("dp", "mp"), scatter_dimension=0, tiled=True),
    )
    return (
        jnp.stack(outputs),
        jnp.stack(grad_tokens),
        jnp.stack(grad_first),
        grad_sum[0],
        grad_sum[1],
        grad_sum[2],
        grad_sum[3],
        grad_sum[4],
        grad_sum[5],
        grad_sum[6],
        gain_parts[0],
        gain_parts[1],
    )


def rope_tables():
    half = HEAD_DIM // 2
    inverse = THETA ** (-2.0 * jnp.arange(half, dtype=jnp.float32) / HEAD_DIM)
    angles = jnp.arange(1024, dtype=jnp.int32).astype(jnp.float32)[:, None] * inverse[None, :]
    cosine, sine = jnp.cos(angles), jnp.sin(angles)
    return (
        jnp.concatenate([cosine] * 4, axis=1),
        jnp.concatenate([-sine, sine, -sine, sine], axis=1),
    )


BF = jnp.bfloat16
F32 = jnp.float32
MESH = pl.DeviceIdType.MESH
CHUNK = 256
HP = 768
PADW = 2560
QROWS = 400


def remote(src, dst, send, recv, device):
    return pltpu.make_async_remote_copy(
        src_ref=src, dst_ref=dst, send_sem=send, recv_sem=recv, device_id=device, device_id_type=MESH
    )


class Place:
    def __init__(self):
        self.d = d = lax.axis_index("dp")
        self.z = z = lax.axis_index("mp")
        core = lax.rem(d, 2)
        along_x = lax.rem(lax.div(d, 2), 2)
        along_y = lax.div(d, 4)
        self.dc = d + 1 - 2 * core
        self.dx = d + 2 - 4 * along_x
        self.dy = d + 4 - 8 * along_y
        self.dxy = self.dx + 4 - 8 * along_y
        self.core = (self.dc, z)
        self.x = (self.dx, z)
        self.y = (self.dy, z)
        self.quads = (d, self.dx, self.dy, self.dxy)
        self.core_quads = tuple(q + 1 - 2 * core for q in self.quads)

    def peer(self, step):
        return lax.rem(self.z + step, 4)

    def greet(self):
        barrier = pltpu.get_barrier_semaphore()
        others = [self.core, self.x, self.y] + [(self.d, self.peer(s)) for s in (1, 2, 3)]
        for other in others:
            pl.semaphore_signal(barrier, inc=1, device_id=other, device_id_type=MESH)
        pl.semaphore_wait(barrier, len(others))

    def hop(self, step, visit):
        for sign in (1, -1):
            m = self.z + sign * step

            @pl.when((m >= 0) & (m <= 3))
            def _():
                visit(m)


class Gather:
    def __init__(self, place, at, own, sems):
        self.p, self.at, self.own = place, at, own
        self.right, self.left, self.sx, self.sy, self.sc, self.arrived = sems

    def send(self, src, m, d, sem, device):
        remote(src, self.at(m, d), sem, self.arrived.at[m, d], device).start()

    def along_z(self, m, src=None):
        p = self.p
        src = self.at(m, p.d) if src is None else src

        @pl.when((m <= p.z) & (p.z < 3))
        def _():
            self.send(src, m, p.d, self.right.at[m], (p.d, p.z + 1))

        @pl.when((m >= p.z) & (p.z > 0))
        def _():
            self.send(src, m, p.d, self.left.at[m], (p.d, p.z - 1))

    def spread(self, m, src=None):
        p = self.p
        src = self.at(m, p.d) if src is None else src
        self.send(src, m, p.d, self.sx.at[m], p.x)
        self.send(src, m, p.d, self.sy.at[m], p.y)
        self.send(src, m, p.d, self.sc.at[m], p.core)

    def take(self, m, d):
        remote(self.at(m, d), self.at(m, d), self.sc.at[0], self.arrived.at[m, d], self.p.core).wait_recv()

    def z_in(self, m):
        self.take(m, self.p.d)
        self.along_z(m)

    def x_in(self, m):
        p = self.p
        self.take(m, p.dx)
        src = self.at(m, p.dx)

        @pl.when(lax.rem(m, 2) == 0)
        def _():
            self.send(src, m, p.dx, self.sy.at[4 + m], p.y)

        self.send(src, m, p.dx, self.sc.at[4 + m], p.core)

    def y_in(self, m):
        p = self.p
        self.take(m, p.dy)
        src = self.at(m, p.dy)

        @pl.when(lax.rem(m, 2) == 1)
        def _():
            self.send(src, m, p.dy, self.sx.at[4 + m], p.x)

        self.send(src, m, p.dy, self.sc.at[8 + m], p.core)

    def diag_in(self, m):
        p = self.p
        self.take(m, p.dxy)
        self.send(self.at(m, p.dxy), m, p.dxy, self.sc.at[12 + m], p.core)

    def core_in(self, m):
        for d in self.p.core_quads:
            self.take(m, d)

    def finish(self):
        p = self.p

        def sent(sem, device):
            remote(self.own, self.own, sem, self.arrived.at[0, 0], device).wait_send()

        for m in range(4):

            @pl.when((m <= p.z) & (p.z < 3))
            def _():
                sent(self.right.at[m], p.core)

            @pl.when((m >= p.z) & (p.z > 0))
            def _():
                sent(self.left.at[m], p.core)

            sent(self.sx.at[m], p.core)
            sent(self.sy.at[m], p.core)
            sent((self.sx if m % 2 else self.sy).at[4 + m], p.core)
            for q in range(4):
                sent(self.sc.at[4 * q + m], p.core)


def gather_sems():
    dma = pltpu.SemaphoreType.DMA
    return [dma((4,)), dma((4,)), dma((8,)), dma((8,)), dma((16,)), dma((4, 8))]


def lanes(shape, width):
    return lax.div(lax.broadcasted_iota(jnp.int32, shape, 1), width)


def turned(x, cosine, sine):
    first = lax.rem(lanes(x.shape, 32), 2) == 0
    width = x.shape[1]
    other = jnp.where(first, pltpu.roll(x, width - 32, 1), pltpu.roll(x, 32, 1))
    return x * cosine + other * sine


def wide(table):
    return jnp.concatenate([table, table], axis=1)


def dot(a, b):
    return lax.dot_general(a, b, (((1,), (0,)), ((), ())), preferred_element_type=F32)


def dot_nt(a, b):
    return lax.dot_general(a, b, (((1,), (1,)), ((), ())), preferred_element_type=F32)


def dot_tn(a, b):
    return lax.dot_general(a, b, (((0,), (0,)), ((), ())), preferred_element_type=F32)


def tile_scores(q_head, keys, tile, packed):
    n = (tile + 1) * CHUNK
    s = dot_nt(q_head, keys) * 0.125
    rows = lax.broadcasted_iota(jnp.int32, (CHUNK, n), 0) + tile * CHUNK
    cols = lax.broadcasted_iota(jnp.int32, (CHUNK, n), 1)
    allowed = cols <= rows
    if tile >= 2:
        allowed = allowed & ((packed != 2) | (cols >= 2 * CHUNK))
    return jnp.where(allowed, s, -1e30)


def forward_kernel(
    seq, tok, fv, wq, wk, wv, wo, wg, wu, wd, gains, cos_t, sin_t,
    f1, f2, qkv, o_head, lse, o_rows, a1, gain_out,
    stage, p2, *sems,
):
    p = Place()
    sems = list(sems)
    g1s, g2s = sems[:6], sems[6:12]
    s_qkv, r_qkv, s_o, r_o, s_local = sems[12:]
    z, d = p.z, p.d
    p.greet()

    f1[z, d, 0:128] = wq[...]
    f1[z, d, 128:256] = wk[...]
    f1[z, d, 256:384] = wv[...]
    f1[z, d, 384:400] = gains[...]
    g1 = Gather(p, lambda m, e: f1.at[m, e], f1.at[0, 0], g1s)
    g2 = Gather(p, lambda m, e: f2.at[m, e], p2, g2s)
    g1.along_z(z)
    g1.spread(z)
    p2[...] = jnp.zeros_like(p2)
    p2[:, 0:256] = wo[...]
    p2[:, 256:960] = wg[...]
    p2[:, 1024:1728] = wu[...]
    p2[:, 1792:2496] = wd[...]
    own_copy = pltpu.make_async_copy(p2, f2.at[z, d], s_local)
    own_copy.start()

    def arrive(g):
        def visit(m):
            g.z_in(m)
            g.spread(m)
        return visit

    def side(g):
        def visit(m):
            g.x_in(m)
            g.y_in(m)
        return visit

    p.hop(1, arrive(g1))
    side(g1)(z)
    p.hop(2, arrive(g1))
    p.hop(1, side(g1))
    g1.diag_in(z)
    p.hop(3, arrive(g1))
    g2.along_z(z, p2)
    p.hop(2, side(g1))
    p.hop(1, g1.diag_in)
    g1.core_in(z)

    gain_row = jnp.concatenate([f1[z, e, 384:400, :].astype(F32)[0:8] for e in range(8)], axis=1)
    for e in range(8):
        gain_out[:, e * 128 : (e + 1) * 128] = gain_row[:, e * 256 + 128 : e * 256 + 256]

    def norm_body(b, carry):
        x = tok[b].astype(F32)
        factor = lax.rsqrt(jnp.mean(x * x, axis=1, keepdims=True) + EPSILON)
        for e in range(8):
            cols = slice(e * 128, (e + 1) * 128)
            a1[pl.ds(pl.multiple_of(b * CHUNK, CHUNK), CHUNK), cols] = (
                x[:, cols] * factor * gain_row[0:1, e * 256 : e * 256 + 128]
            ).astype(BF)
        return carry

    lax.fori_loop(0, 3, norm_body, 0)

    p.hop(3, side(g1))
    p.hop(2, g1.diag_in)
    p.hop(1, g1.core_in)
    p.hop(3, g1.diag_in)
    p.hop(2, g1.core_in)
    p.hop(3, g1.core_in)
    g2.spread(z, p2)

    def project(b):
        pos_full = pl.ds(pl.multiple_of(z * CHUNK, CHUNK), CHUNK)
        low = jnp.where(z >= 2, z - 2, z)
        pos_half = pl.ds(pl.multiple_of(low * CHUNK, CHUNK), CHUNK)
        second = seq[b] == 2
        cosine = wide(jnp.where(second, cos_t[pos_half, :], cos_t[pos_full, :]))
        sine = wide(jnp.where(second, sin_t[pos_half, :], sin_t[pos_full, :]))
        rows = a1[b * CHUNK : (b + 1) * CHUNK, :]

        def one(step, carry):
            m = lax.rem(z + step, 4)
            w = lambda i: f1[m, :, i * 128 : (i + 1) * 128, :].reshape(1024, CHUNK)
            stage[b, m, 0] = turned(dot(rows, w(0)), cosine, sine).astype(BF)
            stage[b, m, 1] = turned(dot(rows, w(1)), cosine, sine).astype(BF)
            first = fv[b, :, pl.ds(pl.multiple_of(m * CHUNK, CHUNK), CHUNK)].astype(F32)
            stage[b, m, 2] = (0.5 * (dot(rows, w(2)) + first)).astype(BF)
            return carry

        lax.fori_loop(0, 4, one, 0)
        for i in range(3):
            qkv[b, i, pl.ds(pl.multiple_of(z * CHUNK, CHUNK), CHUNK), :] = stage[b, z, i]

    def qkv_copy(b, step):
        m = p.peer(step)
        dst = qkv.at[b, :, pl.ds(pl.multiple_of(z * CHUNK, CHUNK), CHUNK), :]
        return remote(stage.at[b, m], dst, s_qkv.at[b, step - 1], r_qkv.at[b, z], (d, m))

    def send_qkv(b):
        for step in (1, 2, 3):
            qkv_copy(b, step).start()

    def sent_qkv(b):
        for step in (1, 2, 3):
            qkv_copy(b, step).wait_send()

    def take_qkv(b):
        for step in (1, 2, 3):
            m = p.peer(step)
            dst = qkv.at[b, :, pl.ds(pl.multiple_of(m * CHUNK, CHUNK), CHUNK), :]
            remote(stage.at[b, m], dst, s_qkv.at[b, 0], r_qkv.at[b, m], (d, m)).wait_recv()

    def o_copy(b, i):
        rows = slice(i * CHUNK, (i + 1) * CHUNK)
        return remote(o_head.at[b, rows, :], o_rows.at[b, z], s_o.at[b, i], r_o.at[b, z], (d, i))

    def attend(b, i):
        n = (i + 1) * CHUNK
        rows = slice(i * CHUNK, n)
        packed = seq[b]
        q = qkv[b, 0, rows, :]
        keys = qkv[b, 1, 0:n, :]
        values = qkv[b, 2, 0:n, :]
        head_of = lanes((CHUNK, CHUNK), 64)
        lane = lax.broadcasted_iota(jnp.int32, (CHUNK, 128), 1)

        def head(h, carry):
            out, stats = carry
            s = tile_scores(jnp.where(head_of == h, q, jnp.zeros_like(q)), keys, i, packed)
            top = jnp.max(s, axis=1, keepdims=True)
            e = jnp.exp(s - top)
            total = jnp.sum(e, axis=1, keepdims=True)
            part = dot(e.astype(BF), values) * (1.0 / total)
            return (
                jnp.where(head_of == h, part, out),
                jnp.where(lane == h, top + jnp.log(total), stats),
            )

        out, stats = lax.fori_loop(
            0, 4, head, (jnp.zeros((CHUNK, CHUNK), F32), jnp.zeros((CHUNK, 128), F32))
        )
        o_head[b, rows, :] = out.astype(BF)
        lse[b, rows, :] = stats

        @pl.when(z == i)
        def _():
            o_rows[b, z] = out.astype(BF)

        @pl.when(z != i)
        def _():
            o_copy(b, i).start()

    for b in range(3):
        project(b)
        if b == 0:
            send_qkv(0)
    p.hop(1, g2.z_in)
    sent_qkv(0)
    send_qkv(1)
    p.hop(2, g2.z_in)
    p.hop(3, g2.z_in)
    p.hop(1, g2.spread)
    side(g2)(z)
    p.hop(2, g2.spread)
    take_qkv(0)
    attend(0, 0)
    attend(0, 1)
    p.hop(1, side(g2))
    sent_qkv(1)
    send_qkv(2)
    attend(0, 2)
    attend(0, 3)
    p.hop(3, g2.spread)
    p.hop(2, side(g2))
    take_qkv(1)
    attend(1, 0)
    attend(1, 1)
    g2.diag_in(z)
    p.hop(1, g2.diag_in)
    attend(1, 2)
    attend(1, 3)
    p.hop(3, side(g2))
    p.hop(2, g2.diag_in)
    take_qkv(2)
    attend(2, 0)
    attend(2, 1)
    p.hop(3, g2.diag_in)
    attend(2, 2)
    attend(2, 3)
    sent_qkv(2)
    for m in range(4):
        g2.core_in(m)
    for b in range(3):
        for step in (1, 2, 3):
            m = p.peer(step)
            remote(o_rows.at[b, m], o_rows.at[b, m], s_o.at[b, 0], r_o.at[b, m], (d, m)).wait_recv()
        for i in range(4):

            @pl.when(z != i)
            def _():
                o_copy(b, i).wait_send()

    g1.finish()
    g2.finish()
    own_copy.wait()


def run_forward(seq, tok, fv, wq, wk, wv, wo, wg, wu, wd, gains, cos_t, sin_t):
    vmem = pl.BlockSpec(memory_space=pltpu.VMEM)
    hbm = pl.BlockSpec(memory_space=pl.ANY)
    dma = pltpu.SemaphoreType.DMA
    shape = jax.ShapeDtypeStruct
    return pl.pallas_call(
        forward_kernel,
        out_shape=(
            shape((4, 8, QROWS, CHUNK), BF),
            shape((4, 8, 128, PADW), BF),
            shape((3, 3, 1024, CHUNK), BF),
            shape((3, 1024, CHUNK), BF),
            shape((3, 1024, 128), F32),
            shape((3, 4, CHUNK, CHUNK), BF),
            shape((768, 1024), BF),
            shape((8, 1024), F32),
        ),
        in_specs=[pl.BlockSpec(memory_space=pltpu.SMEM)] + [vmem] * 12,
        out_specs=(vmem, hbm, vmem, vmem, vmem, vmem, vmem, vmem),
        scratch_shapes=[
            pltpu.VMEM((3, 4, 3, CHUNK, CHUNK), BF),
            pltpu.VMEM((128, PADW), BF),
        ]
        + gather_sems()
        + gather_sems()
        + [dma((3, 3)), dma((3, 4)), dma((3, 4)), dma((3, 4)), dma],
        compiler_params=pltpu.CompilerParams(
            collective_id=1, has_side_effects=True, vmem_limit_bytes=60 * 2**20
        ),
        cost_estimate=pl.CostEstimate(flops=2 * 10**10, bytes_accessed=6 * 10**7, transcendentals=8 * 10**6),
        name="gather_attend",
    )(seq, tok, fv, wq, wk, wv, wo, wg, wu, wd, gains, cos_t, sin_t)


def backward_kernel(
    seq, do_rows, qkv, o_head, lse, cos_t, sin_t,
    d_rows,
    do_head, dk, dv, stage, *sems,
):
    p = Place()
    s_do, r_do, s_d, r_d = sems
    z, d = p.z, p.d
    p.greet()
    mine = pl.ds(pl.multiple_of(z * CHUNK, CHUNK), CHUNK)

    def do_copy(b, step):
        m = p.peer(step)
        return remote(
            do_rows.at[b, m], do_head.at[b, mine, :], s_do.at[b, step - 1], r_do.at[b, z], (d, m)
        )

    def send_do(b):
        for step in (1, 2, 3):
            do_copy(b, step).start()
        do_head[b, mine, :] = do_rows[b, z]

    def take_do(b):
        for step in (1, 2, 3):
            m = p.peer(step)
            dst = do_head.at[b, pl.ds(pl.multiple_of(m * CHUNK, CHUNK), CHUNK), :]
            remote(do_rows.at[b, m], dst, s_do.at[b, 0], r_do.at[b, m], (d, m)).wait_recv()

    def d_copy(b, i):
        return remote(stage.at[b, i], d_rows.at[b, z], s_d.at[b, i], r_d.at[b, z], (d, i))

    def back(b, i):
        n = (i + 1) * CHUNK
        rows = slice(i * CHUNK, n)
        packed = seq[b]
        head_of = lanes((CHUNK, CHUNK), 64)
        lane = lax.broadcasted_iota(jnp.int32, (CHUNK, 128), 1)
        q = qkv[b, 0, rows, :]
        keys = qkv[b, 1, 0:n, :]
        values = qkv[b, 2, 0:n, :]
        grad = do_head[b, rows, :]
        spread = grad.astype(F32) * o_head[b, rows, :].astype(F32)
        stats = lse[b, rows, :]

        def head(h, dq):
            here = head_of == h
            q_h = jnp.where(here, q, jnp.zeros_like(q))
            g_h = jnp.where(here, grad, jnp.zeros_like(grad))
            delta = jnp.sum(jnp.where(here, spread, 0.0), axis=1, keepdims=True)
            level = jnp.sum(jnp.where(lane == h, stats, 0.0), axis=1, keepdims=True)
            prob = jnp.exp(tile_scores(q_h, keys, i, packed) - level)
            dp = dot_nt(g_h, values)
            ds = (prob * (dp - delta)).astype(BF)
            dv_part = dot_tn(prob.astype(BF), g_h)
            dk_part = dot_tn(ds, q_h)
            dv[0:n, :] += dv_part
            dk[0:n, :] += dk_part
            return jnp.where(here, dot(ds, keys), dq)

        dq = lax.fori_loop(0, 4, head, jnp.zeros((CHUNK, CHUNK), F32))
        cosine, sine = cos_t[rows, :], sin_t[rows, :]
        if i >= 2:
            early = slice((i - 2) * CHUNK, (i - 1) * CHUNK)
            cosine = jnp.where(packed == 2, cos_t[early, :], cosine)
            sine = jnp.where(packed == 2, sin_t[early, :], sine)
        cosine, sine = wide(cosine), -wide(sine)
        stage[b, i, :, 0:256] = turned(dq * 0.125, cosine, sine).astype(BF)
        stage[b, i, :, 256:512] = turned(dk[rows, :] * 0.125, cosine, sine).astype(BF)
        stage[b, i, :, 512:768] = dv[rows, :].astype(BF)

        @pl.when(z == i)
        def _():
            d_rows[b, z] = stage[b, i]

        @pl.when(z != i)
        def _():
            d_copy(b, i).start()

    for b in range(3):
        send_do(b)
    for b in range(3):
        take_do(b)
        dk[...] = jnp.zeros_like(dk)
        dv[...] = jnp.zeros_like(dv)
        for i in (3, 2, 1, 0):
            back(b, i)
    for b in range(3):
        for step in (1, 2, 3):
            do_copy(b, step).wait_send()
            m = p.peer(step)
            remote(d_rows.at[b, m], d_rows.at[b, m], s_d.at[b, 0], r_d.at[b, m], (d, m)).wait_recv()
        for i in range(4):

            @pl.when(z != i)
            def _():
                d_copy(b, i).wait_send()


def run_backward(seq, do_rows, qkv, o_head, lse, cos_t, sin_t):
    vmem = pl.BlockSpec(memory_space=pltpu.VMEM)
    dma = pltpu.SemaphoreType.DMA
    return pl.pallas_call(
        backward_kernel,
        out_shape=jax.ShapeDtypeStruct((3, 4, CHUNK, 768), BF),
        in_specs=[pl.BlockSpec(memory_space=pltpu.SMEM)] + [vmem] * 6,
        out_specs=vmem,
        scratch_shapes=[
            pltpu.VMEM((3, 1024, CHUNK), BF),
            pltpu.VMEM((1024, CHUNK), F32),
            pltpu.VMEM((1024, CHUNK), F32),
            pltpu.VMEM((3, 4, CHUNK, 768), BF),
            dma((3, 3)),
            dma((3, 4)),
            dma((3, 4)),
            dma((3, 4)),
        ],
        compiler_params=pltpu.CompilerParams(
            collective_id=2, has_side_effects=True, vmem_limit_bytes=60 * 2**20
        ),
        cost_estimate=pl.CostEstimate(flops=3 * 10**10, bytes_accessed=2 * 10**7, transcendentals=8 * 10**6),
        name="attend_back",
    )(seq, do_rows, qkv, o_head, lse, cos_t, sin_t)


ORDER = (3, 0, 1, 2)


class Scatter:
    def __init__(self, place, part, width, bufs, sems, out):
        self.p, self.part, self.width, self.out = place, part, width, out
        self.own, self.other, self.diag_buf, self.bx, self.by, self.br, self.bl = bufs
        (self.l_own, self.s_core, self.r_core, self.s_diag, self.r_diag,
         self.s_x, self.r_x, self.s_y, self.r_y, self.s_r, self.r_r, self.s_l, self.r_l) = sems

    def core_copy(self, m, q):
        p = self.p
        return remote(
            self.part(m, p.core_quads[q]), self.other.at[m, q],
            self.s_core.at[m, q], self.r_core.at[m, q], p.core,
        )

    def own_copy(self, m, q):
        return pltpu.make_async_copy(
            self.part(m, self.p.quads[q]), self.own.at[m, q], self.l_own.at[m, q]
        )

    def begin(self, m):
        for q in (3, 1, 2, 0):
            self.core_copy(m, q).start()
            self.own_copy(m, q).start()

    def add(self, dst, *terms):
        step = 16

        def rows(r, carry):
            at = pl.ds(pl.multiple_of(r * step, step), step)
            total = dst[at, :].astype(F32)
            for t in terms:
                total = total + t[at, :].astype(F32)
            dst[at, :] = total.astype(dst.dtype)
            return carry

        lax.fori_loop(0, 128 // step, rows, 0)

    def joined(self, m, q, *more):
        self.own_copy(m, q).wait()
        self.core_copy(m, q).wait_recv()
        self.add(self.own.at[m, q], self.other.at[m, q], *more)

    def diag_copy(self, m):
        to = self.p.x if m % 2 == 0 else self.p.y
        return remote(self.own.at[m, 3], self.diag_buf.at[m], self.s_diag.at[m], self.r_diag.at[m], to)

    def x_copy(self, m):
        return remote(self.own.at[m, 1], self.bx.at[m], self.s_x.at[m], self.r_x.at[m], self.p.x)

    def y_copy(self, m):
        return remote(self.own.at[m, 2], self.by.at[m], self.s_y.at[m], self.r_y.at[m], self.p.y)

    def r_copy(self, m):
        return remote(
            self.own.at[m, 0], self.br.at[m], self.s_r.at[m], self.r_r.at[m], (self.p.d, self.p.z + 1)
        )

    def l_copy(self, m):
        return remote(
            self.own.at[m, 0], self.bl.at[m], self.s_l.at[m], self.r_l.at[m], (self.p.d, self.p.z - 1)
        )

    def diag(self, m):
        self.joined(m, 3)
        self.diag_copy(m).start()

    def direct(self, m):
        self.joined(m, 1 if m % 2 == 0 else 2)
        (self.x_copy if m % 2 == 0 else self.y_copy)(m).start()

    def relay(self, m):
        self.diag_copy(m).wait_recv()
        self.joined(m, 2 if m % 2 == 0 else 1, self.diag_buf.at[m])
        (self.y_copy if m % 2 == 0 else self.x_copy)(m).start()

    def quad_sum(self, m):
        self.own_copy(m, 0).wait()
        self.core_copy(m, 0).wait_recv()
        self.x_copy(m).wait_recv()
        self.y_copy(m).wait_recv()
        self.add(self.own.at[m, 0], self.other.at[m, 0], self.bx.at[m], self.by.at[m])

    def along_z(self, m):
        z = self.p.z

        if m > 0:
            @pl.when(z < m)
            def _():
                @pl.when(z > 0)
                def _():
                    self.r_copy(m).wait_recv()
                    self.add(self.own.at[m, 0], self.br.at[m])

                self.r_copy(m).start()

        if m < 3:
            @pl.when(z > m)
            def _():
                @pl.when(z < 3)
                def _():
                    self.l_copy(m).wait_recv()
                    self.add(self.own.at[m, 0], self.bl.at[m])

                self.l_copy(m).start()

    def last(self):
        z = self.p.z
        step = 16

        for m in range(4):
            @pl.when(z == m)
            def _():
                terms = [self.own.at[m, 0]]
                if m > 0:
                    self.r_copy(m).wait_recv()
                    terms.append(self.br.at[m])
                if m < 3:
                    self.l_copy(m).wait_recv()
                    terms.append(self.bl.at[m])

                def rows(r, carry):
                    at = pl.ds(pl.multiple_of(r * step, step), step)
                    total = terms[0][at, :].astype(F32)
                    for t in terms[1:]:
                        total = total + t[at, :].astype(F32)
                    self.out[at, :] = total
                    return carry

                lax.fori_loop(0, 128 // step, rows, 0)

    def finish(self):
        z = self.p.z
        for m in range(4):
            for q in range(4):
                self.core_copy(m, q).wait_send()
            self.diag_copy(m).wait_send()
            self.x_copy(m).wait_send()
            self.y_copy(m).wait_send()
            if m > 0:
                @pl.when(z < m)
                def _():
                    self.r_copy(m).wait_send()
            if m < 3:
                @pl.when(z > m)
                def _():
                    self.l_copy(m).wait_send()

    def steps(self):
        a, b, c, e = ORDER
        return [
            lambda: self.begin(a), lambda: self.begin(b), lambda: self.diag(a), lambda: self.diag(b),
            lambda: self.begin(c), lambda: self.direct(a), lambda: self.direct(b),
            lambda: self.begin(e), lambda: self.diag(c), lambda: self.diag(e),
            lambda: self.relay(a), lambda: self.relay(b), lambda: self.direct(c), lambda: self.direct(e),
            lambda: self.quad_sum(a), lambda: self.along_z(a), lambda: self.quad_sum(b), lambda: self.along_z(b),
            lambda: self.relay(c), lambda: self.relay(e),
            lambda: self.quad_sum(c), lambda: self.along_z(c), lambda: self.quad_sum(e), lambda: self.along_z(e),
            self.last,
        ]


def scatter_buffers(width):
    def buf(*lead):
        return pltpu.VMEM((*lead, 128, width), BF)

    return [buf(4, 4), buf(4, 4), buf(4), buf(4), buf(4), buf(4), buf(4)]


def scatter_sems():
    dma = pltpu.SemaphoreType.DMA
    return [dma((4, 4))] * 3 + [dma((4,))] * 10


def scatter_kernel(part1, part2, out1, out2, *rest):
    rest = list(rest)
    bufs1, bufs2, sems1, sems2 = rest[:7], rest[7:14], rest[14:27], rest[27:40]
    p = Place()
    p.greet()
    big = Scatter(p, lambda m, d: part2.at[m, d], PADW, bufs2, sems2, out2)
    small = Scatter(p, lambda m, d: part1.at[m, d], 768, bufs1, sems1, out1)
    for a, b in zip(big.steps(), small.steps()):
        a()
        b()
    big.finish()
    small.finish()


def run_scatter(part1, part2):
    vmem = pl.BlockSpec(memory_space=pltpu.VMEM)
    hbm = pl.BlockSpec(memory_space=pl.ANY)
    shape = jax.ShapeDtypeStruct
    return pl.pallas_call(
        scatter_kernel,
        out_shape=(shape((128, 768), F32), shape((128, PADW), F32)),
        in_specs=[hbm, hbm],
        out_specs=(vmem, vmem),
        scratch_shapes=scatter_buffers(768) + scatter_buffers(PADW) + scatter_sems() + scatter_sems(),
        compiler_params=pltpu.CompilerParams(
            collective_id=3, has_side_effects=True, vmem_limit_bytes=60 * 2**20
        ),
        cost_estimate=pl.CostEstimate(flops=10**7, bytes_accessed=5 * 10**7, transcendentals=0),
        name="sum_grads",
    )(part1, part2)


def fast_body(
    tokens, first_values, sequences, w_query, w_key, w_value, w_out, w_gate, w_up, w_down,
    gain_attn, gain_mlp, cotangent,
):
    seq = sequences[:, 0]
    gains = jnp.zeros((16, CHUNK), BF).at[0, :128].set(gain_attn).at[0, 128:].set(gain_mlp)
    cos_t, sin_t = rope_tables()
    f1, f2, qkv, o_head, lse, o_rows, a1, gain_out = run_forward(
        seq, tokens, first_values, w_query, w_key, w_value, w_out, w_gate, w_up, w_down, gains, cos_t, sin_t
    )
    gain_two = gain_out[0]
    dotf = lambda eq, a, b: jnp.einsum(eq, a, b, preferred_element_type=F32)
    wo = f2[:, :, :, 0:256].reshape(4, 1024, 256)
    wg = f2[:, :, :, 256:1024].reshape(4, 1024, HP)
    wu = f2[:, :, :, 1024:1792].reshape(4, 1024, HP)
    wd = f2[:, :, :, 1792:2560].reshape(4, 1024, HP)
    x = tokens.reshape(768, 1024).astype(F32)
    g16 = cotangent.reshape(768, 1024)
    o_cols = o_rows.transpose(1, 0, 2, 3).reshape(4, 768, 256)
    x2 = x + dotf("mrc,mdc->rd", o_cols, wo)
    r2 = lax.rsqrt(jnp.mean(x2 * x2, axis=-1, keepdims=True) + EPSILON)
    n2 = x2 * r2
    a2 = (n2 * gain_two[None, :]).astype(BF)
    gate = dotf("rd,mdc->mrc", a2, wg)
    up = dotf("rd,mdc->mrc", a2, wu)
    sg = jax.nn.sigmoid(gate)
    h = (gate * sg * up).astype(BF)
    layer_out = (x2 + dotf("mrc,mdc->rd", h, wd)).astype(BF).reshape(3, 256, 1024)
    dh = dotf("rd,mdc->mrc", g16, wd)
    dgate = (dh * up * sg * (1.0 + gate * (1.0 - sg))).astype(BF)
    dup = (dh * gate * sg).astype(BF)
    da2 = dotf("mrc,mdc->rd", dgate, wg) + dotf("mrc,mdc->rd", dup, wu)
    part_gain2 = jnp.sum(da2 * n2, axis=0)
    dn2 = da2 * gain_two[None, :]
    dx2 = g16.astype(F32) + r2 * (dn2 - n2 * jnp.mean(dn2 * n2, axis=-1, keepdims=True))
    dattn = dx2.astype(BF)
    do_rows = dotf("rd,mdc->mrc", dattn, wo).astype(BF).reshape(4, 3, 256, 256).transpose(1, 0, 2, 3)
    d_rows = run_backward(seq, do_rows, qkv, o_head, lse, cos_t, sin_t)
    gw2 = jnp.concatenate(
        [
            dotf("rd,mrc->mdc", dattn, o_cols).astype(BF),
            dotf("rd,mrc->mdc", a2, dgate).astype(BF),
            dotf("rd,mrc->mdc", a2, dup).astype(BF),
            dotf("rd,mrc->mdc", g16, h).astype(BF),
        ],
        axis=-1,
    ).reshape(4, 8, 128, PADW)
    dcols = d_rows.transpose(1, 0, 2, 3).reshape(4, 768, 768)
    scale = jnp.concatenate([jnp.ones((512,), F32), jnp.full((256,), 0.5, F32)])
    gw1 = (dotf("rd,mrc->mdc", a1, dcols) * scale).astype(BF).reshape(4, 8, 128, 768)
    w1 = f1[:, :, 0:384, :].reshape(4, 8, 3, 128, 256)
    dc = dcols.reshape(4, 768, 3, 256)
    da1 = (
        dotf("mrac,mdac->rd", dc[:, :, 0:2], w1[:, :, 0:2].transpose(0, 1, 3, 2, 4).reshape(4, 1024, 2, 256))
        + 0.5 * dotf("mrc,mdc->rd", dc[:, :, 2], w1[:, :, 2].reshape(4, 1024, 256))
    )
    r1 = lax.rsqrt(jnp.mean(x * x, axis=-1, keepdims=True) + EPSILON)
    n1 = x * r1
    gain_one = f1[0, :, 384, 0:128].reshape(1024).astype(F32)
    part_gain1 = jnp.sum(da1 * n1, axis=0)
    dn1 = da1 * gain_one[None, :]
    grad_tokens = dx2 + r1 * (dn1 - n1 * jnp.mean(dn1 * n1, axis=-1, keepdims=True))
    grad_first = 0.5 * d_rows[:, :, :, 512:768].transpose(0, 2, 1, 3).reshape(3, 256, 1024).astype(F32)
    s1, s2 = run_scatter(gw1, gw2)
    gain_sums = lax.psum(jnp.stack([part_gain1, part_gain2]), ("dp", "mp"))
    place = (lax.axis_index("dp") * 4 + lax.axis_index("mp")) * 32
    gain_mine = lax.dynamic_slice(gain_sums, (0, place), (2, 32))
    return (
        layer_out,
        grad_tokens.reshape(3, 256, 1024),
        grad_first,
        s1[:, 0:256],
        s1[:, 256:512],
        s1[:, 512:768],
        s2[:, 0:256],
        s2[:, 256:960],
        s2[:, 1024:1728],
        s2[:, 1792:2496],
        gain_mine[0],
        gain_mine[1],
    )


def is_small(mesh):
    return mesh.axis_names == ("dp", "mp") and tuple(mesh.devices.shape) == (8, 4)


def solution(mesh):
    return jax.shard_map(
        fast_body if is_small(mesh) else body,
        mesh=mesh,
        in_specs=(
            P(None, ("dp", "mp"), None),
            P(None, ("dp", "mp"), None),
            P(None, "dp"),
            P("dp", "mp"),
            P("dp", "mp"),
            P("dp", "mp"),
            P("dp", "mp"),
            P("dp", "mp"),
            P("dp", "mp"),
            P("dp", "mp"),
            P("dp"),
            P("dp"),
            P(None, ("dp", "mp"), None),
        ),
        out_specs=(
            P(None, ("dp", "mp"), None),
            P(None, ("dp", "mp"), None),
            P(None, ("dp", "mp"), None),
            P("dp", "mp"),
            P("dp", "mp"),
            P("dp", "mp"),
            P("dp", "mp"),
            P("dp", "mp"),
            P("dp", "mp"),
            P("dp", "mp"),
            P(("dp", "mp")),
            P(("dp", "mp")),
        ),
        check_vma=False,
    )
```

```python
import jax
import jax.numpy as jnp
import numpy as np
from jax import lax
from jax.experimental import pallas as pl
from jax.experimental.pallas import tpu as pltpu
from jax.sharding import PartitionSpec as P

HEAD_DIM = 64


EPSILON = 1e-06
THETA = 10000.0


def normalize(rows):
    factor = lax.rsqrt(jnp.mean(rows * rows, axis=-1, keepdims=True) + EPSILON)
    return (rows * factor, factor)


def norm_back(grad_normed, normed, factor):
    return factor * (grad_normed - normed * jnp.mean(grad_normed * normed, axis=-1, keepdims=True))


def rotary_tables(position, head_size):
    halfway = head_size // 2
    inverse = THETA ** (-2.0 * jnp.arange(halfway, dtype=jnp.float32) / head_size)
    angles = position.astype(jnp.float32)[:, None] * inverse[None, :]
    return (jnp.cos(angles), jnp.sin(angles))


def rotate(values, cosine, sine, direction):
    halfway = values.shape[-1] // 2
    former = values[..., :halfway]
    latter = values[..., halfway:]
    cos_rows = cosine[:, None, :]
    sin_rows = direction * sine[:, None, :]
    return jnp.concatenate(
        [former * cos_rows - latter * sin_rows, latter * cos_rows + former * sin_rows], axis=-1
    )


def layout(packed, length):
    index_rows = jnp.arange(length, dtype=jnp.int32)
    second = jnp.where((packed == 2) & (index_rows >= length // 2), 1, 0).astype(jnp.int32)
    return (second, index_rows - second * (length // 2))


def block_scores(query, key_rows, second, offset, block_rows, key_end, scale):
    raw = (
        jnp.einsum(
            "qhd,khd->hqk",
            query[offset : offset + block_rows],
            key_rows,
            preferred_element_type=jnp.float32,
        )
        * scale
    )
    row_ids = offset + jnp.arange(block_rows, dtype=jnp.int32)
    col_ids = jnp.arange(key_end, dtype=jnp.int32)
    allowed = (col_ids[None, :] <= row_ids[:, None]) & (
        second[offset : offset + block_rows][:, None] == second[None, :]
    )
    return jnp.where(allowed[None], raw, -1e30)


def whole_rows(part):
    return lax.all_gather(part, "mp", axis=0, tiled=True)


def summed_rows(term, local_rows):
    return lax.psum_scatter(
        term(jnp.int32(0), local_rows * lax.axis_size("mp")).astype(jnp.bfloat16),
        "mp",
        scatter_dimension=0,
        tiled=True,
    ).astype(jnp.float32)


def fetch(w_query, w_key, w_value, w_out, w_gate, w_up, w_down, gain_attn, gain_mlp):
    return (
        lax.all_gather(w_query, "dp", axis=0, tiled=True),
        lax.all_gather(w_key, "dp", axis=0, tiled=True),
        lax.all_gather(w_value, "dp", axis=0, tiled=True),
        lax.all_gather(w_out, "dp", axis=0, tiled=True),
        lax.all_gather(w_gate, "dp", axis=0, tiled=True),
        lax.all_gather(w_up, "dp", axis=0, tiled=True),
        lax.all_gather(w_down, "dp", axis=0, tiled=True),
        lax.all_gather(gain_attn, "dp", axis=0, tiled=True),
        lax.all_gather(gain_mlp, "dp", axis=0, tiled=True),
    )


def project_back(left, right):
    return jnp.einsum("rc,dc->rd", left, right, preferred_element_type=jnp.float32)


def outer_sum(left, right):
    return jnp.einsum("td,tc->dc", left, right, preferred_element_type=jnp.float32)


def body(
    tokens,
    first_values,
    sequences,
    w_query,
    w_key,
    w_value,
    w_out,
    w_gate,
    w_up,
    w_down,
    gain_attn,
    gain_mlp,
    cotangent,
):
    micro = tokens.shape[0]
    local_rows = tokens.shape[1]
    length = local_rows * lax.axis_size("mp")
    heads_here = w_query.shape[1] // HEAD_DIM
    block_rows = min(512, length)
    scale = HEAD_DIM ** (-0.5)
    saved = []
    outputs = []
    for batch in range(micro):
        full = fetch(w_query, w_key, w_value, w_out, w_gate, w_up, w_down, gain_attn, gain_mlp)
        q_full, k_full, v_full, o_full, gate_full, up_full, down_full, gain_one, gain_two = full
        gain_one = gain_one.astype(jnp.float32)
        gain_two = gain_two.astype(jnp.float32)
        x_rows = tokens[batch].astype(jnp.float32)
        normed_one, factor_one = normalize(x_rows)
        input_one = whole_rows((normed_one * gain_one[None, :]).astype(jnp.bfloat16))
        second, position = layout(sequences[batch, 0], length)
        cosine, sine = rotary_tables(position, HEAD_DIM)
        query = jnp.dot(input_one, q_full, preferred_element_type=jnp.float32).reshape(
            length, heads_here, HEAD_DIM
        )
        query = rotate(query, cosine, sine, 1.0).astype(jnp.bfloat16)
        key_rows = jnp.dot(input_one, k_full, preferred_element_type=jnp.float32).reshape(
            length, heads_here, HEAD_DIM
        )
        key_rows = rotate(key_rows, cosine, sine, 1.0).astype(jnp.bfloat16)
        first_here = lax.all_to_all(
            first_values[batch], "mp", split_axis=1, concat_axis=0, tiled=True
        )
        mixed = 0.5 * (
            jnp.dot(input_one, v_full, preferred_element_type=jnp.float32)
            + first_here.astype(jnp.float32)
        )
        mixed = mixed.astype(jnp.bfloat16).reshape(length, heads_here, HEAD_DIM)
        pieces = []
        logsums = []
        for offset in range(0, length, block_rows):
            key_end = length
            scores = block_scores(query, key_rows, second, offset, block_rows, key_end, scale)
            highest = jnp.max(scores, axis=-1, keepdims=True)
            powers = jnp.exp(scores - highest)
            denominator = jnp.sum(powers, axis=-1, keepdims=True)
            probs_low = (powers / denominator).astype(jnp.bfloat16)
            logsums.append(highest + jnp.log(denominator))
            pieces.append(
                jnp.einsum("hqk,khd->qhd", probs_low, mixed, preferred_element_type=jnp.float32)
            )
        attended = (
            jnp.concatenate(pieces, axis=0)
            .reshape(length, heads_here * HEAD_DIM)
            .astype(jnp.bfloat16)
        )

        def attn_term(offset, amount):
            return project_back(attended, o_full)

        mid_rows = x_rows + summed_rows(attn_term, local_rows)
        normed_two, factor_two = normalize(mid_rows)
        input_two = whole_rows((normed_two * gain_two[None, :]).astype(jnp.bfloat16))
        gate = jnp.dot(input_two, gate_full, preferred_element_type=jnp.float32)
        upward = jnp.dot(input_two, up_full, preferred_element_type=jnp.float32)
        sigma = jax.nn.sigmoid(gate)
        hidden = (gate * sigma * upward).astype(jnp.bfloat16)

        def mlp_term(offset, amount):
            return project_back(hidden, down_full)

        mlp_rows = summed_rows(mlp_term, local_rows)
        outputs.append((mid_rows + mlp_rows).astype(jnp.bfloat16))
        saved.append(
            (
                normed_one,
                factor_one,
                input_one,
                second,
                cosine,
                sine,
                query,
                key_rows,
                mixed,
                logsums,
                attended,
                normed_two,
                factor_two,
                input_two,
                gate,
                sigma,
                upward,
                hidden,
            )
        )
    grad_sum = None
    gain_grad_one = jnp.zeros((tokens.shape[2],), jnp.float32)
    gain_grad_two = jnp.zeros((tokens.shape[2],), jnp.float32)
    grad_tokens = []
    grad_first = []
    for batch in range(micro):
        (
            normed_one,
            factor_one,
            input_one,
            second,
            cosine,
            sine,
            query,
            key_rows,
            mixed,
            logsums,
            attended,
            normed_two,
            factor_two,
            input_two,
            gate,
            sigma,
            upward,
            hidden,
        ) = saved[batch]
        full = fetch(w_query, w_key, w_value, w_out, w_gate, w_up, w_down, gain_attn, gain_mlp)
        q_full, k_full, v_full, o_full, gate_full, up_full, down_full, gain_one, gain_two = full
        gain_one = gain_one.astype(jnp.float32)
        gain_two = gain_two.astype(jnp.float32)
        grad_rows = cotangent[batch]
        grad_full = whole_rows(grad_rows)
        grad_down = outer_sum(grad_full, hidden)
        grad_hidden = jnp.dot(grad_full, down_full, preferred_element_type=jnp.float32)
        grad_gate = (grad_hidden * upward * sigma * (1.0 + gate * (1.0 - sigma))).astype(
            jnp.bfloat16
        )
        grad_up = (grad_hidden * gate * sigma).astype(jnp.bfloat16)
        grad_gate_w = outer_sum(input_two, grad_gate)
        grad_up_w = outer_sum(input_two, grad_up)

        def mlp_back(offset, amount):
            return project_back(grad_gate, gate_full) + project_back(grad_up, up_full)

        grad_input_two = summed_rows(mlp_back, local_rows)
        gain_grad_two = gain_grad_two + jnp.sum(grad_input_two * normed_two, axis=0)
        grad_mid = grad_rows.astype(jnp.float32) + norm_back(
            grad_input_two * gain_two[None, :], normed_two, factor_two
        )
        grad_attn = whole_rows(grad_mid.astype(jnp.bfloat16))
        grad_out_w = outer_sum(grad_attn, attended)
        grad_attended = jnp.dot(grad_attn, o_full, preferred_element_type=jnp.float32)
        grad_attended = grad_attended.astype(jnp.bfloat16).reshape(length, heads_here, HEAD_DIM)
        grad_mixed = jnp.zeros((length, heads_here, HEAD_DIM), jnp.float32)
        grad_key = jnp.zeros((length, heads_here, HEAD_DIM), jnp.float32)
        query_parts = []
        for turn, offset in enumerate(range(0, length, block_rows)):
            key_end = length
            scores = block_scores(query, key_rows, second, offset, block_rows, key_end, scale)
            probs = jnp.exp(scores - logsums[turn])
            grad_block = grad_attended[offset : offset + block_rows]
            grad_probs = jnp.einsum(
                "qhd,khd->hqk", grad_block, mixed, preferred_element_type=jnp.float32
            )
            grad_mixed = grad_mixed.at[:key_end].add(
                jnp.einsum(
                    "hqk,qhd->khd",
                    probs.astype(jnp.bfloat16),
                    grad_block,
                    preferred_element_type=jnp.float32,
                )
            )
            grad_scores = probs * (grad_probs - jnp.sum(probs * grad_probs, axis=-1, keepdims=True))
            grad_scores = grad_scores.astype(jnp.bfloat16)
            query_parts.append(
                jnp.einsum(
                    "hqk,khd->qhd", grad_scores, key_rows, preferred_element_type=jnp.float32
                )
                * scale
            )
            grad_key = grad_key.at[:key_end].add(
                jnp.einsum(
                    "hqk,qhd->khd",
                    grad_scores,
                    query[offset : offset + block_rows],
                    preferred_element_type=jnp.float32,
                )
                * scale
            )
        grad_mixed_low = grad_mixed.reshape(length, heads_here * HEAD_DIM).astype(jnp.bfloat16)
        grad_value = (0.5 * grad_mixed_low.astype(jnp.float32)).astype(jnp.bfloat16)
        grad_query = rotate(jnp.concatenate(query_parts, axis=0), cosine, sine, -1.0)
        grad_query = grad_query.reshape(length, heads_here * HEAD_DIM).astype(jnp.bfloat16)
        grad_key_low = (
            rotate(grad_key, cosine, sine, -1.0)
            .reshape(length, heads_here * HEAD_DIM)
            .astype(jnp.bfloat16)
        )
        grad_query_w = outer_sum(input_one, grad_query)
        grad_key_w = outer_sum(input_one, grad_key_low)
        grad_value_w = outer_sum(input_one, grad_value)

        def attn_back(offset, amount):
            return (
                project_back(grad_query, q_full)
                + project_back(grad_key_low, k_full)
                + project_back(grad_value, v_full)
            )

        grad_input_one = summed_rows(attn_back, local_rows)
        gain_grad_one = gain_grad_one + jnp.sum(grad_input_one * normed_one, axis=0)
        grad_tokens.append(
            grad_mid + norm_back(grad_input_one * gain_one[None, :], normed_one, factor_one)
        )
        returned = lax.all_to_all(grad_mixed_low, "mp", split_axis=0, concat_axis=1, tiled=True)
        grad_first.append(0.5 * returned.astype(jnp.float32))
        shared = (
            lax.psum_scatter(
                grad_query_w.astype(jnp.bfloat16), "dp", scatter_dimension=0, tiled=True
            ).astype(jnp.float32),
            lax.psum_scatter(
                grad_key_w.astype(jnp.bfloat16), "dp", scatter_dimension=0, tiled=True
            ).astype(jnp.float32),
            lax.psum_scatter(
                grad_value_w.astype(jnp.bfloat16), "dp", scatter_dimension=0, tiled=True
            ).astype(jnp.float32),
            lax.psum_scatter(
                grad_out_w.astype(jnp.bfloat16), "dp", scatter_dimension=0, tiled=True
            ).astype(jnp.float32),
            lax.psum_scatter(
                grad_gate_w.astype(jnp.bfloat16), "dp", scatter_dimension=0, tiled=True
            ).astype(jnp.float32),
            lax.psum_scatter(
                grad_up_w.astype(jnp.bfloat16), "dp", scatter_dimension=0, tiled=True
            ).astype(jnp.float32),
            lax.psum_scatter(
                grad_down.astype(jnp.bfloat16), "dp", scatter_dimension=0, tiled=True
            ).astype(jnp.float32),
        )
        grad_sum = shared if grad_sum is None else jax.tree.map(jnp.add, grad_sum, shared)
    gain_parts = (
        lax.psum_scatter(gain_grad_one, ("dp", "mp"), scatter_dimension=0, tiled=True),
        lax.psum_scatter(gain_grad_two, ("dp", "mp"), scatter_dimension=0, tiled=True),
    )
    return (
        jnp.stack(outputs),
        jnp.stack(grad_tokens),
        jnp.stack(grad_first),
        grad_sum[0],
        grad_sum[1],
        grad_sum[2],
        grad_sum[3],
        grad_sum[4],
        grad_sum[5],
        grad_sum[6],
        gain_parts[0],
        gain_parts[1],
    )


def rope_tables():
    half = HEAD_DIM // 2
    inverse = (THETA ** (-2.0 * np.arange(half) / HEAD_DIM)).astype(np.float32)
    angles = np.arange(1024, dtype=np.float32)[:, None] * inverse[None, :]
    cosine, sine = np.cos(angles), np.sin(angles)
    return (
        jnp.asarray(np.concatenate([cosine] * 4, axis=1), jnp.float32),
        jnp.asarray(np.concatenate([-sine, sine, -sine, sine], axis=1), jnp.float32),
    )


BF = jnp.bfloat16
F32 = jnp.float32
MESH = pl.DeviceIdType.MESH
CHUNK = 256
FFC = 704
PIECE = 3 * FFC + 256
QROWS = 400


def remote(src, dst, send, recv, device):
    return pltpu.make_async_remote_copy(
        src_ref=src, dst_ref=dst, send_sem=send, recv_sem=recv, device_id=device, device_id_type=MESH
    )


class Place:
    def __init__(self):
        self.d = d = lax.axis_index("dp")
        self.z = z = lax.axis_index("mp")
        core = lax.rem(d, 2)
        along_x = lax.rem(lax.div(d, 2), 2)
        along_y = lax.div(d, 4)
        self.dc = d + 1 - 2 * core
        self.dx = d + 2 - 4 * along_x
        self.dy = d + 4 - 8 * along_y
        self.dxy = self.dx + 4 - 8 * along_y
        self.core = (self.dc, z)
        self.x = (self.dx, z)
        self.y = (self.dy, z)
        self.quads = (d, self.dx, self.dy, self.dxy)
        self.core_quads = tuple(q + 1 - 2 * core for q in self.quads)

    def peer(self, step):
        return lax.rem(self.z + step, 4)

    def greet(self):
        barrier = pltpu.get_barrier_semaphore()
        others = [self.core, self.x, self.y] + [(self.d, self.peer(s)) for s in (1, 2, 3)]
        for other in others:
            pl.semaphore_signal(barrier, inc=1, device_id=other, device_id_type=MESH)
        pl.semaphore_wait(barrier, len(others))

    def hop(self, step, visit):
        for sign in (1, -1):
            m = self.z + sign * step

            @pl.when((m >= 0) & (m <= 3))
            def _():
                visit(m)


class Gather:
    def __init__(self, place, at, own, sems):
        self.p, self.at, self.own = place, at, own
        self.right, self.left, self.sx, self.sy, self.sc, self.arrived = sems

    def send(self, src, m, d, sem, device):
        remote(src, self.at(m, d), sem, self.arrived.at[m, d], device).start()

    def along_z(self, m, src=None):
        p = self.p
        src = self.at(m, p.d) if src is None else src

        @pl.when((m <= p.z) & (p.z < 3))
        def _():
            self.send(src, m, p.d, self.right.at[m], (p.d, p.z + 1))

        @pl.when((m >= p.z) & (p.z > 0))
        def _():
            self.send(src, m, p.d, self.left.at[m], (p.d, p.z - 1))

    def spread(self, m, src=None):
        p = self.p
        src = self.at(m, p.d) if src is None else src
        self.send(src, m, p.d, self.sx.at[m], p.x)
        self.send(src, m, p.d, self.sy.at[m], p.y)
        self.send(src, m, p.d, self.sc.at[m], p.core)

    def take(self, m, d):
        remote(self.at(m, d), self.at(m, d), self.sc.at[0], self.arrived.at[m, d], self.p.core).wait_recv()

    def z_in(self, m):
        self.take(m, self.p.d)
        self.along_z(m)

    def x_in(self, m):
        p = self.p
        self.take(m, p.dx)
        src = self.at(m, p.dx)

        @pl.when(lax.rem(m, 2) == 0)
        def _():
            self.send(src, m, p.dx, self.sy.at[4 + m], p.y)

        self.send(src, m, p.dx, self.sc.at[4 + m], p.core)

    def y_in(self, m):
        p = self.p
        self.take(m, p.dy)
        src = self.at(m, p.dy)

        @pl.when(lax.rem(m, 2) == 1)
        def _():
            self.send(src, m, p.dy, self.sx.at[4 + m], p.x)

        self.send(src, m, p.dy, self.sc.at[8 + m], p.core)

    def diag_in(self, m):
        p = self.p
        self.take(m, p.dxy)
        self.send(self.at(m, p.dxy), m, p.dxy, self.sc.at[12 + m], p.core)

    def core_in(self, m):
        for d in self.p.core_quads:
            self.take(m, d)

    def finish(self):
        p = self.p

        def sent(sem, device):
            remote(self.own, self.own, sem, self.arrived.at[0, 0], device).wait_send()

        for m in range(4):

            @pl.when((m <= p.z) & (p.z < 3))
            def _():
                sent(self.right.at[m], p.core)

            @pl.when((m >= p.z) & (p.z > 0))
            def _():
                sent(self.left.at[m], p.core)

            sent(self.sx.at[m], p.core)
            sent(self.sy.at[m], p.core)
            sent((self.sx if m % 2 else self.sy).at[4 + m], p.core)
            for q in range(4):
                sent(self.sc.at[4 * q + m], p.core)


def gather_sems():
    dma = pltpu.SemaphoreType.DMA
    return [dma((4,)), dma((4,)), dma((8,)), dma((8,)), dma((16,)), dma((4, 8))]


def lanes(shape, width):
    return lax.div(lax.broadcasted_iota(jnp.int32, shape, 1), width)


def turned(x, cosine, sine):
    first = lax.rem(lanes(x.shape, 32), 2) == 0
    width = x.shape[1]
    other = jnp.where(first, pltpu.roll(x, width - 32, 1), pltpu.roll(x, 32, 1))
    return x * cosine + other * sine


def wide(table):
    return jnp.concatenate([table, table], axis=1)


def dot(a, b):
    return lax.dot_general(a, b, (((1,), (0,)), ((), ())), preferred_element_type=F32)


def dot_nt(a, b):
    return lax.dot_general(a, b, (((1,), (1,)), ((), ())), preferred_element_type=F32)


def dot_tn(a, b):
    return lax.dot_general(a, b, (((0,), (0,)), ((), ())), preferred_element_type=F32)


def tile_scores(q_head, keys, tile, packed):
    n = (tile + 1) * CHUNK
    s = dot_nt(q_head, keys) * 0.125
    rows = lax.broadcasted_iota(jnp.int32, (CHUNK, n), 0) + tile * CHUNK
    cols = lax.broadcasted_iota(jnp.int32, (CHUNK, n), 1)
    allowed = cols <= rows
    if tile >= 2:
        allowed = allowed & ((packed != 2) | (cols >= 2 * CHUNK))
    return jnp.where(allowed, s, -1e30)


def forward_kernel(
    seq, tok, fv, wq, wk, wv, wo, wg_t, wu_t, wd_t, gain_attn, gain_mlp, cos_t, sin_t,
    f1, f2, qkv, o_head, lse, o_rows, a1_t, gain_out,
    a1, stage, p2, *sems,
):
    p = Place()
    sems = list(sems)
    g1s, g2s = sems[:6], sems[6:12]
    s_qkv, r_qkv, s_o, r_o, s_local = sems[12:]
    z, d = p.z, p.d
    p.greet()

    f1[z, d, 0:128] = wq[...]
    f1[z, d, 128:256] = wk[...]
    f1[z, d, 256:384] = wv[...]
    f1[z, d, 384:400, 0:128] = jnp.broadcast_to(gain_attn[...], (16, 128))
    f1[z, d, 384:400, 128:256] = jnp.broadcast_to(gain_mlp[...], (16, 128))
    g1 = Gather(p, lambda m, e: f1.at[m, e], f1.at[0, 0], g1s)
    g2 = Gather(p, lambda m, e: f2.at[m, e], p2, g2s)
    g1.along_z(z)
    g1.spread(z)
    for i, source in enumerate((wg_t, wu_t, wd_t)):
        p2[i * FFC : (i + 1) * FFC, :] = source[...]
    p2[3 * FFC :, :] = wo[...].T
    own_copy = pltpu.make_async_copy(p2, f2.at[z, d], s_local)
    own_copy.start()

    def arrive(g):
        def visit(m):
            g.z_in(m)
            g.spread(m)
        return visit

    def side(g):
        def visit(m):
            g.x_in(m)
            g.y_in(m)
        return visit

    p.hop(1, arrive(g1))
    side(g1)(z)
    p.hop(2, arrive(g1))
    p.hop(1, side(g1))
    g1.diag_in(z)
    p.hop(3, arrive(g1))
    g2.along_z(z, p2)
    p.hop(2, side(g1))
    p.hop(1, g1.diag_in)
    g1.core_in(z)

    gain_row = jnp.concatenate([f1[z, e, 384:400, :].astype(F32)[0:8] for e in range(8)], axis=1)
    for e in range(8):
        gain_out[:, e * 128 : (e + 1) * 128] = gain_row[:, e * 256 + 128 : e * 256 + 256]

    def norm_body(b, carry):
        x = tok[b].astype(F32)
        factor = lax.rsqrt(jnp.mean(x * x, axis=1, keepdims=True) + EPSILON)
        for e in range(8):
            cols = slice(e * 128, (e + 1) * 128)
            a1[pl.ds(pl.multiple_of(b * CHUNK, CHUNK), CHUNK), cols] = (
                x[:, cols] * factor * gain_row[0:1, e * 256 : e * 256 + 128]
            ).astype(BF)
        return carry

    lax.fori_loop(0, 3, norm_body, 0)

    p.hop(3, side(g1))
    p.hop(2, g1.diag_in)
    p.hop(1, g1.core_in)
    p.hop(3, g1.diag_in)
    p.hop(2, g1.core_in)
    p.hop(3, g1.core_in)
    g2.spread(z, p2)

    def project(b):
        pos_full = pl.ds(pl.multiple_of(z * CHUNK, CHUNK), CHUNK)
        low = jnp.where(z >= 2, z - 2, z)
        pos_half = pl.ds(pl.multiple_of(low * CHUNK, CHUNK), CHUNK)
        second = seq[b] == 2
        cosine = wide(jnp.where(second, cos_t[pos_half, :], cos_t[pos_full, :]))
        sine = wide(jnp.where(second, sin_t[pos_half, :], sin_t[pos_full, :]))
        rows = a1[b * CHUNK : (b + 1) * CHUNK, :]

        def one(step, carry):
            m = lax.rem(z + step, 4)
            w = lambda i: f1[m, :, i * 128 : (i + 1) * 128, :].reshape(1024, CHUNK)
            stage[b, m, 0] = turned(dot(rows, w(0)), cosine, sine).astype(BF)
            stage[b, m, 1] = turned(dot(rows, w(1)), cosine, sine).astype(BF)
            first = fv[b, :, pl.ds(pl.multiple_of(m * CHUNK, CHUNK), CHUNK)].astype(F32)
            stage[b, m, 2] = (0.5 * (dot(rows, w(2)) + first)).astype(BF)
            return carry

        lax.fori_loop(0, 4, one, 0)
        for i in range(3):
            qkv[b, i, pl.ds(pl.multiple_of(z * CHUNK, CHUNK), CHUNK), :] = stage[b, z, i]

    def qkv_copy(b, step):
        m = p.peer(step)
        dst = qkv.at[b, :, pl.ds(pl.multiple_of(z * CHUNK, CHUNK), CHUNK), :]
        return remote(stage.at[b, m], dst, s_qkv.at[b, step - 1], r_qkv.at[b, z], (d, m))

    def send_qkv(b):
        for step in (1, 2, 3):
            qkv_copy(b, step).start()

    def sent_qkv(b):
        for step in (1, 2, 3):
            qkv_copy(b, step).wait_send()

    def take_qkv(b):
        for step in (1, 2, 3):
            m = p.peer(step)
            dst = qkv.at[b, :, pl.ds(pl.multiple_of(m * CHUNK, CHUNK), CHUNK), :]
            remote(stage.at[b, m], dst, s_qkv.at[b, 0], r_qkv.at[b, m], (d, m)).wait_recv()

    def o_copy(b, i):
        rows = slice(i * CHUNK, (i + 1) * CHUNK)
        return remote(o_head.at[b, rows, :], o_rows.at[b, z], s_o.at[b, i], r_o.at[b, z], (d, i))

    def attend(b, i):
        n = (i + 1) * CHUNK
        rows = slice(i * CHUNK, n)
        packed = seq[b]
        q = qkv[b, 0, rows, :]
        keys = qkv[b, 1, 0:n, :]
        values = qkv[b, 2, 0:n, :]
        head_of = lanes((CHUNK, CHUNK), 64)
        lane = lax.broadcasted_iota(jnp.int32, (CHUNK, 128), 1)

        def head(h, carry):
            out, stats = carry
            s = tile_scores(jnp.where(head_of == h, q, jnp.zeros_like(q)), keys, i, packed)
            top = jnp.max(s, axis=1, keepdims=True)
            e = jnp.exp(s - top)
            total = jnp.sum(e, axis=1, keepdims=True)
            part = dot(e.astype(BF), values) * (1.0 / total)
            return (
                jnp.where(head_of == h, part, out),
                jnp.where(lane == h, top + jnp.log(total), stats),
            )

        out, stats = lax.fori_loop(
            0, 4, head, (jnp.zeros((CHUNK, CHUNK), F32), jnp.zeros((CHUNK, 128), F32))
        )
        o_head[b, rows, :] = out.astype(BF)
        lse[b, rows, :] = stats

        @pl.when(z == i)
        def _():
            o_rows[b, z] = out.astype(BF)

        @pl.when(z != i)
        def _():
            o_copy(b, i).start()

    for b in range(3):
        project(b)
        if b == 0:
            send_qkv(0)
    a1_t[...] = a1[...].T
    p.hop(1, g2.z_in)
    sent_qkv(0)
    send_qkv(1)
    p.hop(2, g2.z_in)
    p.hop(3, g2.z_in)
    p.hop(1, g2.spread)
    side(g2)(z)
    p.hop(2, g2.spread)
    take_qkv(0)
    attend(0, 0)
    attend(0, 1)
    p.hop(1, side(g2))
    sent_qkv(1)
    send_qkv(2)
    attend(0, 2)
    attend(0, 3)
    p.hop(3, g2.spread)
    p.hop(2, side(g2))
    take_qkv(1)
    attend(1, 0)
    attend(1, 1)
    g2.diag_in(z)
    p.hop(1, g2.diag_in)
    attend(1, 2)
    attend(1, 3)
    p.hop(3, side(g2))
    p.hop(2, g2.diag_in)
    take_qkv(2)
    attend(2, 0)
    attend(2, 1)
    p.hop(3, g2.diag_in)
    attend(2, 2)
    attend(2, 3)
    sent_qkv(2)
    for m in range(4):
        g2.core_in(m)
    for b in range(3):
        for step in (1, 2, 3):
            m = p.peer(step)
            remote(o_rows.at[b, m], o_rows.at[b, m], s_o.at[b, 0], r_o.at[b, m], (d, m)).wait_recv()
        for i in range(4):

            @pl.when(z != i)
            def _():
                o_copy(b, i).wait_send()

    g1.finish()
    g2.finish()
    own_copy.wait()


def run_forward(*args):
    vmem = pl.BlockSpec(memory_space=pltpu.VMEM)
    hbm = pl.BlockSpec(memory_space=pl.ANY)
    dma = pltpu.SemaphoreType.DMA
    shape = jax.ShapeDtypeStruct
    return pl.pallas_call(
        forward_kernel,
        out_shape=(
            shape((4, 8, QROWS, CHUNK), BF),
            shape((4, 8, PIECE, 128), BF),
            shape((3, 3, 1024, CHUNK), BF),
            shape((3, 1024, CHUNK), BF),
            shape((3, 1024, 128), F32),
            shape((3, 4, CHUNK, CHUNK), BF),
            shape((1024, 768), BF),
            shape((8, 1024), F32),
        ),
        in_specs=[pl.BlockSpec(memory_space=pltpu.SMEM)] + [vmem] * (len(args) - 1),
        out_specs=(vmem, hbm, vmem, vmem, vmem, vmem, vmem, vmem),
        scratch_shapes=[
            pltpu.VMEM((768, 1024), BF),
            pltpu.VMEM((3, 4, 3, CHUNK, CHUNK), BF),
            pltpu.VMEM((PIECE, 128), BF),
        ]
        + gather_sems()
        + gather_sems()
        + [dma((3, 3)), dma((3, 4)), dma((3, 4)), dma((3, 4)), dma],
        compiler_params=pltpu.CompilerParams(
            collective_id=1, has_side_effects=True, vmem_limit_bytes=60 * 2**20
        ),
        cost_estimate=pl.CostEstimate(flops=2 * 10**10, bytes_accessed=6 * 10**7, transcendentals=8 * 10**6),
        name="gather_attend",
    )(*args)


def spans(n, step):
    return [(at, min(step, n - at)) for at in range(0, n, step)]


def mlp_kernel(
    tok, cot, o_rows, f2, gain,
    layer_out, dx2, do_rows, part, gain_part,
    w, wo, a2, hid, dga, dup, acc, back, stage, wo_stage, in_sems, wo_sems, out_sems, wo_out,
):
    def w_copy(m, slot, d):
        return pltpu.make_async_copy(
            f2.at[m, d, 0 : 3 * FFC, :], w.at[slot, :, d * 128 : (d + 1) * 128], in_sems.at[slot, d]
        )

    def wo_copy(m, d):
        return pltpu.make_async_copy(
            f2.at[m, d, 3 * FFC :, :], wo.at[m, :, d * 128 : (d + 1) * 128], wo_sems.at[m, d]
        )

    def out_copy(m, slot):
        return pltpu.make_async_copy(stage.at[slot], part.at[m, :, 0 : 3 * FFC, :], out_sems.at[slot])

    def wo_out_copy(m):
        return pltpu.make_async_copy(wo_stage.at[m], part.at[m, :, 3 * FFC :, :], wo_out.at[m])

    for m in range(4):
        for d in range(8):
            wo_copy(m, d).start()
    for d in range(8):
        w_copy(0, 0, d).start()
    for m in range(4):
        for d in range(8):
            wo_copy(m, d).wait()

    def row_block(b):
        return pl.ds(pl.multiple_of(b * CHUNK, CHUNK), CHUNK)

    def enter(b, carry):
        x2 = tok[b].astype(F32)
        for m in range(4):
            x2 = x2 + dot(o_rows[b, m], wo[m])
        dx2[b] = x2
        factor = lax.rsqrt(jnp.mean(x2 * x2, axis=1, keepdims=True) + EPSILON)
        a2[row_block(b), :] = (x2 * factor * gain[0:1, :]).astype(BF)
        return carry

    lax.fori_loop(0, 3, enter, 0)
    grad = cot[...].reshape(768, 1024)

    def chunk(m, carry):
        slot = lax.rem(m, 2)
        for d in range(8):
            w_copy(m, slot, d).wait()

        @pl.when(m < 3)
        def _():
            for d in range(8):
                w_copy(m + 1, 1 - slot, d).start()

        @pl.when(m >= 2)
        def _():
            out_copy(m - 2, slot).wait()

        for at, size in spans(FFC, 256):
            cols = slice(at, at + size)
            gate = dot_nt(a2[...], w[slot, at : at + size, :])
            up = dot_nt(a2[...], w[slot, FFC + at : FFC + at + size, :])
            dh = dot_nt(grad, w[slot, 2 * FFC + at : 2 * FFC + at + size, :])
            sg = jax.nn.sigmoid(gate)
            act = gate * sg
            hid[:, cols] = (act * up).astype(BF)
            dga[:, cols] = (dh * up * (sg + act * (1.0 - sg))).astype(BF)
            dup[:, cols] = (dh * act).astype(BF)
            for i, (left, right) in enumerate(((dga, a2[...]), (dup, a2[...]), (hid, grad))):
                out = dot_tn(left[:, cols], right).astype(BF)
                for d in range(8):
                    stage[slot, d, i * FFC + at : i * FFC + at + size, :] = out[:, d * 128 : (d + 1) * 128]

        for at, size in spans(1024, 256):
            cols = slice(at, at + size)
            y = dot(hid[...], w[slot, 2 * FFC : 3 * FFC, cols])
            u = dot(dga[...], w[slot, 0:FFC, cols]) + dot(dup[...], w[slot, FFC : 2 * FFC, cols])
            acc[:, cols] = jnp.where(m == 0, y, acc[:, cols] + y)
            back[:, cols] = jnp.where(m == 0, u, back[:, cols] + u)

        out_copy(m, slot).start()
        return carry

    lax.fori_loop(0, 4, chunk, 0)

    def leave(b, total):
        x2 = dx2[b]
        rows = row_block(b)
        layer_out[b] = (x2 + acc[rows, :]).astype(BF)
        factor = lax.rsqrt(jnp.mean(x2 * x2, axis=1, keepdims=True) + EPSILON)
        n2 = x2 * factor
        da2 = back[rows, :]
        total = total + jnp.sum(da2 * n2, axis=0, keepdims=True)
        dn2 = da2 * gain[0:1, :]
        grad_mid = cot[b].astype(F32) + factor * (
            dn2 - n2 * jnp.mean(dn2 * n2, axis=1, keepdims=True)
        )
        dx2[b] = grad_mid
        a2[rows, :] = grad_mid.astype(BF)
        return total

    total = lax.fori_loop(0, 3, leave, jnp.zeros((1, 1024), F32))
    gain_part[...] = jnp.broadcast_to(total, (8, 1024))

    def heads(m, carry):
        own = jnp.concatenate([o_rows[b, m] for b in range(3)], axis=0)
        dw = dot_tn(own, a2[...]).astype(BF)
        for d in range(8):
            wo_stage[m, d] = dw[:, d * 128 : (d + 1) * 128]
        wo_out_copy(m).start()
        for b in range(3):
            do_rows[b, m] = dot_nt(a2[b * CHUNK : (b + 1) * CHUNK, :], wo[m]).astype(BF)
        return carry

    lax.fori_loop(0, 4, heads, 0)
    out_copy(2, 0).wait()
    out_copy(3, 1).wait()
    for m in range(4):
        wo_out_copy(m).wait()


def run_mlp(tok, cot, o_rows, f2, gain):
    vmem = pl.BlockSpec(memory_space=pltpu.VMEM)
    hbm = pl.BlockSpec(memory_space=pl.ANY)
    shape = jax.ShapeDtypeStruct
    dma = pltpu.SemaphoreType.DMA
    return pl.pallas_call(
        mlp_kernel,
        out_shape=(
            shape((3, CHUNK, 1024), BF),
            shape((3, CHUNK, 1024), F32),
            shape((3, 4, CHUNK, CHUNK), BF),
            shape((4, 8, PIECE, 128), BF),
            shape((8, 1024), F32),
        ),
        in_specs=[vmem, vmem, vmem, hbm, vmem],
        out_specs=(vmem, vmem, vmem, hbm, vmem),
        scratch_shapes=[
            pltpu.VMEM((2, 3 * FFC, 1024), BF),
            pltpu.VMEM((4, CHUNK, 1024), BF),
            pltpu.VMEM((768, 1024), BF),
            pltpu.VMEM((768, FFC), BF),
            pltpu.VMEM((768, FFC), BF),
            pltpu.VMEM((768, FFC), BF),
            pltpu.VMEM((768, 1024), F32),
            pltpu.VMEM((768, 1024), F32),
            pltpu.VMEM((2, 8, 3 * FFC, 128), BF),
            pltpu.VMEM((4, 8, CHUNK, 128), BF),
            dma((2, 8)),
            dma((4, 8)),
            dma((2,)),
            dma((4,)),
        ],
        compiler_params=pltpu.CompilerParams(vmem_limit_bytes=60 * 2**20),
        cost_estimate=pl.CostEstimate(flops=5 * 10**10, bytes_accessed=6 * 10**7, transcendentals=2 * 10**6),
        name="mlp",
    )(tok, cot, o_rows, f2, gain)


def backward_kernel(
    seq, do_rows, qkv, o_head, lse, cos_t, sin_t, part,
    d_rows, summed,
    do_head, dk, dv, stage, *rest,
):
    p = Place()
    s_do, r_do, s_d, r_d = rest[:4]
    z, d = p.z, p.d
    p.greet()
    mine = pl.ds(pl.multiple_of(z * CHUNK, CHUNK), CHUNK)

    def do_copy(b, step):
        m = p.peer(step)
        return remote(
            do_rows.at[b, m], do_head.at[b, mine, :], s_do.at[b, step - 1], r_do.at[b, z], (d, m)
        )

    def send_do(b):
        for step in (1, 2, 3):
            do_copy(b, step).start()
        do_head[b, mine, :] = do_rows[b, z]

    def take_do(b):
        for step in (1, 2, 3):
            m = p.peer(step)
            dst = do_head.at[b, pl.ds(pl.multiple_of(m * CHUNK, CHUNK), CHUNK), :]
            remote(do_rows.at[b, m], dst, s_do.at[b, 0], r_do.at[b, m], (d, m)).wait_recv()

    def d_copy(b, i):
        return remote(stage.at[b, i], d_rows.at[b, z], s_d.at[b, i], r_d.at[b, z], (d, i))

    def back(b, i):
        n = (i + 1) * CHUNK
        rows = slice(i * CHUNK, n)
        packed = seq[b]
        head_of = lanes((CHUNK, CHUNK), 64)
        lane = lax.broadcasted_iota(jnp.int32, (CHUNK, 128), 1)
        q = qkv[b, 0, rows, :]
        keys = qkv[b, 1, 0:n, :]
        values = qkv[b, 2, 0:n, :]
        grad = do_head[b, rows, :]
        spread = grad.astype(F32) * o_head[b, rows, :].astype(F32)
        stats = lse[b, rows, :]

        def head(h, dq):
            here = head_of == h
            q_h = jnp.where(here, q, jnp.zeros_like(q))
            g_h = jnp.where(here, grad, jnp.zeros_like(grad))
            delta = jnp.sum(jnp.where(here, spread, 0.0), axis=1, keepdims=True)
            level = jnp.sum(jnp.where(lane == h, stats, 0.0), axis=1, keepdims=True)
            prob = jnp.exp(tile_scores(q_h, keys, i, packed) - level)
            dp = dot_nt(g_h, values)
            ds = (prob * (dp - delta)).astype(BF)
            dv_part = dot_tn(prob.astype(BF), g_h)
            dk_part = dot_tn(ds, q_h)
            dv[0:n, :] += dv_part
            dk[0:n, :] += dk_part
            return jnp.where(here, dot(ds, keys), dq)

        dq = lax.fori_loop(0, 4, head, jnp.zeros((CHUNK, CHUNK), F32))
        cosine, sine = cos_t[rows, :], sin_t[rows, :]
        if i >= 2:
            early = slice((i - 2) * CHUNK, (i - 1) * CHUNK)
            cosine = jnp.where(packed == 2, cos_t[early, :], cosine)
            sine = jnp.where(packed == 2, sin_t[early, :], sine)
        cosine, sine = wide(cosine), -wide(sine)
        stage[b, i, :, 0:256] = turned(dq * 0.125, cosine, sine).astype(BF)
        stage[b, i, :, 256:512] = turned(dk[rows, :] * 0.125, cosine, sine).astype(BF)
        stage[b, i, :, 512:768] = (dv[rows, :] * 0.5).astype(BF)

        @pl.when(z == i)
        def _():
            d_rows[b, z] = stage[b, i]

        @pl.when(z != i)
        def _():
            d_copy(b, i).start()

    crossing = Crossing(p, lambda m, e: part.at[m, e], rest[4:9], rest[9:], summed, 592)
    for b in range(3):
        send_do(b)
    plan = crossing.steps()
    for b in range(3):
        take_do(b)
        dk[...] = jnp.zeros_like(dk)
        dv[...] = jnp.zeros_like(dv)
        for i in (3, 2, 1, 0):
            back(b, i)
            for step in plan[:2]:
                step()
            plan = plan[2:]
    for step in plan:
        step()
    crossing.finish()
    for b in range(3):
        for step in (1, 2, 3):
            do_copy(b, step).wait_send()
            m = p.peer(step)
            remote(d_rows.at[b, m], d_rows.at[b, m], s_d.at[b, 0], r_d.at[b, m], (d, m)).wait_recv()
        for i in range(4):

            @pl.when(z != i)
            def _():
                d_copy(b, i).wait_send()


def run_backward(*args):
    vmem = pl.BlockSpec(memory_space=pltpu.VMEM)
    hbm = pl.BlockSpec(memory_space=pl.ANY)
    dma = pltpu.SemaphoreType.DMA
    shape = jax.ShapeDtypeStruct
    return pl.pallas_call(
        backward_kernel,
        out_shape=(shape((3, 4, CHUNK, 768), BF), shape((4, PIECE, 128), BF)),
        in_specs=[pl.BlockSpec(memory_space=pltpu.SMEM)] + [vmem] * 6 + [hbm],
        out_specs=(vmem, vmem),
        scratch_shapes=[
            pltpu.VMEM((3, 1024, CHUNK), BF),
            pltpu.VMEM((1024, CHUNK), F32),
            pltpu.VMEM((1024, CHUNK), F32),
            pltpu.VMEM((3, 4, CHUNK, 768), BF),
            dma((3, 3)),
            dma((3, 4)),
            dma((3, 4)),
            dma((3, 4)),
        ]
        + crossing_scratch(PIECE, 128),
        compiler_params=pltpu.CompilerParams(
            collective_id=2, has_side_effects=True, vmem_limit_bytes=60 * 2**20
        ),
        cost_estimate=pl.CostEstimate(flops=3 * 10**10, bytes_accessed=2 * 10**7, transcendentals=8 * 10**6),
        name="attend_back",
    )(*args)


ORDER = (3, 0, 1, 2)


def add_rows(dst, terms, step):
    def rows(r, carry):
        at = pl.ds(pl.multiple_of(r * step, step), step)
        total = terms[0][at, :].astype(F32)
        for term in terms[1:]:
            total = total + term[at, :].astype(F32)
        dst[at, :] = total.astype(dst.dtype)
        return carry

    lax.fori_loop(0, dst.shape[0] // step, rows, 0)


class Crossing:
    def __init__(self, place, part, bufs, sems, out, step):
        self.p, self.part, self.out, self.step = place, part, out, step
        self.own, self.acc, self.corner, self.bx, self.by = bufs
        (self.l_own, self.s_core, self.r_core, self.s_corner, self.r_corner,
         self.s_x, self.r_x, self.s_y, self.r_y) = sems

    def core_copy(self, m, q):
        p = self.p
        return remote(
            self.part(m, p.core_quads[q]), self.acc.at[m, q],
            self.s_core.at[m, q], self.r_core.at[m, q], p.core,
        )

    def own_copy(self, m, q):
        slot = ORDER.index(m) % 2
        return pltpu.make_async_copy(
            self.part(m, self.p.quads[q]), self.own.at[slot, q], self.l_own.at[slot, q]
        )

    def begin(self, m):
        for q in (3, 1, 2, 0):
            self.core_copy(m, q).start()

    def load(self, m):
        for q in (3, 1, 2, 0):
            self.own_copy(m, q).start()

    def corner_copy(self, m):
        to = self.p.x if m % 2 == 0 else self.p.y
        return remote(self.acc.at[m, 3], self.corner.at[m], self.s_corner.at[m], self.r_corner.at[m], to)

    def x_copy(self, m):
        return remote(self.acc.at[m, 1], self.bx.at[m], self.s_x.at[m], self.r_x.at[m], self.p.x)

    def y_copy(self, m):
        return remote(self.acc.at[m, 2], self.by.at[m], self.s_y.at[m], self.r_y.at[m], self.p.y)

    def join(self, m):
        slot = ORDER.index(m) % 2
        first = 1 if m % 2 == 0 else 2
        for q in (3, first, 3 - first, 0):
            self.own_copy(m, q).wait()
            self.core_copy(m, q).wait_recv()
            add_rows(self.acc.at[m, q], [self.acc.at[m, q], self.own.at[slot, q]], self.step)
            if q == 3:
                self.corner_copy(m).start()
            if q == first:
                (self.x_copy if m % 2 == 0 else self.y_copy)(m).start()

    def relay(self, m):
        q = 2 if m % 2 == 0 else 1
        self.corner_copy(m).wait_recv()
        add_rows(self.acc.at[m, q], [self.acc.at[m, q], self.corner.at[m]], self.step)
        (self.y_copy if m % 2 == 0 else self.x_copy)(m).start()

    def total(self, m):
        self.x_copy(m).wait_recv()
        self.y_copy(m).wait_recv()
        add_rows(self.out.at[m], [self.acc.at[m, 0], self.bx.at[m], self.by.at[m]], self.step)

    def finish(self):
        for m in range(4):
            for q in range(4):
                self.core_copy(m, q).wait_send()
            self.corner_copy(m).wait_send()
            self.x_copy(m).wait_send()
            self.y_copy(m).wait_send()

    def steps(self):
        a, b, c, e = ORDER

        def start():
            for m in ORDER:
                self.begin(m)
            self.load(a)
            self.load(b)

        def join_then_load(m, after):
            self.join(m)
            self.load(after)

        return [
            start,
            lambda: join_then_load(a, c),
            lambda: join_then_load(b, e),
            lambda: self.relay(a),
            lambda: self.relay(b),
            lambda: self.join(c),
            lambda: self.join(e),
            lambda: self.total(a),
            lambda: self.total(b),
            lambda: self.relay(c),
            lambda: self.relay(e),
            lambda: self.total(c),
            lambda: self.total(e),
        ]


def crossing_scratch(rows, width):
    def buf(*lead):
        return pltpu.VMEM((*lead, rows, width), BF)

    dma = pltpu.SemaphoreType.DMA
    return [buf(2, 4), buf(4, 4), buf(4), buf(4), buf(4), dma((2, 4)), dma((4, 4)), dma((4, 4))] + [dma((4,))] * 6


class Chain:
    def __init__(self, place, part, bufs, sems, out, step):
        self.p, self.part, self.out, self.step = place, part, out, step
        self.br, self.bl = bufs
        self.s_r, self.r_r, self.s_l, self.r_l = sems

    def r_copy(self, m):
        p = self.p
        return remote(self.part.at[m], self.br.at[m], self.s_r.at[m], self.r_r.at[m], (p.d, p.z + 1))

    def l_copy(self, m):
        p = self.p
        return remote(self.part.at[m], self.bl.at[m], self.s_l.at[m], self.r_l.at[m], (p.d, p.z - 1))

    def along(self, m):
        z = self.p.z

        if m > 0:

            @pl.when(z < m)
            def _():
                @pl.when(z > 0)
                def _():
                    self.r_copy(m).wait_recv()
                    add_rows(self.part.at[m], [self.part.at[m], self.br.at[m]], self.step)

                self.r_copy(m).start()

        if m < 3:

            @pl.when(z > m)
            def _():
                @pl.when(z < 3)
                def _():
                    self.l_copy(m).wait_recv()
                    add_rows(self.part.at[m], [self.part.at[m], self.bl.at[m]], self.step)

                self.l_copy(m).start()

    def last(self):
        for m in range(4):

            @pl.when(self.p.z == m)
            def _():
                terms = [self.part.at[m]]
                if m > 0:
                    self.r_copy(m).wait_recv()
                    terms.append(self.br.at[m])
                if m < 3:
                    self.l_copy(m).wait_recv()
                    terms.append(self.bl.at[m])
                add_rows(self.out, terms, self.step)

    def finish(self):
        for m in range(4):
            if m > 0:

                @pl.when(self.p.z < m)
                def _():
                    self.r_copy(m).wait_send()

            if m < 3:

                @pl.when(self.p.z > m)
                def _():
                    self.l_copy(m).wait_send()


def chain_scratch(rows, width):
    dma = pltpu.SemaphoreType.DMA
    return [pltpu.VMEM((4, rows, width), BF)] * 2 + [dma((4,))] * 4


def finish_kernel(
    tok, mid, d_rows, a1_t, f1, gain_part, summed,
    grad_tokens, grad_first, dw1, dw2, gain_sum,
    part, acc, total1, total2, gbuf, *rest,
):
    p = Place()
    p.greet()
    rest = list(rest)
    cross = Crossing(p, lambda m, e: part.at[m, e], rest[:5], rest[5:14], total1, 16)
    chain1 = Chain(p, total1, rest[14:16], rest[16:20], dw1, 16)
    chain2 = Chain(p, total2, rest[20:22], rest[22:26], dw2, 592)
    s_gain, r_gain, l_total = rest[26:29]

    def total_copy(m):
        return pltpu.make_async_copy(summed.at[m], total2.at[m], l_total.at[m])

    def along2(m):
        total_copy(m).wait()
        chain2.along(m)

    for m in ORDER:
        total_copy(m).start()

    def weight_grad(m):
        cols = jnp.concatenate([d_rows[b, m] for b in range(3)], axis=0)

        def rows(k, carry):
            at = pl.ds(pl.multiple_of(k * CHUNK, CHUNK), CHUNK)
            part[m, pl.ds(2 * k, 2)] = dot(a1_t[at, :], cols).astype(BF).reshape(2, 128, 768)
            return carry

        lax.fori_loop(0, 4, rows, 0)

    def input_grad(m):
        cols = jnp.concatenate([d_rows[b, m] for b in range(3)], axis=0)

        def tile(k, carry):
            w = jnp.concatenate(
                [f1[m, pl.ds(2 * k, 2), i * 128 : (i + 1) * 128, :].reshape(CHUNK, CHUNK) for i in range(3)],
                axis=1,
            )
            at = pl.ds(pl.multiple_of(k * CHUNK, CHUNK), CHUNK)
            y = dot_nt(cols, w)
            if m == 0:
                acc[:, at] = y
            else:
                acc[:, at] += y
            return carry

        lax.fori_loop(0, 4, tile, 0)

    def leave(b, total):
        x = tok[b].astype(F32)
        factor = lax.rsqrt(jnp.mean(x * x, axis=1, keepdims=True) + EPSILON)
        n1 = x * factor
        da1 = acc[pl.ds(pl.multiple_of(b * CHUNK, CHUNK), CHUNK), :]
        total = total + jnp.sum(da1 * n1, axis=0, keepdims=True)
        gain = jnp.concatenate([f1[0, e, 384:400, 0:128].astype(F32)[0:1] for e in range(8)], axis=1)
        dn1 = da1 * gain
        grad_tokens[b] = mid[b] + factor * (dn1 - n1 * jnp.mean(dn1 * n1, axis=1, keepdims=True))
        for m in range(4):
            grad_first[b, :, m * CHUNK : (m + 1) * CHUNK] = d_rows[b, m, :, 512:768].astype(F32)
        return total

    def gain_copy(i, device):
        return remote(gbuf.at[0] if i == 0 else gbuf.at[4 + i], gbuf.at[1 + i], s_gain.at[i], r_gain.at[i], device)

    a, b, c, e = ORDER
    weight_grad(a)
    cross.begin(a)
    cross.load(a)
    along2(a)
    weight_grad(b)
    cross.begin(b)
    cross.load(b)
    along2(b)
    cross.join(a)
    weight_grad(c)
    cross.begin(c)
    cross.load(c)
    along2(c)
    cross.join(b)
    weight_grad(e)
    cross.begin(e)
    cross.load(e)
    along2(e)
    cross.relay(a)
    cross.relay(b)
    cross.join(c)
    cross.join(e)
    input_grad(0)
    cross.relay(c)
    cross.relay(e)
    cross.total(a)
    chain1.along(a)
    input_grad(1)
    cross.total(b)
    chain1.along(b)
    input_grad(2)
    input_grad(3)
    cross.total(c)
    chain1.along(c)
    cross.total(e)
    chain1.along(e)
    total = lax.fori_loop(0, 3, leave, jnp.zeros((1, 1024), F32))
    row = lax.broadcasted_iota(jnp.int32, (8, 1024), 0)
    gbuf[0] = jnp.where(row == 0, total, gain_part[...])
    gain_copy(0, p.core).start()
    chain2.last()
    gain_copy(0, p.core).wait_recv()
    gbuf[5] = gbuf[0] + gbuf[1]
    gain_copy(1, p.x).start()
    chain1.last()
    gain_copy(1, p.x).wait_recv()
    gbuf[6] = gbuf[5] + gbuf[2]
    gain_copy(2, p.y).start()
    gain_copy(2, p.y).wait_recv()
    gbuf[7] = gbuf[6] + gbuf[3]
    for step in (1, 2, 3):
        m = p.peer(step)
        remote(gbuf.at[7], gbuf.at[8 + p.z], s_gain.at[2 + step], r_gain.at[3 + p.z], (p.d, m)).start()
    gbuf[8 + p.z] = gbuf[7]
    for step in (1, 2, 3):
        m = p.peer(step)
        remote(gbuf.at[7], gbuf.at[8 + m], s_gain.at[2 + step], r_gain.at[3 + m], (p.d, m)).wait_recv()
    gain_sum[...] = (gbuf[8] + gbuf[9]) + (gbuf[10] + gbuf[11])
    for i, device in enumerate((p.core, p.x, p.y)):
        gain_copy(i, device).wait_send()
    for step in (1, 2, 3):
        m = p.peer(step)
        remote(gbuf.at[7], gbuf.at[8 + m], s_gain.at[2 + step], r_gain.at[3 + m], (p.d, m)).wait_send()
    cross.finish()
    chain1.finish()
    chain2.finish()


def run_finish(*args):
    vmem = pl.BlockSpec(memory_space=pltpu.VMEM)
    dma = pltpu.SemaphoreType.DMA
    shape = jax.ShapeDtypeStruct
    return pl.pallas_call(
        finish_kernel,
        out_shape=(
            shape((3, CHUNK, 1024), F32),
            shape((3, CHUNK, 1024), F32),
            shape((128, 768), F32),
            shape((PIECE, 128), F32),
            shape((8, 1024), F32),
        ),
        in_specs=[vmem] * (len(args) - 1) + [pl.BlockSpec(memory_space=pl.ANY)],
        out_specs=(vmem,) * 5,
        scratch_shapes=[
            pltpu.VMEM((4, 8, 128, 768), BF),
            pltpu.VMEM((768, 1024), F32),
            pltpu.VMEM((4, 128, 768), BF),
            pltpu.VMEM((4, PIECE, 128), BF),
            pltpu.VMEM((12, 8, 1024), F32),
        ]
        + crossing_scratch(128, 768)
        + chain_scratch(128, 768)
        + chain_scratch(PIECE, 128)
        + [dma((6,)), dma((7,)), dma((4,))],
        compiler_params=pltpu.CompilerParams(
            collective_id=3, has_side_effects=True, vmem_limit_bytes=60 * 2**20
        ),
        cost_estimate=pl.CostEstimate(flops=10**10, bytes_accessed=5 * 10**7, transcendentals=0),
        name="sum_grads",
    )(*args)


def fast_body(
    tokens, first_values, sequences, w_query, w_key, w_value, w_out, w_gate, w_up, w_down,
    gain_attn, gain_mlp, cotangent,
):
    seq = sequences[:, 0]
    cos_t, sin_t = rope_tables()
    f1, f2, qkv, o_head, lse, o_rows, a1_t, gain_out = run_forward(
        seq, tokens, first_values, w_query, w_key, w_value, w_out, w_gate.T, w_up.T, w_down.T,
        gain_attn[None, :], gain_mlp[None, :], cos_t, sin_t,
    )
    layer_out, mid, do_rows, part, gain_part = run_mlp(tokens, cotangent, o_rows, f2, gain_out)
    d_rows, summed = run_backward(seq, do_rows, qkv, o_head, lse, cos_t, sin_t, part)
    grad_tokens, grad_first, dw1, dw2, gain_sum = run_finish(tokens, mid, d_rows, a1_t, f1, gain_part, summed)
    place = (lax.axis_index("dp") * 4 + lax.axis_index("mp")) * 32
    gain_mine = lax.dynamic_slice(gain_sum, (0, place), (2, 32))
    return (
        layer_out,
        grad_tokens,
        grad_first,
        dw1[:, 0:256],
        dw1[:, 256:512],
        dw1[:, 512:768],
        dw2[3 * FFC :].T,
        dw2[0:FFC].T,
        dw2[FFC : 2 * FFC].T,
        dw2[2 * FFC : 3 * FFC].T,
        gain_mine[0],
        gain_mine[1],
    )


def is_small(mesh):
    return mesh.axis_names == ("dp", "mp") and tuple(mesh.devices.shape) == (8, 4)


def solution(mesh):
    return jax.shard_map(
        fast_body if is_small(mesh) else body,
        mesh=mesh,
        in_specs=(
            P(None, ("dp", "mp"), None),
            P(None, ("dp", "mp"), None),
            P(None, "dp"),
            P("dp", "mp"),
            P("dp", "mp"),
            P("dp", "mp"),
            P("dp", "mp"),
            P("dp", "mp"),
            P("dp", "mp"),
            P("dp", "mp"),
            P("dp"),
            P("dp"),
            P(None, ("dp", "mp"), None),
        ),
        out_specs=(
            P(None, ("dp", "mp"), None),
            P(None, ("dp", "mp"), None),
            P(None, ("dp", "mp"), None),
            P("dp", "mp"),
            P("dp", "mp"),
            P("dp", "mp"),
            P("dp", "mp"),
            P("dp", "mp"),
            P("dp", "mp"),
            P("dp", "mp"),
            P(("dp", "mp")),
            P(("dp", "mp")),
        ),
        check_vma=False,
    )
```

```python
import jax
import jax.numpy as jnp
import numpy as np
from jax import lax
from jax.experimental import pallas as pl
from jax.experimental.pallas import tpu as pltpu
from jax.sharding import PartitionSpec as P

HEAD_DIM = 64


EPSILON = 1e-06
THETA = 10000.0


def normalize(rows):
    factor = lax.rsqrt(jnp.mean(rows * rows, axis=-1, keepdims=True) + EPSILON)
    return (rows * factor, factor)


def norm_back(grad_normed, normed, factor):
    return factor * (grad_normed - normed * jnp.mean(grad_normed * normed, axis=-1, keepdims=True))


def rotary_tables(position, head_size):
    halfway = head_size // 2
    inverse = THETA ** (-2.0 * jnp.arange(halfway, dtype=jnp.float32) / head_size)
    angles = position.astype(jnp.float32)[:, None] * inverse[None, :]
    return (jnp.cos(angles), jnp.sin(angles))


def rotate(values, cosine, sine, direction):
    halfway = values.shape[-1] // 2
    former = values[..., :halfway]
    latter = values[..., halfway:]
    cos_rows = cosine[:, None, :]
    sin_rows = direction * sine[:, None, :]
    return jnp.concatenate(
        [former * cos_rows - latter * sin_rows, latter * cos_rows + former * sin_rows], axis=-1
    )


def layout(packed, length):
    index_rows = jnp.arange(length, dtype=jnp.int32)
    second = jnp.where((packed == 2) & (index_rows >= length // 2), 1, 0).astype(jnp.int32)
    return (second, index_rows - second * (length // 2))


def block_scores(query, key_rows, second, offset, block_rows, key_end, scale):
    raw = (
        jnp.einsum(
            "qhd,khd->hqk",
            query[offset : offset + block_rows],
            key_rows,
            preferred_element_type=jnp.float32,
        )
        * scale
    )
    row_ids = offset + jnp.arange(block_rows, dtype=jnp.int32)
    col_ids = jnp.arange(key_end, dtype=jnp.int32)
    allowed = (col_ids[None, :] <= row_ids[:, None]) & (
        second[offset : offset + block_rows][:, None] == second[None, :]
    )
    return jnp.where(allowed[None], raw, -1e30)


def whole_rows(part):
    return lax.all_gather(part, "mp", axis=0, tiled=True)


def summed_rows(term, local_rows):
    return lax.psum_scatter(
        term(jnp.int32(0), local_rows * lax.axis_size("mp")).astype(jnp.bfloat16),
        "mp",
        scatter_dimension=0,
        tiled=True,
    ).astype(jnp.float32)


def fetch(w_query, w_key, w_value, w_out, w_gate, w_up, w_down, gain_attn, gain_mlp):
    return (
        lax.all_gather(w_query, "dp", axis=0, tiled=True),
        lax.all_gather(w_key, "dp", axis=0, tiled=True),
        lax.all_gather(w_value, "dp", axis=0, tiled=True),
        lax.all_gather(w_out, "dp", axis=0, tiled=True),
        lax.all_gather(w_gate, "dp", axis=0, tiled=True),
        lax.all_gather(w_up, "dp", axis=0, tiled=True),
        lax.all_gather(w_down, "dp", axis=0, tiled=True),
        lax.all_gather(gain_attn, "dp", axis=0, tiled=True),
        lax.all_gather(gain_mlp, "dp", axis=0, tiled=True),
    )


def project_back(left, right):
    return jnp.einsum("rc,dc->rd", left, right, preferred_element_type=jnp.float32)


def outer_sum(left, right):
    return jnp.einsum("td,tc->dc", left, right, preferred_element_type=jnp.float32)


def body(
    tokens,
    first_values,
    sequences,
    w_query,
    w_key,
    w_value,
    w_out,
    w_gate,
    w_up,
    w_down,
    gain_attn,
    gain_mlp,
    cotangent,
):
    micro = tokens.shape[0]
    local_rows = tokens.shape[1]
    length = local_rows * lax.axis_size("mp")
    heads_here = w_query.shape[1] // HEAD_DIM
    block_rows = min(512, length)
    scale = HEAD_DIM ** (-0.5)
    saved = []
    outputs = []
    for batch in range(micro):
        full = fetch(w_query, w_key, w_value, w_out, w_gate, w_up, w_down, gain_attn, gain_mlp)
        q_full, k_full, v_full, o_full, gate_full, up_full, down_full, gain_one, gain_two = full
        gain_one = gain_one.astype(jnp.float32)
        gain_two = gain_two.astype(jnp.float32)
        x_rows = tokens[batch].astype(jnp.float32)
        normed_one, factor_one = normalize(x_rows)
        input_one = whole_rows((normed_one * gain_one[None, :]).astype(jnp.bfloat16))
        second, position = layout(sequences[batch, 0], length)
        cosine, sine = rotary_tables(position, HEAD_DIM)
        query = jnp.dot(input_one, q_full, preferred_element_type=jnp.float32).reshape(
            length, heads_here, HEAD_DIM
        )
        query = rotate(query, cosine, sine, 1.0).astype(jnp.bfloat16)
        key_rows = jnp.dot(input_one, k_full, preferred_element_type=jnp.float32).reshape(
            length, heads_here, HEAD_DIM
        )
        key_rows = rotate(key_rows, cosine, sine, 1.0).astype(jnp.bfloat16)
        first_here = lax.all_to_all(
            first_values[batch], "mp", split_axis=1, concat_axis=0, tiled=True
        )
        mixed = 0.5 * (
            jnp.dot(input_one, v_full, preferred_element_type=jnp.float32)
            + first_here.astype(jnp.float32)
        )
        mixed = mixed.astype(jnp.bfloat16).reshape(length, heads_here, HEAD_DIM)
        pieces = []
        logsums = []
        for offset in range(0, length, block_rows):
            key_end = length
            scores = block_scores(query, key_rows, second, offset, block_rows, key_end, scale)
            highest = jnp.max(scores, axis=-1, keepdims=True)
            powers = jnp.exp(scores - highest)
            denominator = jnp.sum(powers, axis=-1, keepdims=True)
            probs_low = (powers / denominator).astype(jnp.bfloat16)
            logsums.append(highest + jnp.log(denominator))
            pieces.append(
                jnp.einsum("hqk,khd->qhd", probs_low, mixed, preferred_element_type=jnp.float32)
            )
        attended = (
            jnp.concatenate(pieces, axis=0)
            .reshape(length, heads_here * HEAD_DIM)
            .astype(jnp.bfloat16)
        )

        def attn_term(offset, amount):
            return project_back(attended, o_full)

        mid_rows = x_rows + summed_rows(attn_term, local_rows)
        normed_two, factor_two = normalize(mid_rows)
        input_two = whole_rows((normed_two * gain_two[None, :]).astype(jnp.bfloat16))
        gate = jnp.dot(input_two, gate_full, preferred_element_type=jnp.float32)
        upward = jnp.dot(input_two, up_full, preferred_element_type=jnp.float32)
        sigma = jax.nn.sigmoid(gate)
        hidden = (gate * sigma * upward).astype(jnp.bfloat16)

        def mlp_term(offset, amount):
            return project_back(hidden, down_full)

        mlp_rows = summed_rows(mlp_term, local_rows)
        outputs.append((mid_rows + mlp_rows).astype(jnp.bfloat16))
        saved.append(
            (
                normed_one,
                factor_one,
                input_one,
                second,
                cosine,
                sine,
                query,
                key_rows,
                mixed,
                logsums,
                attended,
                normed_two,
                factor_two,
                input_two,
                gate,
                sigma,
                upward,
                hidden,
            )
        )
    grad_sum = None
    gain_grad_one = jnp.zeros((tokens.shape[2],), jnp.float32)
    gain_grad_two = jnp.zeros((tokens.shape[2],), jnp.float32)
    grad_tokens = []
    grad_first = []
    for batch in range(micro):
        (
            normed_one,
            factor_one,
            input_one,
            second,
            cosine,
            sine,
            query,
            key_rows,
            mixed,
            logsums,
            attended,
            normed_two,
            factor_two,
            input_two,
            gate,
            sigma,
            upward,
            hidden,
        ) = saved[batch]
        full = fetch(w_query, w_key, w_value, w_out, w_gate, w_up, w_down, gain_attn, gain_mlp)
        q_full, k_full, v_full, o_full, gate_full, up_full, down_full, gain_one, gain_two = full
        gain_one = gain_one.astype(jnp.float32)
        gain_two = gain_two.astype(jnp.float32)
        grad_rows = cotangent[batch]
        grad_full = whole_rows(grad_rows)
        grad_down = outer_sum(grad_full, hidden)
        grad_hidden = jnp.dot(grad_full, down_full, preferred_element_type=jnp.float32)
        grad_gate = (grad_hidden * upward * sigma * (1.0 + gate * (1.0 - sigma))).astype(
            jnp.bfloat16
        )
        grad_up = (grad_hidden * gate * sigma).astype(jnp.bfloat16)
        grad_gate_w = outer_sum(input_two, grad_gate)
        grad_up_w = outer_sum(input_two, grad_up)

        def mlp_back(offset, amount):
            return project_back(grad_gate, gate_full) + project_back(grad_up, up_full)

        grad_input_two = summed_rows(mlp_back, local_rows)
        gain_grad_two = gain_grad_two + jnp.sum(grad_input_two * normed_two, axis=0)
        grad_mid = grad_rows.astype(jnp.float32) + norm_back(
            grad_input_two * gain_two[None, :], normed_two, factor_two
        )
        grad_attn = whole_rows(grad_mid.astype(jnp.bfloat16))
        grad_out_w = outer_sum(grad_attn, attended)
        grad_attended = jnp.dot(grad_attn, o_full, preferred_element_type=jnp.float32)
        grad_attended = grad_attended.astype(jnp.bfloat16).reshape(length, heads_here, HEAD_DIM)
        grad_mixed = jnp.zeros((length, heads_here, HEAD_DIM), jnp.float32)
        grad_key = jnp.zeros((length, heads_here, HEAD_DIM), jnp.float32)
        query_parts = []
        for turn, offset in enumerate(range(0, length, block_rows)):
            key_end = length
            scores = block_scores(query, key_rows, second, offset, block_rows, key_end, scale)
            probs = jnp.exp(scores - logsums[turn])
            grad_block = grad_attended[offset : offset + block_rows]
            grad_probs = jnp.einsum(
                "qhd,khd->hqk", grad_block, mixed, preferred_element_type=jnp.float32
            )
            grad_mixed = grad_mixed.at[:key_end].add(
                jnp.einsum(
                    "hqk,qhd->khd",
                    probs.astype(jnp.bfloat16),
                    grad_block,
                    preferred_element_type=jnp.float32,
                )
            )
            grad_scores = probs * (grad_probs - jnp.sum(probs * grad_probs, axis=-1, keepdims=True))
            grad_scores = grad_scores.astype(jnp.bfloat16)
            query_parts.append(
                jnp.einsum(
                    "hqk,khd->qhd", grad_scores, key_rows, preferred_element_type=jnp.float32
                )
                * scale
            )
            grad_key = grad_key.at[:key_end].add(
                jnp.einsum(
                    "hqk,qhd->khd",
                    grad_scores,
                    query[offset : offset + block_rows],
                    preferred_element_type=jnp.float32,
                )
                * scale
            )
        grad_mixed_low = grad_mixed.reshape(length, heads_here * HEAD_DIM).astype(jnp.bfloat16)
        grad_value = (0.5 * grad_mixed_low.astype(jnp.float32)).astype(jnp.bfloat16)
        grad_query = rotate(jnp.concatenate(query_parts, axis=0), cosine, sine, -1.0)
        grad_query = grad_query.reshape(length, heads_here * HEAD_DIM).astype(jnp.bfloat16)
        grad_key_low = (
            rotate(grad_key, cosine, sine, -1.0)
            .reshape(length, heads_here * HEAD_DIM)
            .astype(jnp.bfloat16)
        )
        grad_query_w = outer_sum(input_one, grad_query)
        grad_key_w = outer_sum(input_one, grad_key_low)
        grad_value_w = outer_sum(input_one, grad_value)

        def attn_back(offset, amount):
            return (
                project_back(grad_query, q_full)
                + project_back(grad_key_low, k_full)
                + project_back(grad_value, v_full)
            )

        grad_input_one = summed_rows(attn_back, local_rows)
        gain_grad_one = gain_grad_one + jnp.sum(grad_input_one * normed_one, axis=0)
        grad_tokens.append(
            grad_mid + norm_back(grad_input_one * gain_one[None, :], normed_one, factor_one)
        )
        returned = lax.all_to_all(grad_mixed_low, "mp", split_axis=0, concat_axis=1, tiled=True)
        grad_first.append(0.5 * returned.astype(jnp.float32))
        shared = (
            lax.psum_scatter(
                grad_query_w.astype(jnp.bfloat16), "dp", scatter_dimension=0, tiled=True
            ).astype(jnp.float32),
            lax.psum_scatter(
                grad_key_w.astype(jnp.bfloat16), "dp", scatter_dimension=0, tiled=True
            ).astype(jnp.float32),
            lax.psum_scatter(
                grad_value_w.astype(jnp.bfloat16), "dp", scatter_dimension=0, tiled=True
            ).astype(jnp.float32),
            lax.psum_scatter(
                grad_out_w.astype(jnp.bfloat16), "dp", scatter_dimension=0, tiled=True
            ).astype(jnp.float32),
            lax.psum_scatter(
                grad_gate_w.astype(jnp.bfloat16), "dp", scatter_dimension=0, tiled=True
            ).astype(jnp.float32),
            lax.psum_scatter(
                grad_up_w.astype(jnp.bfloat16), "dp", scatter_dimension=0, tiled=True
            ).astype(jnp.float32),
            lax.psum_scatter(
                grad_down.astype(jnp.bfloat16), "dp", scatter_dimension=0, tiled=True
            ).astype(jnp.float32),
        )
        grad_sum = shared if grad_sum is None else jax.tree.map(jnp.add, grad_sum, shared)
    gain_parts = (
        lax.psum_scatter(gain_grad_one, ("dp", "mp"), scatter_dimension=0, tiled=True),
        lax.psum_scatter(gain_grad_two, ("dp", "mp"), scatter_dimension=0, tiled=True),
    )
    return (
        jnp.stack(outputs),
        jnp.stack(grad_tokens),
        jnp.stack(grad_first),
        grad_sum[0],
        grad_sum[1],
        grad_sum[2],
        grad_sum[3],
        grad_sum[4],
        grad_sum[5],
        grad_sum[6],
        gain_parts[0],
        gain_parts[1],
    )


def rope_tables():
    half = HEAD_DIM // 2
    inverse = (THETA ** (-2.0 * np.arange(half) / HEAD_DIM)).astype(np.float32)
    angles = np.arange(1024, dtype=np.float32)[:, None] * inverse[None, :]
    cosine, sine = np.cos(angles), np.sin(angles)
    return (
        jnp.asarray(np.concatenate([cosine] * 4, axis=1), jnp.float32),
        jnp.asarray(np.concatenate([-sine, sine, -sine, sine], axis=1), jnp.float32),
    )


BF = jnp.bfloat16
F32 = jnp.float32
MESH = pl.DeviceIdType.MESH
CHUNK = 256
FFC = 704
PIECE = 3 * FFC + 256
QROWS = 400


def remote(src, dst, send, recv, device):
    return pltpu.make_async_remote_copy(
        src_ref=src, dst_ref=dst, send_sem=send, recv_sem=recv, device_id=device, device_id_type=MESH
    )


class Place:
    def __init__(self):
        self.d = d = lax.axis_index("dp")
        self.z = z = lax.axis_index("mp")
        core = lax.rem(d, 2)
        along_x = lax.rem(lax.div(d, 2), 2)
        along_y = lax.div(d, 4)
        self.dc = d + 1 - 2 * core
        self.dx = d + 2 - 4 * along_x
        self.dy = d + 4 - 8 * along_y
        self.dxy = self.dx + 4 - 8 * along_y
        self.core = (self.dc, z)
        self.x = (self.dx, z)
        self.y = (self.dy, z)
        self.quads = (d, self.dx, self.dy, self.dxy)
        self.core_quads = tuple(q + 1 - 2 * core for q in self.quads)

    def peer(self, step):
        return lax.rem(self.z + step, 4)

    def greet(self):
        barrier = pltpu.get_barrier_semaphore()
        others = [self.core, self.x, self.y] + [(self.d, self.peer(s)) for s in (1, 2, 3)]
        for other in others:
            pl.semaphore_signal(barrier, inc=1, device_id=other, device_id_type=MESH)
        pl.semaphore_wait(barrier, len(others))

    def hop(self, step, visit):
        for sign in (1, -1):
            m = self.z + sign * step

            @pl.when((m >= 0) & (m <= 3))
            def _():
                visit(m)


class Gather:
    def __init__(self, place, at, own, sems):
        self.p, self.at, self.own = place, at, own
        self.right, self.left, self.sx, self.sy, self.sc, self.arrived = sems

    def send(self, src, m, d, sem, device):
        remote(src, self.at(m, d), sem, self.arrived.at[m, d], device).start()

    def along_z(self, m, src=None):
        p = self.p
        src = self.at(m, p.d) if src is None else src

        @pl.when((m <= p.z) & (p.z < 3))
        def _():
            self.send(src, m, p.d, self.right.at[m], (p.d, p.z + 1))

        @pl.when((m >= p.z) & (p.z > 0))
        def _():
            self.send(src, m, p.d, self.left.at[m], (p.d, p.z - 1))

    def spread(self, m, src=None):
        p = self.p
        src = self.at(m, p.d) if src is None else src
        self.send(src, m, p.d, self.sx.at[m], p.x)
        self.send(src, m, p.d, self.sy.at[m], p.y)
        self.send(src, m, p.d, self.sc.at[m], p.core)

    def take(self, m, d):
        remote(self.at(m, d), self.at(m, d), self.sc.at[0], self.arrived.at[m, d], self.p.core).wait_recv()

    def z_in(self, m):
        self.take(m, self.p.d)
        self.along_z(m)

    def x_in(self, m):
        p = self.p
        self.take(m, p.dx)
        src = self.at(m, p.dx)

        @pl.when(lax.rem(m, 2) == 0)
        def _():
            self.send(src, m, p.dx, self.sy.at[4 + m], p.y)

        self.send(src, m, p.dx, self.sc.at[4 + m], p.core)

    def y_in(self, m):
        p = self.p
        self.take(m, p.dy)
        src = self.at(m, p.dy)

        @pl.when(lax.rem(m, 2) == 1)
        def _():
            self.send(src, m, p.dy, self.sx.at[4 + m], p.x)

        self.send(src, m, p.dy, self.sc.at[8 + m], p.core)

    def diag_in(self, m):
        p = self.p
        self.take(m, p.dxy)
        self.send(self.at(m, p.dxy), m, p.dxy, self.sc.at[12 + m], p.core)

    def core_in(self, m):
        for d in self.p.core_quads:
            self.take(m, d)

    def finish(self):
        p = self.p

        def sent(sem, device):
            remote(self.own, self.own, sem, self.arrived.at[0, 0], device).wait_send()

        for m in range(4):

            @pl.when((m <= p.z) & (p.z < 3))
            def _():
                sent(self.right.at[m], p.core)

            @pl.when((m >= p.z) & (p.z > 0))
            def _():
                sent(self.left.at[m], p.core)

            sent(self.sx.at[m], p.core)
            sent(self.sy.at[m], p.core)
            sent((self.sx if m % 2 else self.sy).at[4 + m], p.core)
            for q in range(4):
                sent(self.sc.at[4 * q + m], p.core)


def gather_sems():
    dma = pltpu.SemaphoreType.DMA
    return [dma((4,)), dma((4,)), dma((8,)), dma((8,)), dma((16,)), dma((4, 8))]


def lanes(shape, width):
    return lax.div(lax.broadcasted_iota(jnp.int32, shape, 1), width)


def turned(x, cosine, sine):
    first = lax.rem(lanes(x.shape, 32), 2) == 0
    width = x.shape[1]
    other = jnp.where(first, pltpu.roll(x, width - 32, 1), pltpu.roll(x, 32, 1))
    return x * cosine + other * sine


def wide(table):
    return jnp.concatenate([table, table], axis=1)


def dot(a, b):
    return lax.dot_general(a, b, (((1,), (0,)), ((), ())), preferred_element_type=F32)


def dot_nt(a, b):
    return lax.dot_general(a, b, (((1,), (1,)), ((), ())), preferred_element_type=F32)


def dot_tn(a, b):
    return lax.dot_general(a, b, (((0,), (0,)), ((), ())), preferred_element_type=F32)


def tile_scores(q_head, keys, tile, packed):
    n = (tile + 1) * CHUNK
    s = dot_nt(q_head, keys) * 0.125
    rows = lax.broadcasted_iota(jnp.int32, (CHUNK, n), 0) + tile * CHUNK
    cols = lax.broadcasted_iota(jnp.int32, (CHUNK, n), 1)
    allowed = cols <= rows
    if tile >= 2:
        allowed = allowed & ((packed != 2) | (cols >= 2 * CHUNK))
    return jnp.where(allowed, s, -1e30)


ORDER = (3, 0, 1, 2)


def add_rows(dst, terms, step):
    def rows(r, carry):
        at = pl.ds(pl.multiple_of(r * step, step), step)
        total = terms[0][at, :].astype(F32)
        for term in terms[1:]:
            total = total + term[at, :].astype(F32)
        dst[at, :] = total.astype(dst.dtype)
        return carry

    lax.fori_loop(0, dst.shape[0] // step, rows, 0)


def spans(n, step):
    return [(at, min(step, n - at)) for at in range(0, n, step)]


def block(i):
    return pl.ds(pl.multiple_of(i * CHUNK, CHUNK), CHUNK)


class Moves:
    def __init__(self, sems):
        self.sems, self.made = sems, []

    def start(self, src, dst):
        copy = pltpu.make_async_copy(src, dst, self.sems.at[len(self.made)])
        copy.start()
        self.made.append(copy)
        return len(self.made) - 1

    def wait(self, i):
        self.made[i].wait()
        self.made[i] = self.made[i], True

    def rest(self):
        for copy in self.made:
            if not isinstance(copy, tuple):
                copy.wait()


class Crossing:
    def __init__(self, place, part, bufs, sems, out, step):
        self.p, self.part, self.out, self.step = place, part, out, step
        self.acc, self.corner, self.bx, self.by = bufs
        (self.s_core, self.r_core, self.s_corner, self.r_corner,
         self.s_x, self.r_x, self.s_y, self.r_y) = sems

    def core_copy(self, m, q):
        p = self.p
        return remote(
            self.part(m, p.core_quads[q]), self.acc.at[m, q],
            self.s_core.at[m, q], self.r_core.at[m, q], p.core,
        )

    def begin(self, m):
        for q in (3, 1, 2, 0):
            self.core_copy(m, q).start()

    def corner_copy(self, m):
        to = self.p.x if m % 2 == 0 else self.p.y
        return remote(self.acc.at[m, 3], self.corner.at[m], self.s_corner.at[m], self.r_corner.at[m], to)

    def x_copy(self, m):
        return remote(self.acc.at[m, 1], self.bx.at[m], self.s_x.at[m], self.r_x.at[m], self.p.x)

    def y_copy(self, m):
        return remote(self.acc.at[m, 2], self.by.at[m], self.s_y.at[m], self.r_y.at[m], self.p.y)

    def join(self, m):
        first = 1 if m % 2 == 0 else 2
        for q in (3, first, 3 - first, 0):
            self.core_copy(m, q).wait_recv()
            add_rows(self.acc.at[m, q], [self.acc.at[m, q], self.part(m, self.p.quads[q])], self.step)
            if q == 3:
                self.corner_copy(m).start()
            if q == first:
                (self.x_copy if m % 2 == 0 else self.y_copy)(m).start()

    def relay(self, m):
        q = 2 if m % 2 == 0 else 1
        self.corner_copy(m).wait_recv()
        add_rows(self.acc.at[m, q], [self.acc.at[m, q], self.corner.at[m]], self.step)
        (self.y_copy if m % 2 == 0 else self.x_copy)(m).start()

    def total(self, m):
        self.x_copy(m).wait_recv()
        self.y_copy(m).wait_recv()
        add_rows(self.out.at[m], [self.acc.at[m, 0], self.bx.at[m], self.by.at[m]], self.step)

    def core_sent(self, m):
        for q in range(4):
            self.core_copy(m, q).wait_send()

    def finish(self):
        for m in range(4):
            self.corner_copy(m).wait_send()
            self.x_copy(m).wait_send()
            self.y_copy(m).wait_send()


def crossing_scratch(rows, width):
    def buf(*lead):
        return pltpu.VMEM((*lead, rows, width), BF)

    dma = pltpu.SemaphoreType.DMA
    return [buf(4, 4), buf(4), buf(4), buf(4), dma((4, 4)), dma((4, 4))] + [dma((4,))] * 6


class Chain:
    def __init__(self, place, part, bufs, sems, out, step):
        self.p, self.part, self.out, self.step = place, part, out, step
        self.br, self.bl = bufs
        self.s_r, self.r_r, self.s_l, self.r_l = sems

    def r_copy(self, m):
        p = self.p
        return remote(self.part.at[m], self.br.at[m], self.s_r.at[m], self.r_r.at[m], (p.d, p.z + 1))

    def l_copy(self, m):
        p = self.p
        return remote(self.part.at[m], self.bl.at[m], self.s_l.at[m], self.r_l.at[m], (p.d, p.z - 1))

    def level(self, k):
        @pl.when(self.p.z == k)
        def _():
            for m in range(3, k, -1):
                if k > 0:
                    self.r_copy(m).wait_recv()
                    add_rows(self.part.at[m], [self.part.at[m], self.br.at[m]], self.step)
                self.r_copy(m).start()

        @pl.when(self.p.z == 3 - k)
        def _():
            for m in range(0, 3 - k):
                if k > 0:
                    self.l_copy(m).wait_recv()
                    add_rows(self.part.at[m], [self.part.at[m], self.bl.at[m]], self.step)
                self.l_copy(m).start()

    def last(self):
        for m in range(4):

            @pl.when(self.p.z == m)
            def _():
                terms = [self.part.at[m]]
                if m > 0:
                    self.r_copy(m).wait_recv()
                    terms.append(self.br.at[m])
                if m < 3:
                    self.l_copy(m).wait_recv()
                    terms.append(self.bl.at[m])
                add_rows(self.out, terms, self.step)

    def finish(self):
        for m in range(4):
            if m > 0:

                @pl.when(self.p.z < m)
                def _():
                    self.r_copy(m).wait_send()

            if m < 3:

                @pl.when(self.p.z > m)
                def _():
                    self.l_copy(m).wait_send()


def chain_scratch(rows, width):
    dma = pltpu.SemaphoreType.DMA
    return [pltpu.VMEM((4, rows, width), BF)] * 2 + [dma((4,))] * 4


def forward_kernel(
    seq, wq, wk, wv, wo_own, wg_t, wu_t, wd_t, gain_attn, gain_mlp, cos_t, sin_t, tok_in, fv_in, cot_in,
    f2, acts, f1_out, qkv_out, o_out, lse_out, rows_out, a1t_out, a2_out, dattn_out, mid_out, layer_out, do_out, do_last, gain_part,
    tok, fv, cot, f1, qkv, o_head, lse, o_rows, a1_t, a1, stage, p2, w, wo, a2, mid, y_out, acc, back, act, dattn, do_rows, do_head, *sems,
):
    p = Place()
    sems = list(sems)
    g1s, g2s = sems[:6], sems[6:12]
    s_qkv, r_qkv, s_o, r_o, s_local, s_do, r_do, w_sems, wo_sems, act_sems, move_sems = sems[12:]
    moves = Moves(move_sems)
    z, d = p.z, p.d
    got_tok = moves.start(tok_in, tok)
    got_fv = moves.start(fv_in, fv)
    got_cot = moves.start(cot_in, cot)
    p.greet()

    f1[z, d, 0:128] = wq[...]
    f1[z, d, 128:256] = wk[...]
    f1[z, d, 256:384] = wv[...]
    f1[z, d, 384:400, 0:128] = jnp.broadcast_to(gain_attn[...], (16, 128))
    f1[z, d, 384:400, 128:256] = jnp.broadcast_to(gain_mlp[...], (16, 128))
    g1 = Gather(p, lambda m, e: f1.at[m, e], f1.at[0, 0], g1s)
    g2 = Gather(p, lambda m, e: f2.at[m, e], p2, g2s)
    g1.along_z(z)
    g1.spread(z)
    for i, source in enumerate((wg_t, wu_t, wd_t)):
        p2[i * FFC : (i + 1) * FFC, :] = source[...]
    p2[3 * FFC :, :] = wo_own[...].T
    own_copy = pltpu.make_async_copy(p2, f2.at[z, d], s_local)
    own_copy.start()

    def arrive(g):
        def visit(m):
            g.z_in(m)
            g.spread(m)
        return visit

    def side(g):
        def visit(m):
            g.x_in(m)
            g.y_in(m)
        return visit

    p.hop(1, arrive(g1))
    side(g1)(z)
    p.hop(2, arrive(g1))
    p.hop(1, side(g1))
    g1.diag_in(z)
    p.hop(3, arrive(g1))
    g2.along_z(z, p2)
    p.hop(2, side(g1))
    p.hop(1, g1.diag_in)
    g1.core_in(z)

    gain_row = jnp.concatenate([f1[z, e, 384:400, :].astype(F32)[0:8] for e in range(8)], axis=1)
    gain_two = jnp.concatenate([gain_row[0:1, e * 256 + 128 : e * 256 + 256] for e in range(8)], axis=1)
    moves.wait(got_tok)

    def norm_body(b, carry):
        x = tok[b].astype(F32)
        factor = lax.rsqrt(jnp.mean(x * x, axis=1, keepdims=True) + EPSILON)
        for e in range(8):
            cols = slice(e * 128, (e + 1) * 128)
            a1[pl.ds(pl.multiple_of(b * CHUNK, CHUNK), CHUNK), cols] = (
                x[:, cols] * factor * gain_row[0:1, e * 256 : e * 256 + 128]
            ).astype(BF)
        return carry

    lax.fori_loop(0, 3, norm_body, 0)

    p.hop(3, side(g1))
    p.hop(2, g1.diag_in)
    p.hop(1, g1.core_in)
    p.hop(3, g1.diag_in)
    p.hop(2, g1.core_in)
    p.hop(3, g1.core_in)
    g2.spread(z, p2)
    moves.start(f1, f1_out)
    moves.wait(got_fv)

    def project(b):
        pos_full = pl.ds(pl.multiple_of(z * CHUNK, CHUNK), CHUNK)
        low = jnp.where(z >= 2, z - 2, z)
        pos_half = pl.ds(pl.multiple_of(low * CHUNK, CHUNK), CHUNK)
        second = seq[b] == 2
        cosine = wide(jnp.where(second, cos_t[pos_half, :], cos_t[pos_full, :]))
        sine = wide(jnp.where(second, sin_t[pos_half, :], sin_t[pos_full, :]))
        rows = a1[b * CHUNK : (b + 1) * CHUNK, :]

        def one(step, carry):
            m = lax.rem(z + step, 4)
            w = lambda i: f1[m, :, i * 128 : (i + 1) * 128, :].reshape(1024, CHUNK)
            stage[b, m, 0] = turned(dot(rows, w(0)), cosine, sine).astype(BF)
            stage[b, m, 1] = turned(dot(rows, w(1)), cosine, sine).astype(BF)
            first = fv[b, :, pl.ds(pl.multiple_of(m * CHUNK, CHUNK), CHUNK)].astype(F32)
            stage[b, m, 2] = (0.5 * (dot(rows, w(2)) + first)).astype(BF)
            return carry

        lax.fori_loop(0, 4, one, 0)
        for i in range(3):
            qkv[b, i, block(z), :] = stage[b, z, i]

    def qkv_copy(b, step):
        m = p.peer(step)
        dst = qkv.at[b, :, pl.ds(pl.multiple_of(z * CHUNK, CHUNK), CHUNK), :]
        return remote(stage.at[b, m], dst, s_qkv.at[b, step - 1], r_qkv.at[b, z], (d, m))

    def send_qkv(b):
        for step in (1, 2, 3):
            qkv_copy(b, step).start()

    def sent_qkv(b):
        for step in (1, 2, 3):
            qkv_copy(b, step).wait_send()

    def take_qkv(b):
        for step in (1, 2, 3):
            m = p.peer(step)
            dst = qkv.at[b, :, pl.ds(pl.multiple_of(m * CHUNK, CHUNK), CHUNK), :]
            remote(stage.at[b, m], dst, s_qkv.at[b, 0], r_qkv.at[b, m], (d, m)).wait_recv()

    def o_copy(b, i):
        rows = slice(i * CHUNK, (i + 1) * CHUNK)
        return remote(o_head.at[b, rows, :], o_rows.at[b, z], s_o.at[b, i], r_o.at[b, z], (d, i))

    def attend(b, i):
        n = (i + 1) * CHUNK
        rows = slice(i * CHUNK, n)
        packed = seq[b]
        q = qkv[b, 0, rows, :]
        keys = qkv[b, 1, 0:n, :]
        values = qkv[b, 2, 0:n, :]
        head_of = lanes((CHUNK, CHUNK), 64)
        lane = lax.broadcasted_iota(jnp.int32, (CHUNK, 128), 1)

        def head(h, carry):
            out, stats = carry
            s = tile_scores(jnp.where(head_of == h, q, jnp.zeros_like(q)), keys, i, packed)
            top = jnp.max(s, axis=1, keepdims=True)
            e = jnp.exp(s - top)
            total = jnp.sum(e, axis=1, keepdims=True)
            part = dot(e.astype(BF), values) * (1.0 / total)
            return (
                jnp.where(head_of == h, part, out),
                jnp.where(lane == h, top + jnp.log(total), stats),
            )

        out, stats = lax.fori_loop(
            0, 4, head, (jnp.zeros((CHUNK, CHUNK), F32), jnp.zeros((CHUNK, 128), F32))
        )
        o_head[b, rows, :] = out.astype(BF)
        lse[b, rows, :] = stats

        @pl.when(z == i)
        def _():
            o_rows[b, z] = out.astype(BF)

        @pl.when(z != i)
        def _():
            o_copy(b, i).start()

    def take_o(b):
        for step in (1, 2, 3):
            m = p.peer(step)
            remote(o_rows.at[b, m], o_rows.at[b, m], s_o.at[b, 0], r_o.at[b, m], (d, m)).wait_recv()

    def w_copy(t, e):
        m, slot = lax.rem(t, 4), lax.rem(t, 2)
        return pltpu.make_async_copy(
            f2.at[m, e, 0 : 3 * FFC, :], w.at[slot, :, e * 128 : (e + 1) * 128], w_sems.at[slot, e]
        )

    def wo_copy(m, e):
        return pltpu.make_async_copy(
            f2.at[m, e, 3 * FFC :, :], wo.at[m, :, e * 128 : (e + 1) * 128], wo_sems.at[m, e]
        )

    def act_copy(b, m, slot):
        return pltpu.make_async_copy(
            act.at[slot], acts.at[:, m, b * CHUNK : (b + 1) * CHUNK, :], act_sems.at[slot]
        )

    def load_mlp():
        for m in range(4):
            for e in range(8):
                wo_copy(m, e).start()
        for e in range(8):
            w_copy(0, e).start()
        for m in range(4):
            for e in range(8):
                wo_copy(m, e).wait()

    def do_copy(b, step):
        m = p.peer(step)
        return remote(
            do_rows.at[b, m], do_head.at[b, block(z), :], s_do.at[b, step - 1], r_do.at[b, z], (d, m)
        )

    def mlp_rows(b):
        rows = slice(b * CHUNK, (b + 1) * CHUNK)
        x2 = tok[b].astype(F32)
        for m in range(4):
            x2 = x2 + dot(o_rows[b, m], wo[m])
        factor = lax.rsqrt(jnp.mean(x2 * x2, axis=1, keepdims=True) + EPSILON)
        mid[b] = x2
        a2[rows, :] = (x2 * factor * gain_two).astype(BF)

        def chunk(m, carry):
            t = b * 4 + m
            slot = lax.rem(m, 2)
            for e in range(8):
                w_copy(t, e).wait()

            @pl.when(t < 11)
            def _():
                for e in range(8):
                    w_copy(t + 1, e).start()

            @pl.when(t >= 2)
            def _():
                act_copy(b, m, slot).wait()

            for at, size in spans(FFC, 256):
                cols = slice(at, at + size)
                gate = dot_nt(a2[rows, :], w[slot, at : at + size, :])
                up = dot_nt(a2[rows, :], w[slot, FFC + at : FFC + at + size, :])
                dh = dot_nt(cot[b], w[slot, 2 * FFC + at : 2 * FFC + at + size, :])
                sg = jax.nn.sigmoid(gate)
                silu = gate * sg
                act[slot, 0, :, cols] = (dh * up * (sg + silu * (1.0 - sg))).astype(BF)
                act[slot, 1, :, cols] = (dh * silu).astype(BF)
                act[slot, 2, :, cols] = (silu * up).astype(BF)
            for at, size in spans(1024, 256):
                cols = slice(at, at + size)
                y = dot(act[slot, 2], w[slot, 2 * FFC : 3 * FFC, cols])
                u = dot(act[slot, 0], w[slot, 0:FFC, cols]) + dot(act[slot, 1], w[slot, FFC : 2 * FFC, cols])
                acc[:, cols] = jnp.where(m == 0, y, acc[:, cols] + y)
                back[:, cols] = jnp.where(m == 0, u, back[:, cols] + u)
            act_copy(b, m, slot).start()
            return carry

        lax.fori_loop(0, 4, chunk, 0)
        x2 = mid[b]
        y_out[b] = (x2 + acc[...]).astype(BF)
        factor = lax.rsqrt(jnp.mean(x2 * x2, axis=1, keepdims=True) + EPSILON)
        n2 = x2 * factor
        da2 = back[...]
        sums = jnp.broadcast_to(jnp.sum(da2 * n2, axis=0, keepdims=True), (8, 1024))
        gain_part[...] = sums if b == 0 else gain_part[...] + sums
        dn2 = da2 * gain_two
        grad_mid = cot[b].astype(F32) + factor * (dn2 - n2 * jnp.mean(dn2 * n2, axis=1, keepdims=True))
        mid[b] = grad_mid
        dattn[rows, :] = grad_mid.astype(BF)

        def heads(m, carry):
            do_rows[b, m] = dot_nt(dattn[rows, :], wo[m]).astype(BF)
            return carry

        lax.fori_loop(0, 4, heads, 0)
        if b < 2:
            for step in (1, 2, 3):
                do_copy(b, step).start()
            do_head[b, block(z), :] = do_rows[b, z]
        moves.start(mid.at[b], mid_out.at[b])
        moves.start(y_out.at[b], layer_out.at[b])

    def attend_all(b):
        for i in range(4):
            attend(b, i)
        moves.start(o_head.at[b], o_out.at[b])
        moves.start(lse.at[b], lse_out.at[b])

    for b in range(3):
        project(b)
        if b == 0:
            send_qkv(0)
    a1_t[...] = a1[...].T
    moves.start(a1_t, a1t_out)
    p.hop(1, arrive(g2))
    p.hop(2, arrive(g2))
    side(g2)(z)
    sent_qkv(0)
    send_qkv(1)
    p.hop(3, arrive(g2))
    p.hop(1, side(g2))
    g2.diag_in(z)
    take_qkv(0)
    moves.start(qkv.at[0], qkv_out.at[0])
    attend_all(0)
    p.hop(2, side(g2))
    p.hop(1, g2.diag_in)
    sent_qkv(1)
    send_qkv(2)
    take_qkv(1)
    moves.start(qkv.at[1], qkv_out.at[1])
    attend_all(1)
    p.hop(3, side(g2))
    p.hop(2, g2.diag_in)
    p.hop(3, g2.diag_in)
    for m in range(4):
        g2.core_in(m)
    own_copy.wait()
    load_mlp()
    moves.wait(got_cot)
    take_o(0)
    mlp_rows(0)
    take_qkv(2)
    moves.start(qkv.at[2], qkv_out.at[2])
    attend_all(2)
    take_o(1)
    mlp_rows(1)
    take_o(2)
    moves.start(o_rows, rows_out)
    mlp_rows(2)
    moves.start(a2, a2_out)
    moves.start(dattn, dattn_out)
    moves.start(do_rows.at[2], do_last)
    for b in range(2):
        for step in (1, 2, 3):
            m = p.peer(step)
            dst = do_head.at[b, block(m), :]
            remote(do_rows.at[b, m], dst, s_do.at[b, 0], r_do.at[b, m], (d, m)).wait_recv()
            do_copy(b, step).wait_send()
        moves.start(do_head.at[b], do_out.at[b])
    act_copy(2, 2, 0).wait()
    act_copy(2, 3, 1).wait()
    sent_qkv(2)
    for b in range(3):
        for i in range(4):

            @pl.when(z != i)
            def _():
                o_copy(b, i).wait_send()

    g1.finish()
    g2.finish()
    moves.rest()


def run_forward(*args):
    vmem = pl.BlockSpec(memory_space=pltpu.VMEM)
    hbm = pl.BlockSpec(memory_space=pl.ANY)
    dma = pltpu.SemaphoreType.DMA
    shape = jax.ShapeDtypeStruct
    return pl.pallas_call(
        forward_kernel,
        out_shape=(
            shape((4, 8, PIECE, 128), BF),
            shape((3, 4, 768, FFC), BF),
            shape((4, 8, QROWS, CHUNK), BF),
            shape((3, 3, 1024, CHUNK), BF),
            shape((3, 1024, CHUNK), BF),
            shape((3, 1024, 128), F32),
            shape((3, 4, CHUNK, CHUNK), BF),
            shape((1024, 768), BF),
            shape((768, 1024), BF),
            shape((768, 1024), BF),
            shape((3, CHUNK, 1024), F32),
            shape((3, CHUNK, 1024), BF),
            shape((2, 1024, CHUNK), BF),
            shape((4, CHUNK, CHUNK), BF),
            shape((8, 1024), F32),
        ),
        in_specs=[pl.BlockSpec(memory_space=pltpu.SMEM)] + [vmem] * 11 + [hbm] * 3,
        out_specs=(hbm,) * 14 + (vmem,),
        scratch_shapes=[
            pltpu.VMEM((3, CHUNK, 1024), BF),
            pltpu.VMEM((3, CHUNK, 1024), BF),
            pltpu.VMEM((3, CHUNK, 1024), BF),
            pltpu.VMEM((4, 8, QROWS, CHUNK), BF),
            pltpu.VMEM((3, 3, 1024, CHUNK), BF),
            pltpu.VMEM((3, 1024, CHUNK), BF),
            pltpu.VMEM((3, 1024, 128), F32),
            pltpu.VMEM((3, 4, CHUNK, CHUNK), BF),
            pltpu.VMEM((1024, 768), BF),
            pltpu.VMEM((768, 1024), BF),
            pltpu.VMEM((3, 4, 3, CHUNK, CHUNK), BF),
            pltpu.VMEM((PIECE, 128), BF),
            pltpu.VMEM((2, 3 * FFC, 1024), BF),
            pltpu.VMEM((4, CHUNK, 1024), BF),
            pltpu.VMEM((768, 1024), BF),
            pltpu.VMEM((3, CHUNK, 1024), F32),
            pltpu.VMEM((3, CHUNK, 1024), BF),
            pltpu.VMEM((CHUNK, 1024), F32),
            pltpu.VMEM((CHUNK, 1024), F32),
            pltpu.VMEM((2, 3, CHUNK, FFC), BF),
            pltpu.VMEM((768, 1024), BF),
            pltpu.VMEM((3, 4, CHUNK, CHUNK), BF),
            pltpu.VMEM((2, 1024, CHUNK), BF),
        ]
        + gather_sems()
        + gather_sems()
        + [dma((3, 3)), dma((3, 4)), dma((3, 4)), dma((3, 4)), dma, dma((3, 3)), dma((3, 4))]
        + [dma((2, 8)), dma((4, 8)), dma((2,)), dma((32,))],
        compiler_params=pltpu.CompilerParams(
            collective_id=1, has_side_effects=True, vmem_limit_bytes=62 * 2**20
        ),
        cost_estimate=pl.CostEstimate(flops=5 * 10**10, bytes_accessed=6 * 10**7, transcendentals=8 * 10**6),
        name="gather_forward",
    )(*args)


def backward_kernel(
    seq, cos_t, sin_t, do_last, do_in, qkv_in, o_in, lse_in, rows_in, a2_in, dattn_in, cot_in, acts,
    d_rows, summed,
    do_mine, do_head, qkv, o_head, lse, o_rows, a2, dattn, cot, act, part, total, dk, dv, stage, *rest,
):
    p = Place()
    s_do, r_do, s_d, r_d, act_sems, move_sems = rest[:6]
    z, d = p.z, p.d
    moves = Moves(move_sems)
    got = []
    for b in range(3):
        got.append(
            [moves.start(qkv_in.at[b], qkv.at[b]), moves.start(o_in.at[b], o_head.at[b]), moves.start(lse_in.at[b], lse.at[b])]
            + ([moves.start(do_in.at[b], do_head.at[b])] if b < 2 else [])
        )
        if b == 0:
            got_do = moves.start(do_last, do_mine)
            got_w = [
                moves.start(a2_in, a2), moves.start(dattn_in, dattn), moves.start(cot_in, cot),
                moves.start(rows_in, o_rows),
            ]
    p.greet()

    def act_copy(m, slot):
        return pltpu.make_async_copy(acts.at[:, m], act.at[slot], act_sems.at[slot])

    act_copy(ORDER[0], 0).start()
    moves.wait(got_do)

    def do_copy(step):
        m = p.peer(step)
        return remote(do_mine.at[m], do_head.at[2, block(z), :], s_do.at[step - 1], r_do.at[z], (d, m))

    for step in (1, 2, 3):
        do_copy(step).start()
    do_head[2, block(z), :] = do_mine[z]

    def take_do():
        for step in (1, 2, 3):
            m = p.peer(step)
            dst = do_head.at[2, block(m), :]
            remote(do_mine.at[m], dst, s_do.at[0], r_do.at[m], (d, m)).wait_recv()

    def d_copy(b, i):
        return remote(stage.at[b, i], d_rows.at[b, z], s_d.at[b, i], r_d.at[b, z], (d, i))

    def own_copy(b, i):
        return pltpu.make_async_copy(stage.at[b, i], d_rows.at[b, i], s_d.at[b, i])

    def back(b, i):
        n = (i + 1) * CHUNK
        rows = slice(i * CHUNK, n)
        packed = seq[b]
        head_of = lanes((CHUNK, CHUNK), 64)
        lane = lax.broadcasted_iota(jnp.int32, (CHUNK, 128), 1)
        q = qkv[b, 0, rows, :]
        keys = qkv[b, 1, 0:n, :]
        values = qkv[b, 2, 0:n, :]
        grad = do_head[b, rows, :]
        spread = grad.astype(F32) * o_head[b, rows, :].astype(F32)
        stats = lse[b, rows, :]

        def head(h, dq):
            here = head_of == h
            q_h = jnp.where(here, q, jnp.zeros_like(q))
            g_h = jnp.where(here, grad, jnp.zeros_like(grad))
            delta = jnp.sum(jnp.where(here, spread, 0.0), axis=1, keepdims=True)
            level = jnp.sum(jnp.where(lane == h, stats, 0.0), axis=1, keepdims=True)
            prob = jnp.exp(tile_scores(q_h, keys, i, packed) - level)
            dp = dot_nt(g_h, values)
            ds = (prob * (dp - delta)).astype(BF)
            dv_part = dot_tn(prob.astype(BF), g_h)
            dk_part = dot_tn(ds, q_h)
            dv[0:n, :] += dv_part
            dk[0:n, :] += dk_part
            return jnp.where(here, dot(ds, keys), dq)

        dq = lax.fori_loop(0, 4, head, jnp.zeros((CHUNK, CHUNK), F32))
        cosine, sine = cos_t[rows, :], sin_t[rows, :]
        if i >= 2:
            early = slice((i - 2) * CHUNK, (i - 1) * CHUNK)
            cosine = jnp.where(packed == 2, cos_t[early, :], cosine)
            sine = jnp.where(packed == 2, sin_t[early, :], sine)
        cosine, sine = wide(cosine), -wide(sine)
        stage[b, i, :, 0:256] = turned(dq * 0.125, cosine, sine).astype(BF)
        stage[b, i, :, 256:512] = turned(dk[rows, :] * 0.125, cosine, sine).astype(BF)
        stage[b, i, :, 512:768] = (dv[rows, :] * 0.5).astype(BF)

        @pl.when(z == i)
        def _():
            own_copy(b, i).start()

        @pl.when(z != i)
        def _():
            d_copy(b, i).start()

    def back_all(b):
        for i in got[b]:
            moves.wait(i)
        dk[...] = jnp.zeros_like(dk)
        dv[...] = jnp.zeros_like(dv)
        for i in (3, 2, 1, 0):
            back(b, i)

    crossing = Crossing(p, lambda m, e: part.at[ORDER.index(m) % 2, e], rest[6:10], rest[10:], total, 592)

    def weight_grad(k):
        m, slot = ORDER[k], k % 2
        act_copy(m, slot).wait()
        if k < 3:
            act_copy(ORDER[k + 1], 1 - slot).start()
        if k >= 2:
            crossing.core_sent(ORDER[k - 2])

        for i in range(3):
            right = cot[...].reshape(768, 1024) if i == 2 else a2[...]
            for at, size in spans(FFC, 256):
                out = dot_tn(act[slot, i, :, at : at + size], right).astype(BF)
                for e in range(8):
                    part[slot, e, i * FFC + at : i * FFC + at + size, :] = out[:, e * 128 : (e + 1) * 128]
        own = jnp.concatenate([o_rows[b, m] for b in range(3)], axis=0)
        out = dot_tn(own, dattn[...]).astype(BF)
        for e in range(8):
            part[slot, e, 3 * FFC :, :] = out[:, e * 128 : (e + 1) * 128]
        crossing.begin(m)

    a, b_, c, e_ = ORDER
    back_all(0)
    for i in got_w:
        moves.wait(i)
    weight_grad(0)
    weight_grad(1)
    crossing.join(a)
    crossing.join(b_)
    back_all(1)
    weight_grad(2)
    weight_grad(3)
    crossing.relay(a)
    crossing.relay(b_)
    take_do()
    back_all(2)
    crossing.join(c)
    crossing.join(e_)
    crossing.total(a)
    crossing.total(b_)
    crossing.relay(c)
    crossing.relay(e_)
    crossing.total(c)
    crossing.total(e_)
    moves.start(total, summed)
    crossing.core_sent(c)
    crossing.core_sent(e_)
    crossing.finish()
    for step in (1, 2, 3):
        do_copy(step).wait_send()
    for b in range(3):
        for step in (1, 2, 3):
            m = p.peer(step)
            remote(stage.at[b, m], d_rows.at[b, m], s_d.at[b, 0], r_d.at[b, m], (d, m)).wait_recv()
        for i in range(4):

            @pl.when(z == i)
            def _():
                own_copy(b, i).wait()

            @pl.when(z != i)
            def _():
                d_copy(b, i).wait_send()

    moves.rest()


def run_backward(*args):
    vmem = pl.BlockSpec(memory_space=pltpu.VMEM)
    hbm = pl.BlockSpec(memory_space=pl.ANY)
    dma = pltpu.SemaphoreType.DMA
    shape = jax.ShapeDtypeStruct
    return pl.pallas_call(
        backward_kernel,
        out_shape=(shape((3, 4, CHUNK, 768), BF), shape((4, PIECE, 128), BF)),
        in_specs=[pl.BlockSpec(memory_space=pltpu.SMEM)] + [vmem] * 2 + [hbm] * (len(args) - 3),
        out_specs=(hbm, hbm),
        scratch_shapes=[
            pltpu.VMEM((4, CHUNK, CHUNK), BF),
            pltpu.VMEM((3, 1024, CHUNK), BF),
            pltpu.VMEM((3, 3, 1024, CHUNK), BF),
            pltpu.VMEM((3, 1024, CHUNK), BF),
            pltpu.VMEM((3, 1024, 128), F32),
            pltpu.VMEM((3, 4, CHUNK, CHUNK), BF),
            pltpu.VMEM((768, 1024), BF),
            pltpu.VMEM((768, 1024), BF),
            pltpu.VMEM((3, CHUNK, 1024), BF),
            pltpu.VMEM((2, 3, 768, FFC), BF),
            pltpu.VMEM((2, 8, PIECE, 128), BF),
            pltpu.VMEM((4, PIECE, 128), BF),
            pltpu.VMEM((1024, CHUNK), F32),
            pltpu.VMEM((1024, CHUNK), F32),
            pltpu.VMEM((3, 4, CHUNK, 768), BF),
            dma((3,)),
            dma((4,)),
            dma((3, 4)),
            dma((3, 4)),
            dma((2,)),
            dma((32,)),
        ]
        + crossing_scratch(PIECE, 128),
        compiler_params=pltpu.CompilerParams(
            collective_id=2, has_side_effects=True, vmem_limit_bytes=63 * 2**20
        ),
        cost_estimate=pl.CostEstimate(flops=4 * 10**10, bytes_accessed=4 * 10**7, transcendentals=8 * 10**6),
        name="attend_back",
    )(*args)


def finish_kernel(
    gain_part, tok_in, mid_in, d_rows_in, a1t_in, f1_in, summed,
    grad_tokens, grad_first, dw1, dw2, gain_sum,
    tok, mid, d_rows, a1_t, f1, grad, first, part, acc, total1, total2, gbuf, *rest,
):
    p = Place()
    rest = list(rest)
    cross = Crossing(p, lambda m, e: part.at[m, e], rest[:4], rest[4:12], total1, 16)
    chain1 = Chain(p, total1, rest[12:14], rest[14:18], dw1, 16)
    chain2 = Chain(p, total2, rest[18:20], rest[20:24], dw2, 592)
    s_gain, r_gain, move_sems = rest[24:27]
    moves = Moves(move_sems)
    got_total = moves.start(summed, total2)
    got_d = [moves.start(d_rows_in, d_rows), moves.start(a1t_in, a1_t)]
    got_f1 = moves.start(f1_in, f1)
    got_x = [moves.start(tok_in, tok), moves.start(mid_in, mid)]
    p.greet()

    def weight_grad(m):
        cols = jnp.concatenate([d_rows[b, m] for b in range(3)], axis=0)

        def rows(k, carry):
            at = pl.ds(pl.multiple_of(k * CHUNK, CHUNK), CHUNK)
            part[m, pl.ds(2 * k, 2)] = dot(a1_t[at, :], cols).astype(BF).reshape(2, 128, 768)
            return carry

        lax.fori_loop(0, 4, rows, 0)

    def input_grad(m):
        cols = jnp.concatenate([d_rows[b, m] for b in range(3)], axis=0)

        def tile(k, carry):
            w = jnp.concatenate(
                [f1[m, pl.ds(2 * k, 2), i * 128 : (i + 1) * 128, :].reshape(CHUNK, CHUNK) for i in range(3)],
                axis=1,
            )
            at = pl.ds(pl.multiple_of(k * CHUNK, CHUNK), CHUNK)
            y = dot_nt(cols, w)
            if m == 0:
                acc[:, at] = y
            else:
                acc[:, at] += y
            return carry

        lax.fori_loop(0, 4, tile, 0)

    def leave(b, total):
        x = tok[b].astype(F32)
        factor = lax.rsqrt(jnp.mean(x * x, axis=1, keepdims=True) + EPSILON)
        n1 = x * factor
        da1 = acc[pl.ds(pl.multiple_of(b * CHUNK, CHUNK), CHUNK), :]
        total = total + jnp.sum(da1 * n1, axis=0, keepdims=True)
        gain = jnp.concatenate([f1[0, e, 384:400, 0:128].astype(F32)[0:1] for e in range(8)], axis=1)
        dn1 = da1 * gain
        grad[b] = mid[b] + factor * (dn1 - n1 * jnp.mean(dn1 * n1, axis=1, keepdims=True))
        for m in range(4):
            first[b, :, m * CHUNK : (m + 1) * CHUNK] = d_rows[b, m, :, 512:768].astype(F32)
        return total

    def gain_copy(i, device):
        return remote(gbuf.at[0] if i == 0 else gbuf.at[4 + i], gbuf.at[1 + i], s_gain.at[i], r_gain.at[i], device)

    a, b, c, e = ORDER
    moves.wait(got_total)
    chain2.level(0)
    for i in got_d:
        moves.wait(i)
    for m in ORDER:
        weight_grad(m)
        cross.begin(m)
    cross.join(a)
    cross.join(b)
    cross.join(c)
    cross.join(e)
    chain2.level(1)
    cross.relay(a)
    cross.relay(b)
    moves.wait(got_f1)
    input_grad(0)
    cross.relay(c)
    cross.relay(e)
    input_grad(1)
    cross.total(a)
    cross.total(b)
    input_grad(2)
    chain2.level(2)
    input_grad(3)
    cross.total(c)
    cross.total(e)
    chain1.level(0)
    for i in got_x:
        moves.wait(i)
    total = lax.fori_loop(0, 3, leave, jnp.zeros((1, 1024), F32))
    moves.start(grad, grad_tokens)
    moves.start(first, grad_first)
    row = lax.broadcasted_iota(jnp.int32, (8, 1024), 0)
    gbuf[0] = jnp.where(row == 0, total, gain_part[...])
    gain_copy(0, p.core).start()
    chain1.level(1)
    gain_copy(0, p.core).wait_recv()
    gbuf[5] = gbuf[0] + gbuf[1]
    gain_copy(1, p.x).start()
    chain2.last()
    gain_copy(1, p.x).wait_recv()
    gbuf[6] = gbuf[5] + gbuf[2]
    gain_copy(2, p.y).start()
    chain1.level(2)
    gain_copy(2, p.y).wait_recv()
    gbuf[7] = gbuf[6] + gbuf[3]
    for step in (1, 2, 3):
        m = p.peer(step)
        remote(gbuf.at[7], gbuf.at[8 + p.z], s_gain.at[2 + step], r_gain.at[3 + p.z], (p.d, m)).start()
    gbuf[8 + p.z] = gbuf[7]
    chain1.last()
    for step in (1, 2, 3):
        m = p.peer(step)
        remote(gbuf.at[7], gbuf.at[8 + m], s_gain.at[2 + step], r_gain.at[3 + m], (p.d, m)).wait_recv()
    gain_sum[...] = (gbuf[8] + gbuf[9]) + (gbuf[10] + gbuf[11])
    for i, device in enumerate((p.core, p.x, p.y)):
        gain_copy(i, device).wait_send()
    for step in (1, 2, 3):
        m = p.peer(step)
        remote(gbuf.at[7], gbuf.at[8 + m], s_gain.at[2 + step], r_gain.at[3 + m], (p.d, m)).wait_send()
    for m in range(4):
        cross.core_sent(m)
    cross.finish()
    chain1.finish()
    chain2.finish()
    moves.rest()


def run_finish(*args):
    vmem = pl.BlockSpec(memory_space=pltpu.VMEM)
    hbm = pl.BlockSpec(memory_space=pl.ANY)
    dma = pltpu.SemaphoreType.DMA
    shape = jax.ShapeDtypeStruct
    return pl.pallas_call(
        finish_kernel,
        out_shape=(
            shape((3, CHUNK, 1024), F32),
            shape((3, CHUNK, 1024), F32),
            shape((128, 768), F32),
            shape((PIECE, 128), F32),
            shape((8, 1024), F32),
        ),
        in_specs=[vmem] + [hbm] * (len(args) - 1),
        out_specs=(hbm, hbm, vmem, vmem, vmem),
        scratch_shapes=[
            pltpu.VMEM((3, CHUNK, 1024), BF),
            pltpu.VMEM((3, CHUNK, 1024), F32),
            pltpu.VMEM((3, 4, CHUNK, 768), BF),
            pltpu.VMEM((1024, 768), BF),
            pltpu.VMEM((4, 8, QROWS, CHUNK), BF),
            pltpu.VMEM((3, CHUNK, 1024), F32),
            pltpu.VMEM((3, CHUNK, 1024), F32),
            pltpu.VMEM((4, 8, 128, 768), BF),
            pltpu.VMEM((768, 1024), F32),
            pltpu.VMEM((4, 128, 768), BF),
            pltpu.VMEM((4, PIECE, 128), BF),
            pltpu.VMEM((12, 8, 1024), F32),
        ]
        + crossing_scratch(128, 768)
        + chain_scratch(128, 768)
        + chain_scratch(PIECE, 128)
        + [dma((6,)), dma((7,)), dma((8,))],
        compiler_params=pltpu.CompilerParams(
            collective_id=3, has_side_effects=True, vmem_limit_bytes=62 * 2**20
        ),
        cost_estimate=pl.CostEstimate(flops=10**10, bytes_accessed=5 * 10**7, transcendentals=0),
        name="sum_grads",
    )(*args)


def fast_body(
    tokens, first_values, sequences, w_query, w_key, w_value, w_out, w_gate, w_up, w_down,
    gain_attn, gain_mlp, cotangent,
):
    seq = sequences[:, 0]
    cos_t, sin_t = rope_tables()
    (_, acts, f1, qkv, o_head, lse, o_rows, a1_t, a2, dattn, mid, layer_out, do_head, do_last, gain_part) = run_forward(
        seq, w_query, w_key, w_value, w_out, w_gate.T, w_up.T, w_down.T,
        gain_attn[None, :], gain_mlp[None, :], cos_t, sin_t, tokens, first_values, cotangent,
    )
    d_rows, summed = run_backward(
        seq, cos_t, sin_t, do_last, do_head, qkv, o_head, lse, o_rows, a2, dattn, cotangent, acts
    )
    grad_tokens, grad_first, dw1, dw2, gain_sum = run_finish(gain_part, tokens, mid, d_rows, a1_t, f1, summed)
    place = (lax.axis_index("dp") * 4 + lax.axis_index("mp")) * 32
    gain_mine = lax.dynamic_slice(gain_sum, (0, place), (2, 32))
    return (
        layer_out,
        grad_tokens,
        grad_first,
        dw1[:, 0:256],
        dw1[:, 256:512],
        dw1[:, 512:768],
        dw2[3 * FFC :].T,
        dw2[0:FFC].T,
        dw2[FFC : 2 * FFC].T,
        dw2[2 * FFC : 3 * FFC].T,
        gain_mine[0],
        gain_mine[1],
    )


def is_small(mesh):
    return mesh.axis_names == ("dp", "mp") and tuple(mesh.devices.shape) == (8, 4)


def solution(mesh):
    return jax.shard_map(
        fast_body if is_small(mesh) else body,
        mesh=mesh,
        in_specs=(
            P(None, ("dp", "mp"), None),
            P(None, ("dp", "mp"), None),
            P(None, "dp"),
            P("dp", "mp"),
            P("dp", "mp"),
            P("dp", "mp"),
            P("dp", "mp"),
            P("dp", "mp"),
            P("dp", "mp"),
            P("dp", "mp"),
            P("dp"),
            P("dp"),
            P(None, ("dp", "mp"), None),
        ),
        out_specs=(
            P(None, ("dp", "mp"), None),
            P(None, ("dp", "mp"), None),
            P(None, ("dp", "mp"), None),
            P("dp", "mp"),
            P("dp", "mp"),
            P("dp", "mp"),
            P("dp", "mp"),
            P("dp", "mp"),
            P("dp", "mp"),
            P("dp", "mp"),
            P(("dp", "mp")),
            P(("dp", "mp")),
        ),
        check_vma=False,
    )
```

```python
import jax
import jax.numpy as jnp
import numpy as np
from jax import lax
from jax.experimental import pallas as pl
from jax.experimental.pallas import tpu as pltpu
from jax.sharding import PartitionSpec as P

HEAD_DIM = 64


EPSILON = 1e-06
THETA = 10000.0


def normalize(rows):
    factor = lax.rsqrt(jnp.mean(rows * rows, axis=-1, keepdims=True) + EPSILON)
    return (rows * factor, factor)


def norm_back(grad_normed, normed, factor):
    return factor * (grad_normed - normed * jnp.mean(grad_normed * normed, axis=-1, keepdims=True))


def rotary_tables(position, head_size):
    halfway = head_size // 2
    inverse = THETA ** (-2.0 * jnp.arange(halfway, dtype=jnp.float32) / head_size)
    angles = position.astype(jnp.float32)[:, None] * inverse[None, :]
    return (jnp.cos(angles), jnp.sin(angles))


def rotate(values, cosine, sine, direction):
    halfway = values.shape[-1] // 2
    former = values[..., :halfway]
    latter = values[..., halfway:]
    cos_rows = cosine[:, None, :]
    sin_rows = direction * sine[:, None, :]
    return jnp.concatenate(
        [former * cos_rows - latter * sin_rows, latter * cos_rows + former * sin_rows], axis=-1
    )


def layout(packed, length):
    index_rows = jnp.arange(length, dtype=jnp.int32)
    second = jnp.where((packed == 2) & (index_rows >= length // 2), 1, 0).astype(jnp.int32)
    return (second, index_rows - second * (length // 2))


def block_scores(query, key_rows, second, offset, block_rows, key_end, scale):
    raw = (
        jnp.einsum(
            "qhd,khd->hqk",
            query[offset : offset + block_rows],
            key_rows,
            preferred_element_type=jnp.float32,
        )
        * scale
    )
    row_ids = offset + jnp.arange(block_rows, dtype=jnp.int32)
    col_ids = jnp.arange(key_end, dtype=jnp.int32)
    allowed = (col_ids[None, :] <= row_ids[:, None]) & (
        second[offset : offset + block_rows][:, None] == second[None, :]
    )
    return jnp.where(allowed[None], raw, -1e30)


def whole_rows(part):
    return lax.all_gather(part, "mp", axis=0, tiled=True)


def summed_rows(term, local_rows):
    return lax.psum_scatter(
        term(jnp.int32(0), local_rows * lax.axis_size("mp")).astype(jnp.bfloat16),
        "mp",
        scatter_dimension=0,
        tiled=True,
    ).astype(jnp.float32)


def fetch(w_query, w_key, w_value, w_out, w_gate, w_up, w_down, gain_attn, gain_mlp):
    return (
        lax.all_gather(w_query, "dp", axis=0, tiled=True),
        lax.all_gather(w_key, "dp", axis=0, tiled=True),
        lax.all_gather(w_value, "dp", axis=0, tiled=True),
        lax.all_gather(w_out, "dp", axis=0, tiled=True),
        lax.all_gather(w_gate, "dp", axis=0, tiled=True),
        lax.all_gather(w_up, "dp", axis=0, tiled=True),
        lax.all_gather(w_down, "dp", axis=0, tiled=True),
        lax.all_gather(gain_attn, "dp", axis=0, tiled=True),
        lax.all_gather(gain_mlp, "dp", axis=0, tiled=True),
    )


def project_back(left, right):
    return jnp.einsum("rc,dc->rd", left, right, preferred_element_type=jnp.float32)


def outer_sum(left, right):
    return jnp.einsum("td,tc->dc", left, right, preferred_element_type=jnp.float32)


def body(
    tokens,
    first_values,
    sequences,
    w_query,
    w_key,
    w_value,
    w_out,
    w_gate,
    w_up,
    w_down,
    gain_attn,
    gain_mlp,
    cotangent,
):
    micro = tokens.shape[0]
    local_rows = tokens.shape[1]
    length = local_rows * lax.axis_size("mp")
    heads_here = w_query.shape[1] // HEAD_DIM
    block_rows = min(512, length)
    scale = HEAD_DIM ** (-0.5)
    saved = []
    outputs = []
    for batch in range(micro):
        full = fetch(w_query, w_key, w_value, w_out, w_gate, w_up, w_down, gain_attn, gain_mlp)
        q_full, k_full, v_full, o_full, gate_full, up_full, down_full, gain_one, gain_two = full
        gain_one = gain_one.astype(jnp.float32)
        gain_two = gain_two.astype(jnp.float32)
        x_rows = tokens[batch].astype(jnp.float32)
        normed_one, factor_one = normalize(x_rows)
        input_one = whole_rows((normed_one * gain_one[None, :]).astype(jnp.bfloat16))
        second, position = layout(sequences[batch, 0], length)
        cosine, sine = rotary_tables(position, HEAD_DIM)
        query = jnp.dot(input_one, q_full, preferred_element_type=jnp.float32).reshape(
            length, heads_here, HEAD_DIM
        )
        query = rotate(query, cosine, sine, 1.0).astype(jnp.bfloat16)
        key_rows = jnp.dot(input_one, k_full, preferred_element_type=jnp.float32).reshape(
            length, heads_here, HEAD_DIM
        )
        key_rows = rotate(key_rows, cosine, sine, 1.0).astype(jnp.bfloat16)
        first_here = lax.all_to_all(
            first_values[batch], "mp", split_axis=1, concat_axis=0, tiled=True
        )
        mixed = 0.5 * (
            jnp.dot(input_one, v_full, preferred_element_type=jnp.float32)
            + first_here.astype(jnp.float32)
        )
        mixed = mixed.astype(jnp.bfloat16).reshape(length, heads_here, HEAD_DIM)
        pieces = []
        logsums = []
        for offset in range(0, length, block_rows):
            key_end = length
            scores = block_scores(query, key_rows, second, offset, block_rows, key_end, scale)
            highest = jnp.max(scores, axis=-1, keepdims=True)
            powers = jnp.exp(scores - highest)
            denominator = jnp.sum(powers, axis=-1, keepdims=True)
            probs_low = (powers / denominator).astype(jnp.bfloat16)
            logsums.append(highest + jnp.log(denominator))
            pieces.append(
                jnp.einsum("hqk,khd->qhd", probs_low, mixed, preferred_element_type=jnp.float32)
            )
        attended = (
            jnp.concatenate(pieces, axis=0)
            .reshape(length, heads_here * HEAD_DIM)
            .astype(jnp.bfloat16)
        )

        def attn_term(offset, amount):
            return project_back(attended, o_full)

        mid_rows = x_rows + summed_rows(attn_term, local_rows)
        normed_two, factor_two = normalize(mid_rows)
        input_two = whole_rows((normed_two * gain_two[None, :]).astype(jnp.bfloat16))
        gate = jnp.dot(input_two, gate_full, preferred_element_type=jnp.float32)
        upward = jnp.dot(input_two, up_full, preferred_element_type=jnp.float32)
        sigma = jax.nn.sigmoid(gate)
        hidden = (gate * sigma * upward).astype(jnp.bfloat16)

        def mlp_term(offset, amount):
            return project_back(hidden, down_full)

        mlp_rows = summed_rows(mlp_term, local_rows)
        outputs.append((mid_rows + mlp_rows).astype(jnp.bfloat16))
        saved.append(
            (
                normed_one,
                factor_one,
                input_one,
                second,
                cosine,
                sine,
                query,
                key_rows,
                mixed,
                logsums,
                attended,
                normed_two,
                factor_two,
                input_two,
                gate,
                sigma,
                upward,
                hidden,
            )
        )
    grad_sum = None
    gain_grad_one = jnp.zeros((tokens.shape[2],), jnp.float32)
    gain_grad_two = jnp.zeros((tokens.shape[2],), jnp.float32)
    grad_tokens = []
    grad_first = []
    for batch in range(micro):
        (
            normed_one,
            factor_one,
            input_one,
            second,
            cosine,
            sine,
            query,
            key_rows,
            mixed,
            logsums,
            attended,
            normed_two,
            factor_two,
            input_two,
            gate,
            sigma,
            upward,
            hidden,
        ) = saved[batch]
        full = fetch(w_query, w_key, w_value, w_out, w_gate, w_up, w_down, gain_attn, gain_mlp)
        q_full, k_full, v_full, o_full, gate_full, up_full, down_full, gain_one, gain_two = full
        gain_one = gain_one.astype(jnp.float32)
        gain_two = gain_two.astype(jnp.float32)
        grad_rows = cotangent[batch]
        grad_full = whole_rows(grad_rows)
        grad_down = outer_sum(grad_full, hidden)
        grad_hidden = jnp.dot(grad_full, down_full, preferred_element_type=jnp.float32)
        grad_gate = (grad_hidden * upward * sigma * (1.0 + gate * (1.0 - sigma))).astype(
            jnp.bfloat16
        )
        grad_up = (grad_hidden * gate * sigma).astype(jnp.bfloat16)
        grad_gate_w = outer_sum(input_two, grad_gate)
        grad_up_w = outer_sum(input_two, grad_up)

        def mlp_back(offset, amount):
            return project_back(grad_gate, gate_full) + project_back(grad_up, up_full)

        grad_input_two = summed_rows(mlp_back, local_rows)
        gain_grad_two = gain_grad_two + jnp.sum(grad_input_two * normed_two, axis=0)
        grad_mid = grad_rows.astype(jnp.float32) + norm_back(
            grad_input_two * gain_two[None, :], normed_two, factor_two
        )
        grad_attn = whole_rows(grad_mid.astype(jnp.bfloat16))
        grad_out_w = outer_sum(grad_attn, attended)
        grad_attended = jnp.dot(grad_attn, o_full, preferred_element_type=jnp.float32)
        grad_attended = grad_attended.astype(jnp.bfloat16).reshape(length, heads_here, HEAD_DIM)
        grad_mixed = jnp.zeros((length, heads_here, HEAD_DIM), jnp.float32)
        grad_key = jnp.zeros((length, heads_here, HEAD_DIM), jnp.float32)
        query_parts = []
        for turn, offset in enumerate(range(0, length, block_rows)):
            key_end = length
            scores = block_scores(query, key_rows, second, offset, block_rows, key_end, scale)
            probs = jnp.exp(scores - logsums[turn])
            grad_block = grad_attended[offset : offset + block_rows]
            grad_probs = jnp.einsum(
                "qhd,khd->hqk", grad_block, mixed, preferred_element_type=jnp.float32
            )
            grad_mixed = grad_mixed.at[:key_end].add(
                jnp.einsum(
                    "hqk,qhd->khd",
                    probs.astype(jnp.bfloat16),
                    grad_block,
                    preferred_element_type=jnp.float32,
                )
            )
            grad_scores = probs * (grad_probs - jnp.sum(probs * grad_probs, axis=-1, keepdims=True))
            grad_scores = grad_scores.astype(jnp.bfloat16)
            query_parts.append(
                jnp.einsum(
                    "hqk,khd->qhd", grad_scores, key_rows, preferred_element_type=jnp.float32
                )
                * scale
            )
            grad_key = grad_key.at[:key_end].add(
                jnp.einsum(
                    "hqk,qhd->khd",
                    grad_scores,
                    query[offset : offset + block_rows],
                    preferred_element_type=jnp.float32,
                )
                * scale
            )
        grad_mixed_low = grad_mixed.reshape(length, heads_here * HEAD_DIM).astype(jnp.bfloat16)
        grad_value = (0.5 * grad_mixed_low.astype(jnp.float32)).astype(jnp.bfloat16)
        grad_query = rotate(jnp.concatenate(query_parts, axis=0), cosine, sine, -1.0)
        grad_query = grad_query.reshape(length, heads_here * HEAD_DIM).astype(jnp.bfloat16)
        grad_key_low = (
            rotate(grad_key, cosine, sine, -1.0)
            .reshape(length, heads_here * HEAD_DIM)
            .astype(jnp.bfloat16)
        )
        grad_query_w = outer_sum(input_one, grad_query)
        grad_key_w = outer_sum(input_one, grad_key_low)
        grad_value_w = outer_sum(input_one, grad_value)

        def attn_back(offset, amount):
            return (
                project_back(grad_query, q_full)
                + project_back(grad_key_low, k_full)
                + project_back(grad_value, v_full)
            )

        grad_input_one = summed_rows(attn_back, local_rows)
        gain_grad_one = gain_grad_one + jnp.sum(grad_input_one * normed_one, axis=0)
        grad_tokens.append(
            grad_mid + norm_back(grad_input_one * gain_one[None, :], normed_one, factor_one)
        )
        returned = lax.all_to_all(grad_mixed_low, "mp", split_axis=0, concat_axis=1, tiled=True)
        grad_first.append(0.5 * returned.astype(jnp.float32))
        shared = (
            lax.psum_scatter(
                grad_query_w.astype(jnp.bfloat16), "dp", scatter_dimension=0, tiled=True
            ).astype(jnp.float32),
            lax.psum_scatter(
                grad_key_w.astype(jnp.bfloat16), "dp", scatter_dimension=0, tiled=True
            ).astype(jnp.float32),
            lax.psum_scatter(
                grad_value_w.astype(jnp.bfloat16), "dp", scatter_dimension=0, tiled=True
            ).astype(jnp.float32),
            lax.psum_scatter(
                grad_out_w.astype(jnp.bfloat16), "dp", scatter_dimension=0, tiled=True
            ).astype(jnp.float32),
            lax.psum_scatter(
                grad_gate_w.astype(jnp.bfloat16), "dp", scatter_dimension=0, tiled=True
            ).astype(jnp.float32),
            lax.psum_scatter(
                grad_up_w.astype(jnp.bfloat16), "dp", scatter_dimension=0, tiled=True
            ).astype(jnp.float32),
            lax.psum_scatter(
                grad_down.astype(jnp.bfloat16), "dp", scatter_dimension=0, tiled=True
            ).astype(jnp.float32),
        )
        grad_sum = shared if grad_sum is None else jax.tree.map(jnp.add, grad_sum, shared)
    gain_parts = (
        lax.psum_scatter(gain_grad_one, ("dp", "mp"), scatter_dimension=0, tiled=True),
        lax.psum_scatter(gain_grad_two, ("dp", "mp"), scatter_dimension=0, tiled=True),
    )
    return (
        jnp.stack(outputs),
        jnp.stack(grad_tokens),
        jnp.stack(grad_first),
        grad_sum[0],
        grad_sum[1],
        grad_sum[2],
        grad_sum[3],
        grad_sum[4],
        grad_sum[5],
        grad_sum[6],
        gain_parts[0],
        gain_parts[1],
    )


def rope_tables():
    half = HEAD_DIM // 2
    inverse = (THETA ** (-2.0 * np.arange(half) / HEAD_DIM)).astype(np.float32)
    angles = np.arange(1024, dtype=np.float32)[:, None] * inverse[None, :]
    cosine, sine = np.cos(angles), np.sin(angles)
    return (
        jnp.asarray(np.concatenate([cosine] * 4, axis=1), jnp.float32),
        jnp.asarray(np.concatenate([-sine, sine, -sine, sine], axis=1), jnp.float32),
    )


BF = jnp.bfloat16
F32 = jnp.float32
MESH = pl.DeviceIdType.MESH
CHUNK = 256
FFC = 704
PIECE = 3 * FFC + 256
QROWS = 400


def remote(src, dst, send, recv, device):
    return pltpu.make_async_remote_copy(
        src_ref=src, dst_ref=dst, send_sem=send, recv_sem=recv, device_id=device, device_id_type=MESH
    )


class Place:
    def __init__(self):
        self.d = d = lax.axis_index("dp")
        self.z = z = lax.axis_index("mp")
        core = lax.rem(d, 2)
        along_x = lax.rem(lax.div(d, 2), 2)
        along_y = lax.div(d, 4)
        self.dc = d + 1 - 2 * core
        self.dx = d + 2 - 4 * along_x
        self.dy = d + 4 - 8 * along_y
        self.dxy = self.dx + 4 - 8 * along_y
        self.core = (self.dc, z)
        self.x = (self.dx, z)
        self.y = (self.dy, z)
        self.quads = (d, self.dx, self.dy, self.dxy)
        self.core_quads = tuple(q + 1 - 2 * core for q in self.quads)

    def peer(self, step):
        return lax.rem(self.z + step, 4)

    def greet(self):
        barrier = pltpu.get_barrier_semaphore()
        others = [self.core, self.x, self.y] + [(self.d, self.peer(s)) for s in (1, 2, 3)]
        for other in others:
            pl.semaphore_signal(barrier, inc=1, device_id=other, device_id_type=MESH)
        pl.semaphore_wait(barrier, len(others))

    def hop(self, step, visit):
        for sign in (1, -1):
            m = self.z + sign * step

            @pl.when((m >= 0) & (m <= 3))
            def _():
                visit(m)


class Gather:
    def __init__(self, place, at, own, sems):
        self.p, self.at, self.own = place, at, own
        self.right, self.left, self.sx, self.sy, self.sc, self.arrived = sems

    def send(self, src, m, d, sem, device):
        remote(src, self.at(m, d), sem, self.arrived.at[m, d], device).start()

    def along_z(self, m, src=None):
        p = self.p
        src = self.at(m, p.d) if src is None else src

        @pl.when((m <= p.z) & (p.z < 3))
        def _():
            self.send(src, m, p.d, self.right.at[m], (p.d, p.z + 1))

        @pl.when((m >= p.z) & (p.z > 0))
        def _():
            self.send(src, m, p.d, self.left.at[m], (p.d, p.z - 1))

    def spread(self, m, src=None):
        p = self.p
        src = self.at(m, p.d) if src is None else src
        self.send(src, m, p.d, self.sx.at[m], p.x)
        self.send(src, m, p.d, self.sy.at[m], p.y)
        self.send(src, m, p.d, self.sc.at[m], p.core)

    def take(self, m, d):
        remote(self.at(m, d), self.at(m, d), self.sc.at[0], self.arrived.at[m, d], self.p.core).wait_recv()

    def z_in(self, m):
        self.take(m, self.p.d)
        self.along_z(m)

    def x_in(self, m):
        p = self.p
        self.take(m, p.dx)
        src = self.at(m, p.dx)

        @pl.when(lax.rem(m, 2) == 0)
        def _():
            self.send(src, m, p.dx, self.sy.at[4 + m], p.y)

        self.send(src, m, p.dx, self.sc.at[4 + m], p.core)

    def y_in(self, m):
        p = self.p
        self.take(m, p.dy)
        src = self.at(m, p.dy)

        @pl.when(lax.rem(m, 2) == 1)
        def _():
            self.send(src, m, p.dy, self.sx.at[4 + m], p.x)

        self.send(src, m, p.dy, self.sc.at[8 + m], p.core)

    def diag_in(self, m):
        p = self.p
        self.take(m, p.dxy)
        self.send(self.at(m, p.dxy), m, p.dxy, self.sc.at[12 + m], p.core)

    def core_in(self, m):
        for d in self.p.core_quads:
            self.take(m, d)

    def finish(self):
        p = self.p

        def sent(sem, device):
            remote(self.own, self.own, sem, self.arrived.at[0, 0], device).wait_send()

        for m in range(4):

            @pl.when((m <= p.z) & (p.z < 3))
            def _():
                sent(self.right.at[m], p.core)

            @pl.when((m >= p.z) & (p.z > 0))
            def _():
                sent(self.left.at[m], p.core)

            sent(self.sx.at[m], p.core)
            sent(self.sy.at[m], p.core)
            sent((self.sx if m % 2 else self.sy).at[4 + m], p.core)
            for q in range(4):
                sent(self.sc.at[4 * q + m], p.core)


def gather_sems():
    dma = pltpu.SemaphoreType.DMA
    return [dma((4,)), dma((4,)), dma((8,)), dma((8,)), dma((16,)), dma((4, 8))]


def lanes(shape, width):
    return lax.div(lax.broadcasted_iota(jnp.int32, shape, 1), width)


def turned(x, cosine, sine):
    first = lax.rem(lanes(x.shape, 32), 2) == 0
    width = x.shape[1]
    other = jnp.where(first, pltpu.roll(x, width - 32, 1), pltpu.roll(x, 32, 1))
    return x * cosine + other * sine


def wide(table):
    return jnp.concatenate([table, table], axis=1)


def dot(a, b):
    return lax.dot_general(a, b, (((1,), (0,)), ((), ())), preferred_element_type=F32)


def dot_nt(a, b):
    return lax.dot_general(a, b, (((1,), (1,)), ((), ())), preferred_element_type=F32)


def dot_tn(a, b):
    return lax.dot_general(a, b, (((0,), (0,)), ((), ())), preferred_element_type=F32)


def tile_scores(q_head, keys, tile, packed):
    n = (tile + 1) * CHUNK
    s = dot_nt(q_head, keys) * 0.125
    rows = lax.broadcasted_iota(jnp.int32, (CHUNK, n), 0) + tile * CHUNK
    cols = lax.broadcasted_iota(jnp.int32, (CHUNK, n), 1)
    allowed = cols <= rows
    if tile >= 2:
        allowed = allowed & ((packed != 2) | (cols >= 2 * CHUNK))
    return jnp.where(allowed, s, -1e30)


ORDER = (3, 0, 1, 2)


def add_rows(dst, terms, step):
    def rows(r, carry):
        at = pl.ds(pl.multiple_of(r * step, step), step)
        total = terms[0][at, :].astype(F32)
        for term in terms[1:]:
            total = total + term[at, :].astype(F32)
        dst[at, :] = total.astype(dst.dtype)
        return carry

    lax.fori_loop(0, dst.shape[0] // step, rows, 0)


def spans(n, step):
    return [(at, min(step, n - at)) for at in range(0, n, step)]


def block(i):
    return pl.ds(pl.multiple_of(i * CHUNK, CHUNK), CHUNK)


class Moves:
    def __init__(self, sems):
        self.sems, self.made = sems, []

    def start(self, src, dst):
        copy = pltpu.make_async_copy(src, dst, self.sems.at[len(self.made)])
        copy.start()
        self.made.append(copy)
        return len(self.made) - 1

    def wait(self, i):
        self.made[i].wait()
        self.made[i] = self.made[i], True

    def rest(self):
        for copy in self.made:
            if not isinstance(copy, tuple):
                copy.wait()


class Crossing:
    def __init__(self, place, part, bufs, sems, out, step):
        self.p, self.part, self.out, self.step = place, part, out, step
        self.acc, self.corner, self.bx, self.by = bufs
        (self.s_core, self.r_core, self.s_corner, self.r_corner,
         self.s_x, self.r_x, self.s_y, self.r_y) = sems

    def core_copy(self, m, q):
        p = self.p
        return remote(
            self.part(m, p.core_quads[q]), self.acc.at[m, q],
            self.s_core.at[m, q], self.r_core.at[m, q], p.core,
        )

    def begin(self, m):
        for q in (3, 1, 2, 0):
            self.core_copy(m, q).start()

    def corner_copy(self, m):
        to = self.p.x if m % 2 == 0 else self.p.y
        return remote(self.acc.at[m, 3], self.corner.at[m], self.s_corner.at[m], self.r_corner.at[m], to)

    def x_copy(self, m):
        return remote(self.acc.at[m, 1], self.bx.at[m], self.s_x.at[m], self.r_x.at[m], self.p.x)

    def y_copy(self, m):
        return remote(self.acc.at[m, 2], self.by.at[m], self.s_y.at[m], self.r_y.at[m], self.p.y)

    def join(self, m):
        first = 1 if m % 2 == 0 else 2
        for q in (3, first, 3 - first, 0):
            self.core_copy(m, q).wait_recv()
            add_rows(self.acc.at[m, q], [self.acc.at[m, q], self.part(m, self.p.quads[q])], self.step)
            if q == 3:
                self.corner_copy(m).start()
            if q == first:
                (self.x_copy if m % 2 == 0 else self.y_copy)(m).start()

    def relay(self, m):
        q = 2 if m % 2 == 0 else 1
        self.corner_copy(m).wait_recv()
        add_rows(self.acc.at[m, q], [self.acc.at[m, q], self.corner.at[m]], self.step)
        (self.y_copy if m % 2 == 0 else self.x_copy)(m).start()

    def total(self, m):
        self.x_copy(m).wait_recv()
        self.y_copy(m).wait_recv()
        add_rows(self.out.at[m], [self.acc.at[m, 0], self.bx.at[m], self.by.at[m]], self.step)

    def core_sent(self, m):
        for q in range(4):
            self.core_copy(m, q).wait_send()

    def finish(self):
        for m in range(4):
            self.corner_copy(m).wait_send()
            self.x_copy(m).wait_send()
            self.y_copy(m).wait_send()


def crossing_scratch(rows, width):
    def buf(*lead):
        return pltpu.VMEM((*lead, rows, width), BF)

    dma = pltpu.SemaphoreType.DMA
    return [buf(4, 4), buf(4), buf(4), buf(4), dma((4, 4)), dma((4, 4))] + [dma((4,))] * 6


class Chain:
    def __init__(self, place, part, bufs, sems, out, step):
        self.p, self.part, self.out, self.step = place, part, out, step
        self.br, self.bl = bufs
        self.s_r, self.r_r, self.s_l, self.r_l = sems

    def r_copy(self, m):
        p = self.p
        return remote(self.part.at[m], self.br.at[m], self.s_r.at[m], self.r_r.at[m], (p.d, p.z + 1))

    def l_copy(self, m):
        p = self.p
        return remote(self.part.at[m], self.bl.at[m], self.s_l.at[m], self.r_l.at[m], (p.d, p.z - 1))

    def level(self, k):
        @pl.when(self.p.z == k)
        def _():
            for m in range(3, k, -1):
                if k > 0:
                    self.r_copy(m).wait_recv()
                    add_rows(self.part.at[m], [self.part.at[m], self.br.at[m]], self.step)
                self.r_copy(m).start()

        @pl.when(self.p.z == 3 - k)
        def _():
            for m in range(0, 3 - k):
                if k > 0:
                    self.l_copy(m).wait_recv()
                    add_rows(self.part.at[m], [self.part.at[m], self.bl.at[m]], self.step)
                self.l_copy(m).start()

    def last(self):
        for m in range(4):

            @pl.when(self.p.z == m)
            def _():
                terms = [self.part.at[m]]
                if m > 0:
                    self.r_copy(m).wait_recv()
                    terms.append(self.br.at[m])
                if m < 3:
                    self.l_copy(m).wait_recv()
                    terms.append(self.bl.at[m])
                add_rows(self.out, terms, self.step)

    def finish(self):
        for m in range(4):
            if m > 0:

                @pl.when(self.p.z < m)
                def _():
                    self.r_copy(m).wait_send()

            if m < 3:

                @pl.when(self.p.z > m)
                def _():
                    self.l_copy(m).wait_send()


def chain_scratch(rows, width):
    dma = pltpu.SemaphoreType.DMA
    return [pltpu.VMEM((4, rows, width), BF)] * 2 + [dma((4,))] * 4


def forward_kernel(
    seq, wq, wk, wv, wo_own, wg_t, wu_t, wd_t, gain_attn, gain_mlp, cos_t, sin_t, tok_in, fv_in, cot_in,
    f2, acts, f1_out, qkv_out, o_out, lse_out, rows_out, a1t_out, a2_out, dattn_out, mid_out, layer_out, do_out, do_last, gain_part,
    tok, fv, cot, f1, qkv, o_head, lse, o_rows, a1_t, a1, stage, p2, w, wo, a2, mid, y_out, acc, back, act, dattn, do_rows, do_head, *sems,
):
    p = Place()
    sems = list(sems)
    g1s, g2s = sems[:6], sems[6:12]
    s_qkv, r_qkv, s_o, r_o, s_local, s_do, r_do, w_sems, wo_sems, act_sems, move_sems = sems[12:]
    moves = Moves(move_sems)
    z, d = p.z, p.d
    got_tok = moves.start(tok_in, tok)
    got_fv = moves.start(fv_in, fv)
    got_cot = moves.start(cot_in, cot)
    p.greet()

    f1[z, d, 0:128] = wq[...]
    f1[z, d, 128:256] = wk[...]
    f1[z, d, 256:384] = wv[...]
    f1[z, d, 384:400, 0:128] = jnp.broadcast_to(gain_attn[...], (16, 128))
    f1[z, d, 384:400, 128:256] = jnp.broadcast_to(gain_mlp[...], (16, 128))
    g1 = Gather(p, lambda m, e: f1.at[m, e], f1.at[0, 0], g1s)
    g2 = Gather(p, lambda m, e: f2.at[m, e], p2, g2s)
    g1.along_z(z)
    g1.spread(z)
    for i, source in enumerate((wg_t, wu_t, wd_t)):
        p2[i * FFC : (i + 1) * FFC, :] = source[...]
    p2[3 * FFC :, :] = wo_own[...].T
    own_copy = pltpu.make_async_copy(p2, f2.at[z, d], s_local)
    own_copy.start()

    def arrive(g):
        def visit(m):
            g.z_in(m)
            g.spread(m)
        return visit

    def side(g):
        def visit(m):
            g.x_in(m)
            g.y_in(m)
        return visit

    p.hop(1, arrive(g1))
    side(g1)(z)
    p.hop(2, arrive(g1))
    g2.along_z(z, p2)
    p.hop(1, side(g1))
    g1.diag_in(z)
    p.hop(3, arrive(g1))
    g1.core_in(z)

    gain_row = jnp.concatenate([f1[z, e, 384:400, :].astype(F32)[0:8] for e in range(8)], axis=1)
    gain_two = jnp.concatenate([gain_row[0:1, e * 256 + 128 : e * 256 + 256] for e in range(8)], axis=1)
    moves.wait(got_tok)

    def norm_body(b, carry):
        x = tok[b].astype(F32)
        factor = lax.rsqrt(jnp.mean(x * x, axis=1, keepdims=True) + EPSILON)
        for e in range(8):
            cols = slice(e * 128, (e + 1) * 128)
            a1[pl.ds(pl.multiple_of(b * CHUNK, CHUNK), CHUNK), cols] = (
                x[:, cols] * factor * gain_row[0:1, e * 256 : e * 256 + 128]
            ).astype(BF)
        return carry

    lax.fori_loop(0, 3, norm_body, 0)

    p.hop(2, side(g1))
    p.hop(1, g1.diag_in)
    p.hop(3, side(g1))
    p.hop(2, g1.diag_in)
    p.hop(1, g2.z_in)
    p.hop(1, g1.core_in)
    p.hop(3, g1.diag_in)
    p.hop(2, g1.core_in)
    p.hop(3, g1.core_in)
    g2.spread(z, p2)
    p.hop(1, g2.spread)
    moves.start(f1, f1_out)
    moves.wait(got_fv)

    def project(b):
        pos_full = pl.ds(pl.multiple_of(z * CHUNK, CHUNK), CHUNK)
        low = jnp.where(z >= 2, z - 2, z)
        pos_half = pl.ds(pl.multiple_of(low * CHUNK, CHUNK), CHUNK)
        second = seq[b] == 2
        cosine = wide(jnp.where(second, cos_t[pos_half, :], cos_t[pos_full, :]))
        sine = wide(jnp.where(second, sin_t[pos_half, :], sin_t[pos_full, :]))
        rows = a1[b * CHUNK : (b + 1) * CHUNK, :]

        def one(step, carry):
            m = lax.rem(z + step, 4)
            w = lambda i: f1[m, :, i * 128 : (i + 1) * 128, :].reshape(1024, CHUNK)
            stage[b, m, 0] = turned(dot(rows, w(0)), cosine, sine).astype(BF)
            stage[b, m, 1] = turned(dot(rows, w(1)), cosine, sine).astype(BF)
            first = fv[b, :, pl.ds(pl.multiple_of(m * CHUNK, CHUNK), CHUNK)].astype(F32)
            stage[b, m, 2] = (0.5 * (dot(rows, w(2)) + first)).astype(BF)
            return carry

        lax.fori_loop(0, 4, one, 0)
        for i in range(3):
            qkv[b, i, block(z), :] = stage[b, z, i]

    def qkv_copy(b, step):
        m = p.peer(step)
        dst = qkv.at[b, :, pl.ds(pl.multiple_of(z * CHUNK, CHUNK), CHUNK), :]
        return remote(stage.at[b, m], dst, s_qkv.at[b, step - 1], r_qkv.at[b, z], (d, m))

    def send_qkv(b):
        for step in (1, 2, 3):
            qkv_copy(b, step).start()

    def sent_qkv(b):
        for step in (1, 2, 3):
            qkv_copy(b, step).wait_send()

    def take_qkv(b):
        for step in (1, 2, 3):
            m = p.peer(step)
            dst = qkv.at[b, :, pl.ds(pl.multiple_of(m * CHUNK, CHUNK), CHUNK), :]
            remote(stage.at[b, m], dst, s_qkv.at[b, 0], r_qkv.at[b, m], (d, m)).wait_recv()

    def o_copy(b, i):
        rows = slice(i * CHUNK, (i + 1) * CHUNK)
        return remote(o_head.at[b, rows, :], o_rows.at[b, z], s_o.at[b, i], r_o.at[b, z], (d, i))

    def attend(b, i):
        n = (i + 1) * CHUNK
        rows = slice(i * CHUNK, n)
        packed = seq[b]
        q = qkv[b, 0, rows, :]
        keys = qkv[b, 1, 0:n, :]
        values = qkv[b, 2, 0:n, :]
        head_of = lanes((CHUNK, CHUNK), 64)
        lane = lax.broadcasted_iota(jnp.int32, (CHUNK, 128), 1)

        def head(h, carry):
            out, stats = carry
            s = tile_scores(jnp.where(head_of == h, q, jnp.zeros_like(q)), keys, i, packed)
            top = jnp.max(s, axis=1, keepdims=True)
            e = jnp.exp(s - top)
            total = jnp.sum(e, axis=1, keepdims=True)
            part = dot(e.astype(BF), values) * (1.0 / total)
            return (
                jnp.where(head_of == h, part, out),
                jnp.where(lane == h, top + jnp.log(total), stats),
            )

        out, stats = lax.fori_loop(
            0, 4, head, (jnp.zeros((CHUNK, CHUNK), F32), jnp.zeros((CHUNK, 128), F32))
        )
        o_head[b, rows, :] = out.astype(BF)
        lse[b, rows, :] = stats

        @pl.when(z == i)
        def _():
            o_rows[b, z] = out.astype(BF)

        @pl.when(z != i)
        def _():
            o_copy(b, i).start()

    def take_o(b):
        for step in (1, 2, 3):
            m = p.peer(step)
            remote(o_rows.at[b, m], o_rows.at[b, m], s_o.at[b, 0], r_o.at[b, m], (d, m)).wait_recv()

    def w_copy(t, e):
        m, slot = lax.rem(t, 4), lax.rem(t, 2)
        return pltpu.make_async_copy(
            f2.at[m, e, 0 : 3 * FFC, :], w.at[slot, :, e * 128 : (e + 1) * 128], w_sems.at[slot, e]
        )

    def wo_copy(m, e):
        return pltpu.make_async_copy(
            f2.at[m, e, 3 * FFC :, :], wo.at[m, :, e * 128 : (e + 1) * 128], wo_sems.at[m, e]
        )

    def act_copy(b, m, slot):
        return pltpu.make_async_copy(
            act.at[slot], acts.at[:, m, b * CHUNK : (b + 1) * CHUNK, :], act_sems.at[slot]
        )

    def load_mlp():
        for m in range(4):
            for e in range(8):
                wo_copy(m, e).start()
        for e in range(8):
            w_copy(0, e).start()
        for m in range(4):
            for e in range(8):
                wo_copy(m, e).wait()

    def do_copy(b, step):
        m = p.peer(step)
        return remote(
            do_rows.at[b, m], do_head.at[b, block(z), :], s_do.at[b, step - 1], r_do.at[b, z], (d, m)
        )

    def send_do(b):
        for step in (1, 2, 3):
            do_copy(b, step).start()
        do_head[b, block(z), :] = do_rows[b, z]

    def mlp_rows(b):
        rows = slice(b * CHUNK, (b + 1) * CHUNK)
        x2 = tok[b].astype(F32)
        for m in range(4):
            x2 = x2 + dot(o_rows[b, m], wo[m])
        factor = lax.rsqrt(jnp.mean(x2 * x2, axis=1, keepdims=True) + EPSILON)
        mid[b] = x2
        a2[rows, :] = (x2 * factor * gain_two).astype(BF)

        def chunk(m, carry):
            t = b * 4 + m
            slot = lax.rem(m, 2)
            for e in range(8):
                w_copy(t, e).wait()

            @pl.when(t < 11)
            def _():
                for e in range(8):
                    w_copy(t + 1, e).start()

            @pl.when(t >= 2)
            def _():
                act_copy(b, m, slot).wait()

            for at, size in spans(FFC, 256):
                cols = slice(at, at + size)
                gate = dot_nt(a2[rows, :], w[slot, at : at + size, :])
                up = dot_nt(a2[rows, :], w[slot, FFC + at : FFC + at + size, :])
                dh = dot_nt(cot[b], w[slot, 2 * FFC + at : 2 * FFC + at + size, :])
                sg = jax.nn.sigmoid(gate)
                silu = gate * sg
                act[slot, 0, :, cols] = (dh * up * (sg + silu * (1.0 - sg))).astype(BF)
                act[slot, 1, :, cols] = (dh * silu).astype(BF)
                act[slot, 2, :, cols] = (silu * up).astype(BF)
            for at, size in spans(1024, 256):
                cols = slice(at, at + size)
                y = dot(act[slot, 2], w[slot, 2 * FFC : 3 * FFC, cols])
                u = dot(act[slot, 0], w[slot, 0:FFC, cols]) + dot(act[slot, 1], w[slot, FFC : 2 * FFC, cols])
                acc[:, cols] = jnp.where(m == 0, y, acc[:, cols] + y)
                back[:, cols] = jnp.where(m == 0, u, back[:, cols] + u)
            act_copy(b, m, slot).start()
            return carry

        lax.fori_loop(0, 4, chunk, 0)
        x2 = mid[b]
        y_out[b] = (x2 + acc[...]).astype(BF)
        factor = lax.rsqrt(jnp.mean(x2 * x2, axis=1, keepdims=True) + EPSILON)
        n2 = x2 * factor
        da2 = back[...]
        sums = jnp.broadcast_to(jnp.sum(da2 * n2, axis=0, keepdims=True), (8, 1024))
        gain_part[...] = sums if b == 0 else gain_part[...] + sums
        dn2 = da2 * gain_two
        grad_mid = cot[b].astype(F32) + factor * (dn2 - n2 * jnp.mean(dn2 * n2, axis=1, keepdims=True))
        mid[b] = grad_mid
        dattn[rows, :] = grad_mid.astype(BF)

        def heads(m, carry):
            do_rows[b, m] = dot_nt(dattn[rows, :], wo[m]).astype(BF)
            return carry

        lax.fori_loop(0, 4, heads, 0)
        moves.start(mid.at[b], mid_out.at[b])
        moves.start(y_out.at[b], layer_out.at[b])

    def attend_all(b):
        for i in range(4):
            attend(b, i)
        moves.start(o_head.at[b], o_out.at[b])
        moves.start(lse.at[b], lse_out.at[b])

    project(0)
    send_qkv(0)
    p.hop(2, arrive(g2))
    project(1)
    project(2)
    a1_t[...] = a1[...].T
    moves.start(a1_t, a1t_out)
    p.hop(3, arrive(g2))
    side(g2)(z)
    sent_qkv(0)
    send_qkv(1)
    p.hop(1, side(g2))
    g2.diag_in(z)
    take_qkv(0)
    moves.start(qkv.at[0], qkv_out.at[0])
    attend_all(0)
    p.hop(2, side(g2))
    p.hop(1, g2.diag_in)
    sent_qkv(1)
    send_qkv(2)
    take_qkv(1)
    moves.start(qkv.at[1], qkv_out.at[1])
    attend_all(1)
    p.hop(3, side(g2))
    p.hop(2, g2.diag_in)
    p.hop(3, g2.diag_in)
    for m in range(4):
        g2.core_in(m)
    own_copy.wait()
    load_mlp()
    moves.wait(got_cot)
    take_o(0)
    mlp_rows(0)
    take_o(1)
    mlp_rows(1)
    take_qkv(2)
    moves.start(qkv.at[2], qkv_out.at[2])
    attend_all(2)
    send_do(0)
    send_do(1)
    take_o(2)
    moves.start(o_rows, rows_out)
    mlp_rows(2)
    moves.start(a2, a2_out)
    moves.start(dattn, dattn_out)
    moves.start(do_rows.at[2], do_last)
    for b in range(2):
        for step in (1, 2, 3):
            m = p.peer(step)
            dst = do_head.at[b, block(m), :]
            remote(do_rows.at[b, m], dst, s_do.at[b, 0], r_do.at[b, m], (d, m)).wait_recv()
            do_copy(b, step).wait_send()
        moves.start(do_head.at[b], do_out.at[b])
    act_copy(2, 2, 0).wait()
    act_copy(2, 3, 1).wait()
    sent_qkv(2)
    for b in range(3):
        for i in range(4):

            @pl.when(z != i)
            def _():
                o_copy(b, i).wait_send()

    g1.finish()
    g2.finish()
    moves.rest()


def run_forward(*args):
    vmem = pl.BlockSpec(memory_space=pltpu.VMEM)
    hbm = pl.BlockSpec(memory_space=pl.ANY)
    dma = pltpu.SemaphoreType.DMA
    shape = jax.ShapeDtypeStruct
    return pl.pallas_call(
        forward_kernel,
        out_shape=(
            shape((4, 8, PIECE, 128), BF),
            shape((3, 4, 768, FFC), BF),
            shape((4, 8, QROWS, CHUNK), BF),
            shape((3, 3, 1024, CHUNK), BF),
            shape((3, 1024, CHUNK), BF),
            shape((3, 1024, 128), F32),
            shape((3, 4, CHUNK, CHUNK), BF),
            shape((1024, 768), BF),
            shape((768, 1024), BF),
            shape((768, 1024), BF),
            shape((3, CHUNK, 1024), F32),
            shape((3, CHUNK, 1024), BF),
            shape((2, 1024, CHUNK), BF),
            shape((4, CHUNK, CHUNK), BF),
            shape((8, 1024), F32),
        ),
        in_specs=[pl.BlockSpec(memory_space=pltpu.SMEM)] + [vmem] * 11 + [hbm] * 3,
        out_specs=(hbm,) * 14 + (vmem,),
        scratch_shapes=[
            pltpu.VMEM((3, CHUNK, 1024), BF),
            pltpu.VMEM((3, CHUNK, 1024), BF),
            pltpu.VMEM((3, CHUNK, 1024), BF),
            pltpu.VMEM((4, 8, QROWS, CHUNK), BF),
            pltpu.VMEM((3, 3, 1024, CHUNK), BF),
            pltpu.VMEM((3, 1024, CHUNK), BF),
            pltpu.VMEM((3, 1024, 128), F32),
            pltpu.VMEM((3, 4, CHUNK, CHUNK), BF),
            pltpu.VMEM((1024, 768), BF),
            pltpu.VMEM((768, 1024), BF),
            pltpu.VMEM((3, 4, 3, CHUNK, CHUNK), BF),
            pltpu.VMEM((PIECE, 128), BF),
            pltpu.VMEM((2, 3 * FFC, 1024), BF),
            pltpu.VMEM((4, CHUNK, 1024), BF),
            pltpu.VMEM((768, 1024), BF),
            pltpu.VMEM((3, CHUNK, 1024), F32),
            pltpu.VMEM((3, CHUNK, 1024), BF),
            pltpu.VMEM((CHUNK, 1024), F32),
            pltpu.VMEM((CHUNK, 1024), F32),
            pltpu.VMEM((2, 3, CHUNK, FFC), BF),
            pltpu.VMEM((768, 1024), BF),
            pltpu.VMEM((3, 4, CHUNK, CHUNK), BF),
            pltpu.VMEM((2, 1024, CHUNK), BF),
        ]
        + gather_sems()
        + gather_sems()
        + [dma((3, 3)), dma((3, 4)), dma((3, 4)), dma((3, 4)), dma, dma((3, 3)), dma((3, 4))]
        + [dma((2, 8)), dma((4, 8)), dma((2,)), dma((32,))],
        compiler_params=pltpu.CompilerParams(
            collective_id=1, has_side_effects=True, vmem_limit_bytes=62 * 2**20
        ),
        cost_estimate=pl.CostEstimate(flops=5 * 10**10, bytes_accessed=6 * 10**7, transcendentals=8 * 10**6),
        name="gather_forward",
    )(*args)


def backward_kernel(
    seq, cos_t, sin_t, do_last, do_in, qkv_in, o_in, lse_in, rows_in, a2_in, dattn_in, cot_in, acts,
    d_rows, summed,
    do_mine, do_head, qkv, o_head, lse, o_rows, a2, dattn, cot, act, part, total, dk, dv, stage, *rest,
):
    p = Place()
    s_do, r_do, s_d, r_d, act_sems, move_sems = rest[:6]
    z, d = p.z, p.d
    moves = Moves(move_sems)
    got = []
    for b in range(3):
        got.append(
            [moves.start(qkv_in.at[b], qkv.at[b]), moves.start(o_in.at[b], o_head.at[b]), moves.start(lse_in.at[b], lse.at[b])]
            + ([moves.start(do_in.at[b], do_head.at[b])] if b < 2 else [])
        )
        if b == 0:
            got_do = moves.start(do_last, do_mine)
            got_w = [
                moves.start(a2_in, a2), moves.start(dattn_in, dattn), moves.start(cot_in, cot),
                moves.start(rows_in, o_rows),
            ]
    p.greet()

    def act_copy(m, slot):
        return pltpu.make_async_copy(acts.at[:, m], act.at[slot], act_sems.at[slot])

    act_copy(ORDER[0], 0).start()
    moves.wait(got_do)

    def do_copy(step):
        m = p.peer(step)
        return remote(do_mine.at[m], do_head.at[2, block(z), :], s_do.at[step - 1], r_do.at[z], (d, m))

    for step in (1, 2, 3):
        do_copy(step).start()
    do_head[2, block(z), :] = do_mine[z]

    def take_do():
        for step in (1, 2, 3):
            m = p.peer(step)
            dst = do_head.at[2, block(m), :]
            remote(do_mine.at[m], dst, s_do.at[0], r_do.at[m], (d, m)).wait_recv()

    def d_copy(b, i):
        return remote(stage.at[b, i], d_rows.at[b, z], s_d.at[b, i], r_d.at[b, z], (d, i))

    def own_copy(b, i):
        return pltpu.make_async_copy(stage.at[b, i], d_rows.at[b, i], s_d.at[b, i])

    def back(b, i):
        n = (i + 1) * CHUNK
        rows = slice(i * CHUNK, n)
        packed = seq[b]
        head_of = lanes((CHUNK, CHUNK), 64)
        lane = lax.broadcasted_iota(jnp.int32, (CHUNK, 128), 1)
        q = qkv[b, 0, rows, :]
        keys = qkv[b, 1, 0:n, :]
        values = qkv[b, 2, 0:n, :]
        grad = do_head[b, rows, :]
        spread = grad.astype(F32) * o_head[b, rows, :].astype(F32)
        stats = lse[b, rows, :]

        def head(h, dq):
            here = head_of == h
            q_h = jnp.where(here, q, jnp.zeros_like(q))
            g_h = jnp.where(here, grad, jnp.zeros_like(grad))
            delta = jnp.sum(jnp.where(here, spread, 0.0), axis=1, keepdims=True)
            level = jnp.sum(jnp.where(lane == h, stats, 0.0), axis=1, keepdims=True)
            prob = jnp.exp(tile_scores(q_h, keys, i, packed) - level)
            dp = dot_nt(g_h, values)
            ds = (prob * (dp - delta)).astype(BF)
            dv_part = dot_tn(prob.astype(BF), g_h)
            dk_part = dot_tn(ds, q_h)
            dv[0:n, :] += dv_part
            dk[0:n, :] += dk_part
            return jnp.where(here, dot(ds, keys), dq)

        dq = lax.fori_loop(0, 4, head, jnp.zeros((CHUNK, CHUNK), F32))
        cosine, sine = cos_t[rows, :], sin_t[rows, :]
        if i >= 2:
            early = slice((i - 2) * CHUNK, (i - 1) * CHUNK)
            cosine = jnp.where(packed == 2, cos_t[early, :], cosine)
            sine = jnp.where(packed == 2, sin_t[early, :], sine)
        cosine, sine = wide(cosine), -wide(sine)
        stage[b, i, :, 0:256] = turned(dq * 0.125, cosine, sine).astype(BF)
        stage[b, i, :, 256:512] = turned(dk[rows, :] * 0.125, cosine, sine).astype(BF)
        stage[b, i, :, 512:768] = (dv[rows, :] * 0.5).astype(BF)

        @pl.when(z == i)
        def _():
            own_copy(b, i).start()

        @pl.when(z != i)
        def _():
            d_copy(b, i).start()

    def back_all(b):
        for i in got[b]:
            moves.wait(i)
        dk[...] = jnp.zeros_like(dk)
        dv[...] = jnp.zeros_like(dv)
        for i in (3, 2, 1, 0):
            back(b, i)

    crossing = Crossing(p, lambda m, e: part.at[ORDER.index(m) % 2, e], rest[6:10], rest[10:], total, 592)

    def weight_grad(k):
        m, slot = ORDER[k], k % 2
        act_copy(m, slot).wait()
        if k < 3:
            act_copy(ORDER[k + 1], 1 - slot).start()
        if k >= 2:
            crossing.core_sent(ORDER[k - 2])

        for i in range(3):
            right = cot[...].reshape(768, 1024) if i == 2 else a2[...]
            for at, size in spans(FFC, 256):
                out = dot_tn(act[slot, i, :, at : at + size], right).astype(BF)
                for e in range(8):
                    part[slot, e, i * FFC + at : i * FFC + at + size, :] = out[:, e * 128 : (e + 1) * 128]
        own = jnp.concatenate([o_rows[b, m] for b in range(3)], axis=0)
        out = dot_tn(own, dattn[...]).astype(BF)
        for e in range(8):
            part[slot, e, 3 * FFC :, :] = out[:, e * 128 : (e + 1) * 128]
        crossing.begin(m)

    a, b_, c, e_ = ORDER
    back_all(0)
    for i in got_w:
        moves.wait(i)
    weight_grad(0)
    weight_grad(1)
    crossing.join(a)
    crossing.join(b_)
    back_all(1)
    weight_grad(2)
    weight_grad(3)
    crossing.relay(a)
    crossing.relay(b_)
    take_do()
    back_all(2)
    crossing.join(c)
    crossing.join(e_)
    crossing.total(a)
    crossing.total(b_)
    crossing.relay(c)
    crossing.relay(e_)
    crossing.total(c)
    crossing.total(e_)
    moves.start(total, summed)
    crossing.core_sent(c)
    crossing.core_sent(e_)
    crossing.finish()
    for step in (1, 2, 3):
        do_copy(step).wait_send()
    for b in range(3):
        for step in (1, 2, 3):
            m = p.peer(step)
            remote(stage.at[b, m], d_rows.at[b, m], s_d.at[b, 0], r_d.at[b, m], (d, m)).wait_recv()
        for i in range(4):

            @pl.when(z == i)
            def _():
                own_copy(b, i).wait()

            @pl.when(z != i)
            def _():
                d_copy(b, i).wait_send()

    moves.rest()


def run_backward(*args):
    vmem = pl.BlockSpec(memory_space=pltpu.VMEM)
    hbm = pl.BlockSpec(memory_space=pl.ANY)
    dma = pltpu.SemaphoreType.DMA
    shape = jax.ShapeDtypeStruct
    return pl.pallas_call(
        backward_kernel,
        out_shape=(shape((3, 4, CHUNK, 768), BF), shape((4, PIECE, 128), BF)),
        in_specs=[pl.BlockSpec(memory_space=pltpu.SMEM)] + [vmem] * 2 + [hbm] * (len(args) - 3),
        out_specs=(hbm, hbm),
        scratch_shapes=[
            pltpu.VMEM((4, CHUNK, CHUNK), BF),
            pltpu.VMEM((3, 1024, CHUNK), BF),
            pltpu.VMEM((3, 3, 1024, CHUNK), BF),
            pltpu.VMEM((3, 1024, CHUNK), BF),
            pltpu.VMEM((3, 1024, 128), F32),
            pltpu.VMEM((3, 4, CHUNK, CHUNK), BF),
            pltpu.VMEM((768, 1024), BF),
            pltpu.VMEM((768, 1024), BF),
            pltpu.VMEM((3, CHUNK, 1024), BF),
            pltpu.VMEM((2, 3, 768, FFC), BF),
            pltpu.VMEM((2, 8, PIECE, 128), BF),
            pltpu.VMEM((4, PIECE, 128), BF),
            pltpu.VMEM((1024, CHUNK), F32),
            pltpu.VMEM((1024, CHUNK), F32),
            pltpu.VMEM((3, 4, CHUNK, 768), BF),
            dma((3,)),
            dma((4,)),
            dma((3, 4)),
            dma((3, 4)),
            dma((2,)),
            dma((32,)),
        ]
        + crossing_scratch(PIECE, 128),
        compiler_params=pltpu.CompilerParams(
            collective_id=2, has_side_effects=True, vmem_limit_bytes=63 * 2**20
        ),
        cost_estimate=pl.CostEstimate(flops=4 * 10**10, bytes_accessed=4 * 10**7, transcendentals=8 * 10**6),
        name="attend_back",
    )(*args)


def finish_kernel(
    gain_part, tok_in, mid_in, d_rows_in, a1t_in, f1_in, summed,
    grad_tokens, grad_first, dw1, dw2, gain_sum,
    tok, mid, d_rows, a1_t, f1, grad, first, part, acc, total1, total2, gbuf, *rest,
):
    p = Place()
    rest = list(rest)
    cross = Crossing(p, lambda m, e: part.at[m, e], rest[:4], rest[4:12], total1, 16)
    chain1 = Chain(p, total1, rest[12:14], rest[14:18], dw1, 16)
    chain2 = Chain(p, total2, rest[18:20], rest[20:24], dw2, 592)
    s_gain, r_gain, move_sems = rest[24:27]
    moves = Moves(move_sems)
    got_total = moves.start(summed, total2)
    got_d = [moves.start(d_rows_in, d_rows), moves.start(a1t_in, a1_t)]
    got_f1 = moves.start(f1_in, f1)
    got_x = [moves.start(tok_in, tok), moves.start(mid_in, mid)]
    p.greet()

    def weight_grad(m):
        cols = jnp.concatenate([d_rows[b, m] for b in range(3)], axis=0)

        def rows(k, carry):
            at = pl.ds(pl.multiple_of(k * CHUNK, CHUNK), CHUNK)
            part[m, pl.ds(2 * k, 2)] = dot(a1_t[at, :], cols).astype(BF).reshape(2, 128, 768)
            return carry

        lax.fori_loop(0, 4, rows, 0)

    def input_grad(m):
        cols = jnp.concatenate([d_rows[b, m] for b in range(3)], axis=0)

        def tile(k, carry):
            w = jnp.concatenate(
                [f1[m, pl.ds(2 * k, 2), i * 128 : (i + 1) * 128, :].reshape(CHUNK, CHUNK) for i in range(3)],
                axis=1,
            )
            at = pl.ds(pl.multiple_of(k * CHUNK, CHUNK), CHUNK)
            y = dot_nt(cols, w)
            if m == 0:
                acc[:, at] = y
            else:
                acc[:, at] += y
            return carry

        lax.fori_loop(0, 4, tile, 0)

    def leave(b, total):
        x = tok[b].astype(F32)
        factor = lax.rsqrt(jnp.mean(x * x, axis=1, keepdims=True) + EPSILON)
        n1 = x * factor
        da1 = acc[pl.ds(pl.multiple_of(b * CHUNK, CHUNK), CHUNK), :]
        total = total + jnp.sum(da1 * n1, axis=0, keepdims=True)
        gain = jnp.concatenate([f1[0, e, 384:400, 0:128].astype(F32)[0:1] for e in range(8)], axis=1)
        dn1 = da1 * gain
        grad[b] = mid[b] + factor * (dn1 - n1 * jnp.mean(dn1 * n1, axis=1, keepdims=True))
        for m in range(4):
            first[b, :, m * CHUNK : (m + 1) * CHUNK] = d_rows[b, m, :, 512:768].astype(F32)
        return total

    def gain_copy(i, device):
        return remote(gbuf.at[0] if i == 0 else gbuf.at[4 + i], gbuf.at[1 + i], s_gain.at[i], r_gain.at[i], device)

    a, b, c, e = ORDER
    moves.wait(got_total)
    chain2.level(0)
    for i in got_d:
        moves.wait(i)
    for m in ORDER:
        weight_grad(m)
        cross.begin(m)
    cross.join(a)
    cross.join(b)
    cross.join(c)
    cross.join(e)
    chain2.level(1)
    cross.relay(a)
    cross.relay(b)
    moves.wait(got_f1)
    input_grad(0)
    cross.relay(c)
    cross.relay(e)
    input_grad(1)
    cross.total(a)
    cross.total(b)
    input_grad(2)
    chain2.level(2)
    input_grad(3)
    cross.total(c)
    cross.total(e)
    chain1.level(0)
    for i in got_x:
        moves.wait(i)
    total = lax.fori_loop(0, 3, leave, jnp.zeros((1, 1024), F32))
    moves.start(grad, grad_tokens)
    moves.start(first, grad_first)
    row = lax.broadcasted_iota(jnp.int32, (8, 1024), 0)
    gbuf[0] = jnp.where(row == 0, total, gain_part[...])
    gain_copy(0, p.core).start()
    chain1.level(1)
    gain_copy(0, p.core).wait_recv()
    gbuf[5] = gbuf[0] + gbuf[1]
    gain_copy(1, p.x).start()
    chain2.last()
    gain_copy(1, p.x).wait_recv()
    gbuf[6] = gbuf[5] + gbuf[2]
    gain_copy(2, p.y).start()
    chain1.level(2)
    gain_copy(2, p.y).wait_recv()
    gbuf[7] = gbuf[6] + gbuf[3]
    for step in (1, 2, 3):
        m = p.peer(step)
        remote(gbuf.at[7], gbuf.at[8 + p.z], s_gain.at[2 + step], r_gain.at[3 + p.z], (p.d, m)).start()
    gbuf[8 + p.z] = gbuf[7]
    chain1.last()
    for step in (1, 2, 3):
        m = p.peer(step)
        remote(gbuf.at[7], gbuf.at[8 + m], s_gain.at[2 + step], r_gain.at[3 + m], (p.d, m)).wait_recv()
    gain_sum[...] = (gbuf[8] + gbuf[9]) + (gbuf[10] + gbuf[11])
    for i, device in enumerate((p.core, p.x, p.y)):
        gain_copy(i, device).wait_send()
    for step in (1, 2, 3):
        m = p.peer(step)
        remote(gbuf.at[7], gbuf.at[8 + m], s_gain.at[2 + step], r_gain.at[3 + m], (p.d, m)).wait_send()
    for m in range(4):
        cross.core_sent(m)
    cross.finish()
    chain1.finish()
    chain2.finish()
    moves.rest()


def run_finish(*args):
    vmem = pl.BlockSpec(memory_space=pltpu.VMEM)
    hbm = pl.BlockSpec(memory_space=pl.ANY)
    dma = pltpu.SemaphoreType.DMA
    shape = jax.ShapeDtypeStruct
    return pl.pallas_call(
        finish_kernel,
        out_shape=(
            shape((3, CHUNK, 1024), F32),
            shape((3, CHUNK, 1024), F32),
            shape((128, 768), F32),
            shape((PIECE, 128), F32),
            shape((8, 1024), F32),
        ),
        in_specs=[vmem] + [hbm] * (len(args) - 1),
        out_specs=(hbm, hbm, vmem, vmem, vmem),
        scratch_shapes=[
            pltpu.VMEM((3, CHUNK, 1024), BF),
            pltpu.VMEM((3, CHUNK, 1024), F32),
            pltpu.VMEM((3, 4, CHUNK, 768), BF),
            pltpu.VMEM((1024, 768), BF),
            pltpu.VMEM((4, 8, QROWS, CHUNK), BF),
            pltpu.VMEM((3, CHUNK, 1024), F32),
            pltpu.VMEM((3, CHUNK, 1024), F32),
            pltpu.VMEM((4, 8, 128, 768), BF),
            pltpu.VMEM((768, 1024), F32),
            pltpu.VMEM((4, 128, 768), BF),
            pltpu.VMEM((4, PIECE, 128), BF),
            pltpu.VMEM((12, 8, 1024), F32),
        ]
        + crossing_scratch(128, 768)
        + chain_scratch(128, 768)
        + chain_scratch(PIECE, 128)
        + [dma((6,)), dma((7,)), dma((8,))],
        compiler_params=pltpu.CompilerParams(
            collective_id=3, has_side_effects=True, vmem_limit_bytes=62 * 2**20
        ),
        cost_estimate=pl.CostEstimate(flops=10**10, bytes_accessed=5 * 10**7, transcendentals=0),
        name="sum_grads",
    )(*args)


def fast_body(
    tokens, first_values, sequences, w_query, w_key, w_value, w_out, w_gate, w_up, w_down,
    gain_attn, gain_mlp, cotangent,
):
    seq = sequences[:, 0]
    cos_t, sin_t = rope_tables()
    (_, acts, f1, qkv, o_head, lse, o_rows, a1_t, a2, dattn, mid, layer_out, do_head, do_last, gain_part) = run_forward(
        seq, w_query, w_key, w_value, w_out, w_gate.T, w_up.T, w_down.T,
        gain_attn[None, :], gain_mlp[None, :], cos_t, sin_t, tokens, first_values, cotangent,
    )
    d_rows, summed = run_backward(
        seq, cos_t, sin_t, do_last, do_head, qkv, o_head, lse, o_rows, a2, dattn, cotangent, acts
    )
    grad_tokens, grad_first, dw1, dw2, gain_sum = run_finish(gain_part, tokens, mid, d_rows, a1_t, f1, summed)
    place = (lax.axis_index("dp") * 4 + lax.axis_index("mp")) * 32
    gain_mine = lax.dynamic_slice(gain_sum, (0, place), (2, 32))
    return (
        layer_out,
        grad_tokens,
        grad_first,
        dw1[:, 0:256],
        dw1[:, 256:512],
        dw1[:, 512:768],
        dw2[3 * FFC :].T,
        dw2[0:FFC].T,
        dw2[FFC : 2 * FFC].T,
        dw2[2 * FFC : 3 * FFC].T,
        gain_mine[0],
        gain_mine[1],
    )


def is_small(mesh):
    return mesh.axis_names == ("dp", "mp") and tuple(mesh.devices.shape) == (8, 4)


def solution(mesh):
    return jax.shard_map(
        fast_body if is_small(mesh) else body,
        mesh=mesh,
        in_specs=(
            P(None, ("dp", "mp"), None),
            P(None, ("dp", "mp"), None),
            P(None, "dp"),
            P("dp", "mp"),
            P("dp", "mp"),
            P("dp", "mp"),
            P("dp", "mp"),
            P("dp", "mp"),
            P("dp", "mp"),
            P("dp", "mp"),
            P("dp"),
            P("dp"),
            P(None, ("dp", "mp"), None),
        ),
        out_specs=(
            P(None, ("dp", "mp"), None),
            P(None, ("dp", "mp"), None),
            P(None, ("dp", "mp"), None),
            P("dp", "mp"),
            P("dp", "mp"),
            P("dp", "mp"),
            P("dp", "mp"),
            P("dp", "mp"),
            P("dp", "mp"),
            P("dp", "mp"),
            P(("dp", "mp")),
            P(("dp", "mp")),
        ),
        check_vma=False,
    )
```

```python
import jax
import jax.numpy as jnp
import numpy as np
from jax import lax
from jax.experimental import pallas as pl
from jax.experimental.pallas import tpu as pltpu
from jax.sharding import PartitionSpec as P

HEAD_DIM = 64


EPSILON = 1e-06
THETA = 10000.0


def normalize(rows):
    factor = lax.rsqrt(jnp.mean(rows * rows, axis=-1, keepdims=True) + EPSILON)
    return (rows * factor, factor)


def norm_back(grad_normed, normed, factor):
    return factor * (grad_normed - normed * jnp.mean(grad_normed * normed, axis=-1, keepdims=True))


def rotary_tables(position, head_size):
    halfway = head_size // 2
    inverse = THETA ** (-2.0 * jnp.arange(halfway, dtype=jnp.float32) / head_size)
    angles = position.astype(jnp.float32)[:, None] * inverse[None, :]
    return (jnp.cos(angles), jnp.sin(angles))


def rotate(values, cosine, sine, direction):
    halfway = values.shape[-1] // 2
    former = values[..., :halfway]
    latter = values[..., halfway:]
    cos_rows = cosine[:, None, :]
    sin_rows = direction * sine[:, None, :]
    return jnp.concatenate(
        [former * cos_rows - latter * sin_rows, latter * cos_rows + former * sin_rows], axis=-1
    )


def layout(packed, length):
    index_rows = jnp.arange(length, dtype=jnp.int32)
    second = jnp.where((packed == 2) & (index_rows >= length // 2), 1, 0).astype(jnp.int32)
    return (second, index_rows - second * (length // 2))


def block_scores(query, key_rows, second, offset, block_rows, key_end, scale):
    raw = (
        jnp.einsum(
            "qhd,khd->hqk",
            query[offset : offset + block_rows],
            key_rows,
            preferred_element_type=jnp.float32,
        )
        * scale
    )
    row_ids = offset + jnp.arange(block_rows, dtype=jnp.int32)
    col_ids = jnp.arange(key_end, dtype=jnp.int32)
    allowed = (col_ids[None, :] <= row_ids[:, None]) & (
        second[offset : offset + block_rows][:, None] == second[None, :]
    )
    return jnp.where(allowed[None], raw, -1e30)


def whole_rows(part):
    return lax.all_gather(part, "mp", axis=0, tiled=True)


def summed_rows(term, local_rows):
    return lax.psum_scatter(
        term(jnp.int32(0), local_rows * lax.axis_size("mp")).astype(jnp.bfloat16),
        "mp",
        scatter_dimension=0,
        tiled=True,
    ).astype(jnp.float32)


def fetch(w_query, w_key, w_value, w_out, w_gate, w_up, w_down, gain_attn, gain_mlp):
    return (
        lax.all_gather(w_query, "dp", axis=0, tiled=True),
        lax.all_gather(w_key, "dp", axis=0, tiled=True),
        lax.all_gather(w_value, "dp", axis=0, tiled=True),
        lax.all_gather(w_out, "dp", axis=0, tiled=True),
        lax.all_gather(w_gate, "dp", axis=0, tiled=True),
        lax.all_gather(w_up, "dp", axis=0, tiled=True),
        lax.all_gather(w_down, "dp", axis=0, tiled=True),
        lax.all_gather(gain_attn, "dp", axis=0, tiled=True),
        lax.all_gather(gain_mlp, "dp", axis=0, tiled=True),
    )


def project_back(left, right):
    return jnp.einsum("rc,dc->rd", left, right, preferred_element_type=jnp.float32)


def outer_sum(left, right):
    return jnp.einsum("td,tc->dc", left, right, preferred_element_type=jnp.float32)


def body(
    tokens,
    first_values,
    sequences,
    w_query,
    w_key,
    w_value,
    w_out,
    w_gate,
    w_up,
    w_down,
    gain_attn,
    gain_mlp,
    cotangent,
):
    micro = tokens.shape[0]
    local_rows = tokens.shape[1]
    length = local_rows * lax.axis_size("mp")
    heads_here = w_query.shape[1] // HEAD_DIM
    block_rows = min(512, length)
    scale = HEAD_DIM ** (-0.5)
    saved = []
    outputs = []
    for batch in range(micro):
        full = fetch(w_query, w_key, w_value, w_out, w_gate, w_up, w_down, gain_attn, gain_mlp)
        q_full, k_full, v_full, o_full, gate_full, up_full, down_full, gain_one, gain_two = full
        gain_one = gain_one.astype(jnp.float32)
        gain_two = gain_two.astype(jnp.float32)
        x_rows = tokens[batch].astype(jnp.float32)
        normed_one, factor_one = normalize(x_rows)
        input_one = whole_rows((normed_one * gain_one[None, :]).astype(jnp.bfloat16))
        second, position = layout(sequences[batch, 0], length)
        cosine, sine = rotary_tables(position, HEAD_DIM)
        query = jnp.dot(input_one, q_full, preferred_element_type=jnp.float32).reshape(
            length, heads_here, HEAD_DIM
        )
        query = rotate(query, cosine, sine, 1.0).astype(jnp.bfloat16)
        key_rows = jnp.dot(input_one, k_full, preferred_element_type=jnp.float32).reshape(
            length, heads_here, HEAD_DIM
        )
        key_rows = rotate(key_rows, cosine, sine, 1.0).astype(jnp.bfloat16)
        first_here = lax.all_to_all(
            first_values[batch], "mp", split_axis=1, concat_axis=0, tiled=True
        )
        mixed = 0.5 * (
            jnp.dot(input_one, v_full, preferred_element_type=jnp.float32)
            + first_here.astype(jnp.float32)
        )
        mixed = mixed.astype(jnp.bfloat16).reshape(length, heads_here, HEAD_DIM)
        pieces = []
        logsums = []
        for offset in range(0, length, block_rows):
            key_end = length
            scores = block_scores(query, key_rows, second, offset, block_rows, key_end, scale)
            highest = jnp.max(scores, axis=-1, keepdims=True)
            powers = jnp.exp(scores - highest)
            denominator = jnp.sum(powers, axis=-1, keepdims=True)
            probs_low = (powers / denominator).astype(jnp.bfloat16)
            logsums.append(highest + jnp.log(denominator))
            pieces.append(
                jnp.einsum("hqk,khd->qhd", probs_low, mixed, preferred_element_type=jnp.float32)
            )
        attended = (
            jnp.concatenate(pieces, axis=0)
            .reshape(length, heads_here * HEAD_DIM)
            .astype(jnp.bfloat16)
        )

        def attn_term(offset, amount):
            return project_back(attended, o_full)

        mid_rows = x_rows + summed_rows(attn_term, local_rows)
        normed_two, factor_two = normalize(mid_rows)
        input_two = whole_rows((normed_two * gain_two[None, :]).astype(jnp.bfloat16))
        gate = jnp.dot(input_two, gate_full, preferred_element_type=jnp.float32)
        upward = jnp.dot(input_two, up_full, preferred_element_type=jnp.float32)
        sigma = jax.nn.sigmoid(gate)
        hidden = (gate * sigma * upward).astype(jnp.bfloat16)

        def mlp_term(offset, amount):
            return project_back(hidden, down_full)

        mlp_rows = summed_rows(mlp_term, local_rows)
        outputs.append((mid_rows + mlp_rows).astype(jnp.bfloat16))
        saved.append(
            (
                normed_one,
                factor_one,
                input_one,
                second,
                cosine,
                sine,
                query,
                key_rows,
                mixed,
                logsums,
                attended,
                normed_two,
                factor_two,
                input_two,
                gate,
                sigma,
                upward,
                hidden,
            )
        )
    grad_sum = None
    gain_grad_one = jnp.zeros((tokens.shape[2],), jnp.float32)
    gain_grad_two = jnp.zeros((tokens.shape[2],), jnp.float32)
    grad_tokens = []
    grad_first = []
    for batch in range(micro):
        (
            normed_one,
            factor_one,
            input_one,
            second,
            cosine,
            sine,
            query,
            key_rows,
            mixed,
            logsums,
            attended,
            normed_two,
            factor_two,
            input_two,
            gate,
            sigma,
            upward,
            hidden,
        ) = saved[batch]
        full = fetch(w_query, w_key, w_value, w_out, w_gate, w_up, w_down, gain_attn, gain_mlp)
        q_full, k_full, v_full, o_full, gate_full, up_full, down_full, gain_one, gain_two = full
        gain_one = gain_one.astype(jnp.float32)
        gain_two = gain_two.astype(jnp.float32)
        grad_rows = cotangent[batch]
        grad_full = whole_rows(grad_rows)
        grad_down = outer_sum(grad_full, hidden)
        grad_hidden = jnp.dot(grad_full, down_full, preferred_element_type=jnp.float32)
        grad_gate = (grad_hidden * upward * sigma * (1.0 + gate * (1.0 - sigma))).astype(
            jnp.bfloat16
        )
        grad_up = (grad_hidden * gate * sigma).astype(jnp.bfloat16)
        grad_gate_w = outer_sum(input_two, grad_gate)
        grad_up_w = outer_sum(input_two, grad_up)

        def mlp_back(offset, amount):
            return project_back(grad_gate, gate_full) + project_back(grad_up, up_full)

        grad_input_two = summed_rows(mlp_back, local_rows)
        gain_grad_two = gain_grad_two + jnp.sum(grad_input_two * normed_two, axis=0)
        grad_mid = grad_rows.astype(jnp.float32) + norm_back(
            grad_input_two * gain_two[None, :], normed_two, factor_two
        )
        grad_attn = whole_rows(grad_mid.astype(jnp.bfloat16))
        grad_out_w = outer_sum(grad_attn, attended)
        grad_attended = jnp.dot(grad_attn, o_full, preferred_element_type=jnp.float32)
        grad_attended = grad_attended.astype(jnp.bfloat16).reshape(length, heads_here, HEAD_DIM)
        grad_mixed = jnp.zeros((length, heads_here, HEAD_DIM), jnp.float32)
        grad_key = jnp.zeros((length, heads_here, HEAD_DIM), jnp.float32)
        query_parts = []
        for turn, offset in enumerate(range(0, length, block_rows)):
            key_end = length
            scores = block_scores(query, key_rows, second, offset, block_rows, key_end, scale)
            probs = jnp.exp(scores - logsums[turn])
            grad_block = grad_attended[offset : offset + block_rows]
            grad_probs = jnp.einsum(
                "qhd,khd->hqk", grad_block, mixed, preferred_element_type=jnp.float32
            )
            grad_mixed = grad_mixed.at[:key_end].add(
                jnp.einsum(
                    "hqk,qhd->khd",
                    probs.astype(jnp.bfloat16),
                    grad_block,
                    preferred_element_type=jnp.float32,
                )
            )
            grad_scores = probs * (grad_probs - jnp.sum(probs * grad_probs, axis=-1, keepdims=True))
            grad_scores = grad_scores.astype(jnp.bfloat16)
            query_parts.append(
                jnp.einsum(
                    "hqk,khd->qhd", grad_scores, key_rows, preferred_element_type=jnp.float32
                )
                * scale
            )
            grad_key = grad_key.at[:key_end].add(
                jnp.einsum(
                    "hqk,qhd->khd",
                    grad_scores,
                    query[offset : offset + block_rows],
                    preferred_element_type=jnp.float32,
                )
                * scale
            )
        grad_mixed_low = grad_mixed.reshape(length, heads_here * HEAD_DIM).astype(jnp.bfloat16)
        grad_value = (0.5 * grad_mixed_low.astype(jnp.float32)).astype(jnp.bfloat16)
        grad_query = rotate(jnp.concatenate(query_parts, axis=0), cosine, sine, -1.0)
        grad_query = grad_query.reshape(length, heads_here * HEAD_DIM).astype(jnp.bfloat16)
        grad_key_low = (
            rotate(grad_key, cosine, sine, -1.0)
            .reshape(length, heads_here * HEAD_DIM)
            .astype(jnp.bfloat16)
        )
        grad_query_w = outer_sum(input_one, grad_query)
        grad_key_w = outer_sum(input_one, grad_key_low)
        grad_value_w = outer_sum(input_one, grad_value)

        def attn_back(offset, amount):
            return (
                project_back(grad_query, q_full)
                + project_back(grad_key_low, k_full)
                + project_back(grad_value, v_full)
            )

        grad_input_one = summed_rows(attn_back, local_rows)
        gain_grad_one = gain_grad_one + jnp.sum(grad_input_one * normed_one, axis=0)
        grad_tokens.append(
            grad_mid + norm_back(grad_input_one * gain_one[None, :], normed_one, factor_one)
        )
        returned = lax.all_to_all(grad_mixed_low, "mp", split_axis=0, concat_axis=1, tiled=True)
        grad_first.append(0.5 * returned.astype(jnp.float32))
        shared = (
            lax.psum_scatter(
                grad_query_w.astype(jnp.bfloat16), "dp", scatter_dimension=0, tiled=True
            ).astype(jnp.float32),
            lax.psum_scatter(
                grad_key_w.astype(jnp.bfloat16), "dp", scatter_dimension=0, tiled=True
            ).astype(jnp.float32),
            lax.psum_scatter(
                grad_value_w.astype(jnp.bfloat16), "dp", scatter_dimension=0, tiled=True
            ).astype(jnp.float32),
            lax.psum_scatter(
                grad_out_w.astype(jnp.bfloat16), "dp", scatter_dimension=0, tiled=True
            ).astype(jnp.float32),
            lax.psum_scatter(
                grad_gate_w.astype(jnp.bfloat16), "dp", scatter_dimension=0, tiled=True
            ).astype(jnp.float32),
            lax.psum_scatter(
                grad_up_w.astype(jnp.bfloat16), "dp", scatter_dimension=0, tiled=True
            ).astype(jnp.float32),
            lax.psum_scatter(
                grad_down.astype(jnp.bfloat16), "dp", scatter_dimension=0, tiled=True
            ).astype(jnp.float32),
        )
        grad_sum = shared if grad_sum is None else jax.tree.map(jnp.add, grad_sum, shared)
    gain_parts = (
        lax.psum_scatter(gain_grad_one, ("dp", "mp"), scatter_dimension=0, tiled=True),
        lax.psum_scatter(gain_grad_two, ("dp", "mp"), scatter_dimension=0, tiled=True),
    )
    return (
        jnp.stack(outputs),
        jnp.stack(grad_tokens),
        jnp.stack(grad_first),
        grad_sum[0],
        grad_sum[1],
        grad_sum[2],
        grad_sum[3],
        grad_sum[4],
        grad_sum[5],
        grad_sum[6],
        gain_parts[0],
        gain_parts[1],
    )


def rope_tables():
    half = HEAD_DIM // 2
    inverse = (THETA ** (-2.0 * np.arange(half) / HEAD_DIM)).astype(np.float32)
    angles = np.arange(1024, dtype=np.float32)[:, None] * inverse[None, :]
    cosine, sine = np.cos(angles), np.sin(angles)
    return (
        jnp.asarray(np.concatenate([cosine] * 4, axis=1), jnp.float32),
        jnp.asarray(np.concatenate([-sine, sine, -sine, sine], axis=1), jnp.float32),
    )


BF = jnp.bfloat16
F32 = jnp.float32
MESH = pl.DeviceIdType.MESH
CHUNK = 256
FFC = 704
PIECE = 3 * FFC + 256
QROWS = 400


def remote(src, dst, send, recv, device):
    return pltpu.make_async_remote_copy(
        src_ref=src, dst_ref=dst, send_sem=send, recv_sem=recv, device_id=device, device_id_type=MESH
    )


class Place:
    def __init__(self):
        self.d = d = lax.axis_index("dp")
        self.z = z = lax.axis_index("mp")
        core = lax.rem(d, 2)
        along_x = lax.rem(lax.div(d, 2), 2)
        along_y = lax.div(d, 4)
        self.dc = d + 1 - 2 * core
        self.dx = d + 2 - 4 * along_x
        self.dy = d + 4 - 8 * along_y
        self.dxy = self.dx + 4 - 8 * along_y
        self.core = (self.dc, z)
        self.x = (self.dx, z)
        self.y = (self.dy, z)
        self.quads = (d, self.dx, self.dy, self.dxy)
        self.core_quads = tuple(q + 1 - 2 * core for q in self.quads)

    def peer(self, step):
        return lax.rem(self.z + step, 4)

    def greet(self):
        barrier = pltpu.get_barrier_semaphore()
        others = [self.core, self.x, self.y, (self.dxy, self.z)] + [(self.d, self.peer(s)) for s in (1, 2, 3)]
        for other in others:
            pl.semaphore_signal(barrier, inc=1, device_id=other, device_id_type=MESH)
        pl.semaphore_wait(barrier, len(others))

    def hop(self, step, visit):
        for sign in (1, -1):
            m = self.z + sign * step

            @pl.when((m >= 0) & (m <= 3))
            def _():
                visit(m)


class Gather:
    def __init__(self, place, at, own, sems):
        self.p, self.at, self.own = place, at, own
        self.right, self.left, self.sx, self.sy, self.sc, self.arrived = sems

    def send(self, src, m, d, sem, device):
        remote(src, self.at(m, d), sem, self.arrived.at[m, d], device).start()

    def along_z(self, m, src=None):
        p = self.p
        src = self.at(m, p.d) if src is None else src

        @pl.when((m <= p.z) & (p.z < 3))
        def _():
            self.send(src, m, p.d, self.right.at[m], (p.d, p.z + 1))

        @pl.when((m >= p.z) & (p.z > 0))
        def _():
            self.send(src, m, p.d, self.left.at[m], (p.d, p.z - 1))

    def spread(self, m, src=None):
        p = self.p
        src = self.at(m, p.d) if src is None else src
        self.send(src, m, p.d, self.sx.at[m], p.x)
        self.send(src, m, p.d, self.sy.at[m], p.y)
        self.send(src, m, p.d, self.sc.at[m], p.core)

    def take(self, m, d):
        remote(self.at(m, d), self.at(m, d), self.sc.at[0], self.arrived.at[m, d], self.p.core).wait_recv()

    def z_in(self, m):
        self.take(m, self.p.d)
        self.along_z(m)

    def x_in(self, m):
        p = self.p
        self.take(m, p.dx)
        src = self.at(m, p.dx)

        @pl.when(lax.rem(m, 2) == 0)
        def _():
            self.send(src, m, p.dx, self.sy.at[4 + m], p.y)

        self.send(src, m, p.dx, self.sc.at[4 + m], p.core)

    def y_in(self, m):
        p = self.p
        self.take(m, p.dy)
        src = self.at(m, p.dy)

        @pl.when(lax.rem(m, 2) == 1)
        def _():
            self.send(src, m, p.dy, self.sx.at[4 + m], p.x)

        self.send(src, m, p.dy, self.sc.at[8 + m], p.core)

    def diag_in(self, m):
        p = self.p
        self.take(m, p.dxy)
        self.send(self.at(m, p.dxy), m, p.dxy, self.sc.at[12 + m], p.core)

    def core_in(self, m):
        for d in self.p.core_quads:
            self.take(m, d)

    def second(self, m):
        return (self.sx if m % 2 else self.sy).at[4 + m]

    def finish(self):
        p = self.p

        def sent(sem, device):
            remote(self.own, self.own, sem, self.arrived.at[0, 0], device).wait_send()

        for m in range(4):

            @pl.when((m <= p.z) & (p.z < 3))
            def _():
                sent(self.right.at[m], p.core)

            @pl.when((m >= p.z) & (p.z > 0))
            def _():
                sent(self.left.at[m], p.core)

            sent(self.sx.at[m], p.core)
            sent(self.sy.at[m], p.core)
            sent(self.second(m), p.core)
            for q in range(4):
                sent(self.sc.at[4 * q + m], p.core)


class Direct(Gather):
    def spread(self, m, src=None):
        p = self.p
        src = self.at(m, p.d) if src is None else src
        super().spread(m, src)
        self.send(src, m, p.d, self.sx.at[4 + m], (p.dxy, p.z))

    def x_in(self, m):
        self.take(m, self.p.dx)
        self.send(self.at(m, self.p.dx), m, self.p.dx, self.sc.at[4 + m], self.p.core)

    def y_in(self, m):
        self.take(m, self.p.dy)
        self.send(self.at(m, self.p.dy), m, self.p.dy, self.sc.at[8 + m], self.p.core)

    def second(self, m):
        return self.sx.at[4 + m]


def gather_sems():
    dma = pltpu.SemaphoreType.DMA
    return [dma((4,)), dma((4,)), dma((8,)), dma((8,)), dma((16,)), dma((4, 8))]


def lanes(shape, width):
    return lax.div(lax.broadcasted_iota(jnp.int32, shape, 1), width)


def turned(x, cosine, sine):
    first = lax.rem(lanes(x.shape, 32), 2) == 0
    width = x.shape[1]
    other = jnp.where(first, pltpu.roll(x, width - 32, 1), pltpu.roll(x, 32, 1))
    return x * cosine + other * sine


def wide(table):
    return jnp.concatenate([table, table], axis=1)


def dot(a, b):
    return lax.dot_general(a, b, (((1,), (0,)), ((), ())), preferred_element_type=F32)


def dot_nt(a, b):
    return lax.dot_general(a, b, (((1,), (1,)), ((), ())), preferred_element_type=F32)


def dot_tn(a, b):
    return lax.dot_general(a, b, (((0,), (0,)), ((), ())), preferred_element_type=F32)


def tile_scores(q_head, keys, tile, packed):
    n = (tile + 1) * CHUNK
    s = dot_nt(q_head, keys) * 0.125
    rows = lax.broadcasted_iota(jnp.int32, (CHUNK, n), 0) + tile * CHUNK
    cols = lax.broadcasted_iota(jnp.int32, (CHUNK, n), 1)
    allowed = cols <= rows
    if tile >= 2:
        allowed = allowed & ((packed != 2) | (cols >= 2 * CHUNK))
    return jnp.where(allowed, s, -1e30)


ORDER = (3, 0, 1, 2)


def add_rows(dst, terms, step):
    def rows(r, carry):
        at = pl.ds(pl.multiple_of(r * step, step), step)
        total = terms[0][at, :].astype(F32)
        for term in terms[1:]:
            total = total + term[at, :].astype(F32)
        dst[at, :] = total.astype(dst.dtype)
        return carry

    lax.fori_loop(0, dst.shape[0] // step, rows, 0)


def spans(n, step):
    return [(at, min(step, n - at)) for at in range(0, n, step)]


def block(i):
    return pl.ds(pl.multiple_of(i * CHUNK, CHUNK), CHUNK)


class Moves:
    def __init__(self, sems):
        self.sems, self.made = sems, []

    def start(self, src, dst):
        copy = pltpu.make_async_copy(src, dst, self.sems.at[len(self.made)])
        copy.start()
        self.made.append(copy)
        return len(self.made) - 1

    def wait(self, i):
        self.made[i].wait()
        self.made[i] = self.made[i], True

    def rest(self):
        for copy in self.made:
            if not isinstance(copy, tuple):
                copy.wait()


class Crossing:
    def __init__(self, place, part, bufs, sems, out, step):
        self.p, self.part, self.out, self.step = place, part, out, step
        self.acc, self.corner, self.bx, self.by = bufs
        (self.s_core, self.r_core, self.s_corner, self.r_corner,
         self.s_x, self.r_x, self.s_y, self.r_y) = sems

    def core_copy(self, m, q):
        p = self.p
        return remote(
            self.part(m, p.core_quads[q]), self.acc.at[m, q],
            self.s_core.at[m, q], self.r_core.at[m, q], p.core,
        )

    def begin(self, m):
        for q in (3, 1, 2, 0):
            self.core_copy(m, q).start()

    def corner_copy(self, m):
        to = self.p.x if m % 2 == 0 else self.p.y
        return remote(self.acc.at[m, 3], self.corner.at[m], self.s_corner.at[m], self.r_corner.at[m], to)

    def x_copy(self, m):
        return remote(self.acc.at[m, 1], self.bx.at[m], self.s_x.at[m], self.r_x.at[m], self.p.x)

    def y_copy(self, m):
        return remote(self.acc.at[m, 2], self.by.at[m], self.s_y.at[m], self.r_y.at[m], self.p.y)

    def join(self, m):
        first = 1 if m % 2 == 0 else 2
        for q in (3, first, 3 - first, 0):
            self.core_copy(m, q).wait_recv()
            add_rows(self.acc.at[m, q], [self.acc.at[m, q], self.part(m, self.p.quads[q])], self.step)
            if q == 3:
                self.corner_copy(m).start()
            if q == first:
                (self.x_copy if m % 2 == 0 else self.y_copy)(m).start()

    def relay(self, m):
        q = 2 if m % 2 == 0 else 1
        self.corner_copy(m).wait_recv()
        add_rows(self.acc.at[m, q], [self.acc.at[m, q], self.corner.at[m]], self.step)
        (self.y_copy if m % 2 == 0 else self.x_copy)(m).start()

    def total(self, m):
        self.x_copy(m).wait_recv()
        self.y_copy(m).wait_recv()
        add_rows(self.out.at[m], [self.acc.at[m, 0], self.bx.at[m], self.by.at[m]], self.step)

    def core_sent(self, m):
        for q in range(4):
            self.core_copy(m, q).wait_send()

    def finish(self):
        for m in range(4):
            self.corner_copy(m).wait_send()
            self.x_copy(m).wait_send()
            self.y_copy(m).wait_send()


def crossing_scratch(rows, width):
    def buf(*lead):
        return pltpu.VMEM((*lead, rows, width), BF)

    dma = pltpu.SemaphoreType.DMA
    return [buf(4, 4), buf(4), buf(4), buf(4), dma((4, 4)), dma((4, 4))] + [dma((4,))] * 6


class Chain:
    def __init__(self, place, part, bufs, sems, out, step):
        self.p, self.part, self.out, self.step = place, part, out, step
        self.br, self.bl = bufs
        self.s_r, self.r_r, self.s_l, self.r_l = sems

    def r_copy(self, m):
        p = self.p
        return remote(self.part.at[m], self.br.at[m], self.s_r.at[m], self.r_r.at[m], (p.d, p.z + 1))

    def l_copy(self, m):
        p = self.p
        return remote(self.part.at[m], self.bl.at[m], self.s_l.at[m], self.r_l.at[m], (p.d, p.z - 1))

    def level(self, k):
        @pl.when(self.p.z == k)
        def _():
            for m in range(3, k, -1):
                if k > 0:
                    self.r_copy(m).wait_recv()
                    add_rows(self.part.at[m], [self.part.at[m], self.br.at[m]], self.step)
                self.r_copy(m).start()

        @pl.when(self.p.z == 3 - k)
        def _():
            for m in range(0, 3 - k):
                if k > 0:
                    self.l_copy(m).wait_recv()
                    add_rows(self.part.at[m], [self.part.at[m], self.bl.at[m]], self.step)
                self.l_copy(m).start()

    def last(self):
        for m in range(4):

            @pl.when(self.p.z == m)
            def _():
                terms = [self.part.at[m]]
                if m > 0:
                    self.r_copy(m).wait_recv()
                    terms.append(self.br.at[m])
                if m < 3:
                    self.l_copy(m).wait_recv()
                    terms.append(self.bl.at[m])
                add_rows(self.out, terms, self.step)

    def finish(self):
        for m in range(4):
            if m > 0:

                @pl.when(self.p.z < m)
                def _():
                    self.r_copy(m).wait_send()

            if m < 3:

                @pl.when(self.p.z > m)
                def _():
                    self.l_copy(m).wait_send()


def chain_scratch(rows, width):
    dma = pltpu.SemaphoreType.DMA
    return [pltpu.VMEM((4, rows, width), BF)] * 2 + [dma((4,))] * 4


def forward_kernel(
    seq, wq, wk, wv, wo_own, wg_t, wu_t, wd_t, gain_attn, gain_mlp, cos_t, sin_t, tok_in, fv_in, cot_in,
    f2, acts, f1_out, qkv_out, o_out, lse_out, rows_out, a1t_out, a2_out, dattn_out, mid_out, layer_out, do_out, do_last, gain_part,
    tok, fv, cot, f1, qkv, o_head, lse, o_rows, a1_t, a1, stage, p2, w, wo, a2, mid, y_out, acc, back, act, dattn, do_rows, do_head, *sems,
):
    p = Place()
    sems = list(sems)
    g1s, g2s = sems[:6], sems[6:12]
    s_qkv, r_qkv, s_o, r_o, s_local, s_do, r_do, w_sems, wo_sems, act_sems, move_sems = sems[12:]
    moves = Moves(move_sems)
    z, d = p.z, p.d
    got_tok = moves.start(tok_in, tok)
    got_fv = moves.start(fv_in, fv)
    got_cot = moves.start(cot_in, cot)
    p.greet()

    f1[z, d, 0:128] = wq[...]
    f1[z, d, 128:256] = wk[...]
    f1[z, d, 256:384] = wv[...]
    f1[z, d, 384:400, 0:128] = jnp.broadcast_to(gain_attn[...], (16, 128))
    f1[z, d, 384:400, 128:256] = jnp.broadcast_to(gain_mlp[...], (16, 128))
    g1 = Gather(p, lambda m, e: f1.at[m, e], f1.at[0, 0], g1s)
    g2 = Direct(p, lambda m, e: f2.at[m, e], p2, g2s)
    g1.along_z(z)
    g1.spread(z)
    for i, source in enumerate((wg_t, wu_t, wd_t)):
        p2[i * FFC : (i + 1) * FFC, :] = source[...]
    p2[3 * FFC :, :] = wo_own[...].T
    own_copy = pltpu.make_async_copy(p2, f2.at[z, d], s_local)
    own_copy.start()

    def arrive(g):
        def visit(m):
            g.z_in(m)
            g.spread(m)
        return visit

    def side(g):
        def visit(m):
            g.x_in(m)
            g.y_in(m)
        return visit

    p.hop(1, arrive(g1))
    side(g1)(z)
    p.hop(2, arrive(g1))
    g2.along_z(z, p2)
    p.hop(1, side(g1))
    g1.diag_in(z)
    p.hop(3, arrive(g1))
    g1.core_in(z)

    gain_row = jnp.concatenate([f1[z, e, 384:400, :].astype(F32)[0:8] for e in range(8)], axis=1)
    gain_two = jnp.concatenate([gain_row[0:1, e * 256 + 128 : e * 256 + 256] for e in range(8)], axis=1)
    moves.wait(got_tok)

    def norm_body(b, carry):
        x = tok[b].astype(F32)
        factor = lax.rsqrt(jnp.mean(x * x, axis=1, keepdims=True) + EPSILON)
        for e in range(8):
            cols = slice(e * 128, (e + 1) * 128)
            a1[pl.ds(pl.multiple_of(b * CHUNK, CHUNK), CHUNK), cols] = (
                x[:, cols] * factor * gain_row[0:1, e * 256 : e * 256 + 128]
            ).astype(BF)
        return carry

    lax.fori_loop(0, 3, norm_body, 0)

    p.hop(2, side(g1))
    p.hop(1, g1.diag_in)
    p.hop(3, side(g1))
    p.hop(2, g1.diag_in)
    p.hop(1, g2.z_in)
    p.hop(1, g1.core_in)
    p.hop(3, g1.diag_in)
    p.hop(2, g1.core_in)
    p.hop(3, g1.core_in)
    g2.spread(z, p2)
    p.hop(1, g2.spread)
    moves.start(f1, f1_out)
    moves.wait(got_fv)

    def project(b):
        pos_full = pl.ds(pl.multiple_of(z * CHUNK, CHUNK), CHUNK)
        low = jnp.where(z >= 2, z - 2, z)
        pos_half = pl.ds(pl.multiple_of(low * CHUNK, CHUNK), CHUNK)
        second = seq[b] == 2
        cosine = wide(jnp.where(second, cos_t[pos_half, :], cos_t[pos_full, :]))
        sine = wide(jnp.where(second, sin_t[pos_half, :], sin_t[pos_full, :]))
        rows = a1[b * CHUNK : (b + 1) * CHUNK, :]

        def one(step, carry):
            m = lax.rem(z + step, 4)
            w = lambda i: f1[m, :, i * 128 : (i + 1) * 128, :].reshape(1024, CHUNK)
            stage[b, m, 0] = turned(dot(rows, w(0)), cosine, sine).astype(BF)
            stage[b, m, 1] = turned(dot(rows, w(1)), cosine, sine).astype(BF)
            first = fv[b, :, pl.ds(pl.multiple_of(m * CHUNK, CHUNK), CHUNK)].astype(F32)
            stage[b, m, 2] = (0.5 * (dot(rows, w(2)) + first)).astype(BF)
            return carry

        lax.fori_loop(0, 4, one, 0)
        for i in range(3):
            qkv[b, i, block(z), :] = stage[b, z, i]

    def qkv_copy(b, step):
        m = p.peer(step)
        dst = qkv.at[b, :, pl.ds(pl.multiple_of(z * CHUNK, CHUNK), CHUNK), :]
        return remote(stage.at[b, m], dst, s_qkv.at[b, step - 1], r_qkv.at[b, z], (d, m))

    def send_qkv(b):
        for step in (1, 2, 3):
            qkv_copy(b, step).start()

    def sent_qkv(b):
        for step in (1, 2, 3):
            qkv_copy(b, step).wait_send()

    def take_qkv(b):
        for step in (1, 2, 3):
            m = p.peer(step)
            dst = qkv.at[b, :, pl.ds(pl.multiple_of(m * CHUNK, CHUNK), CHUNK), :]
            remote(stage.at[b, m], dst, s_qkv.at[b, 0], r_qkv.at[b, m], (d, m)).wait_recv()

    def o_copy(b, i):
        rows = slice(i * CHUNK, (i + 1) * CHUNK)
        return remote(o_head.at[b, rows, :], o_rows.at[b, z], s_o.at[b, i], r_o.at[b, z], (d, i))

    def attend(b, i):
        n = (i + 1) * CHUNK
        rows = slice(i * CHUNK, n)
        packed = seq[b]
        q = qkv[b, 0, rows, :]
        keys = qkv[b, 1, 0:n, :]
        values = qkv[b, 2, 0:n, :]
        head_of = lanes((CHUNK, CHUNK), 64)
        lane = lax.broadcasted_iota(jnp.int32, (CHUNK, 128), 1)

        def head(h, carry):
            out, stats = carry
            s = tile_scores(jnp.where(head_of == h, q, jnp.zeros_like(q)), keys, i, packed)
            top = jnp.max(s, axis=1, keepdims=True)
            e = jnp.exp(s - top)
            total = jnp.sum(e, axis=1, keepdims=True)
            part = dot(e.astype(BF), values) * (1.0 / total)
            return (
                jnp.where(head_of == h, part, out),
                jnp.where(lane == h, top + jnp.log(total), stats),
            )

        out, stats = lax.fori_loop(
            0, 4, head, (jnp.zeros((CHUNK, CHUNK), F32), jnp.zeros((CHUNK, 128), F32))
        )
        o_head[b, rows, :] = out.astype(BF)
        lse[b, rows, :] = stats

        @pl.when(z == i)
        def _():
            o_rows[b, z] = out.astype(BF)

        @pl.when(z != i)
        def _():
            o_copy(b, i).start()

    def take_o(b):
        for step in (1, 2, 3):
            m = p.peer(step)
            remote(o_rows.at[b, m], o_rows.at[b, m], s_o.at[b, 0], r_o.at[b, m], (d, m)).wait_recv()

    def w_copy(t, e):
        m, slot = lax.rem(t, 4), lax.rem(t, 2)
        return pltpu.make_async_copy(
            f2.at[m, e, 0 : 3 * FFC, :], w.at[slot, :, e * 128 : (e + 1) * 128], w_sems.at[slot, e]
        )

    def wo_copy(m, e):
        return pltpu.make_async_copy(
            f2.at[m, e, 3 * FFC :, :], wo.at[m, :, e * 128 : (e + 1) * 128], wo_sems.at[m, e]
        )

    def act_copy(b, m, slot):
        return pltpu.make_async_copy(
            act.at[slot], acts.at[:, m, b * CHUNK : (b + 1) * CHUNK, :], act_sems.at[slot]
        )

    def load_mlp():
        for m in range(4):
            for e in range(8):
                wo_copy(m, e).start()
        for e in range(8):
            w_copy(0, e).start()
        for m in range(4):
            for e in range(8):
                wo_copy(m, e).wait()

    def do_copy(b, step):
        m = p.peer(step)
        return remote(
            do_rows.at[b, m], do_head.at[b, block(z), :], s_do.at[b, step - 1], r_do.at[b, z], (d, m)
        )

    def send_do(b):
        for step in (1, 2, 3):
            do_copy(b, step).start()
        do_head[b, block(z), :] = do_rows[b, z]

    def mlp_rows(b):
        rows = slice(b * CHUNK, (b + 1) * CHUNK)
        x2 = tok[b].astype(F32)
        for m in range(4):
            x2 = x2 + dot(o_rows[b, m], wo[m])
        factor = lax.rsqrt(jnp.mean(x2 * x2, axis=1, keepdims=True) + EPSILON)
        mid[b] = x2
        a2[rows, :] = (x2 * factor * gain_two).astype(BF)

        def chunk(m, carry):
            t = b * 4 + m
            slot = lax.rem(m, 2)
            for e in range(8):
                w_copy(t, e).wait()

            @pl.when(t < 11)
            def _():
                for e in range(8):
                    w_copy(t + 1, e).start()

            @pl.when(t >= 2)
            def _():
                act_copy(b, m, slot).wait()

            for at, size in spans(FFC, 256):
                cols = slice(at, at + size)
                gate = dot_nt(a2[rows, :], w[slot, at : at + size, :])
                up = dot_nt(a2[rows, :], w[slot, FFC + at : FFC + at + size, :])
                dh = dot_nt(cot[b], w[slot, 2 * FFC + at : 2 * FFC + at + size, :])
                sg = jax.nn.sigmoid(gate)
                silu = gate * sg
                act[slot, 0, :, cols] = (dh * up * (sg + silu * (1.0 - sg))).astype(BF)
                act[slot, 1, :, cols] = (dh * silu).astype(BF)
                act[slot, 2, :, cols] = (silu * up).astype(BF)
            for at, size in spans(1024, 256):
                cols = slice(at, at + size)
                y = dot(act[slot, 2], w[slot, 2 * FFC : 3 * FFC, cols])
                u = dot(act[slot, 0], w[slot, 0:FFC, cols]) + dot(act[slot, 1], w[slot, FFC : 2 * FFC, cols])
                acc[:, cols] = jnp.where(m == 0, y, acc[:, cols] + y)
                back[:, cols] = jnp.where(m == 0, u, back[:, cols] + u)
            act_copy(b, m, slot).start()
            return carry

        lax.fori_loop(0, 4, chunk, 0)
        x2 = mid[b]
        y_out[b] = (x2 + acc[...]).astype(BF)
        factor = lax.rsqrt(jnp.mean(x2 * x2, axis=1, keepdims=True) + EPSILON)
        n2 = x2 * factor
        da2 = back[...]
        sums = jnp.broadcast_to(jnp.sum(da2 * n2, axis=0, keepdims=True), (8, 1024))
        gain_part[...] = sums if b == 0 else gain_part[...] + sums
        dn2 = da2 * gain_two
        grad_mid = cot[b].astype(F32) + factor * (dn2 - n2 * jnp.mean(dn2 * n2, axis=1, keepdims=True))
        mid[b] = grad_mid
        dattn[rows, :] = grad_mid.astype(BF)

        def heads(m, carry):
            do_rows[b, m] = dot_nt(dattn[rows, :], wo[m]).astype(BF)
            return carry

        lax.fori_loop(0, 4, heads, 0)
        moves.start(mid.at[b], mid_out.at[b])
        moves.start(y_out.at[b], layer_out.at[b])

    def attend_all(b):
        for i in range(4):
            attend(b, i)
        moves.start(o_head.at[b], o_out.at[b])
        moves.start(lse.at[b], lse_out.at[b])

    project(0)
    send_qkv(0)
    p.hop(2, arrive(g2))
    project(1)
    project(2)
    a1_t[...] = a1[...].T
    moves.start(a1_t, a1t_out)
    p.hop(3, arrive(g2))
    send_qkv(1)
    take_qkv(0)
    moves.start(qkv.at[0], qkv_out.at[0])
    send_qkv(2)
    attend(0, 0)
    attend(0, 1)
    attend(0, 2)
    attend(0, 3)
    moves.start(o_head.at[0], o_out.at[0])
    moves.start(lse.at[0], lse_out.at[0])
    side(g2)(z)
    p.hop(1, side(g2))
    take_qkv(1)
    moves.start(qkv.at[1], qkv_out.at[1])
    attend(1, 0)
    attend(1, 1)
    g2.diag_in(z)
    attend(1, 2)
    attend(1, 3)
    p.hop(2, side(g2))
    moves.start(o_head.at[1], o_out.at[1])
    moves.start(lse.at[1], lse_out.at[1])
    p.hop(1, g2.diag_in)
    take_qkv(2)
    moves.start(qkv.at[2], qkv_out.at[2])
    attend(2, 0)
    attend(2, 1)
    p.hop(2, g2.diag_in)
    attend(2, 2)
    attend(2, 3)
    p.hop(3, side(g2))
    moves.start(o_head.at[2], o_out.at[2])
    moves.start(lse.at[2], lse_out.at[2])
    p.hop(3, g2.diag_in)
    for m in range(4):
        g2.core_in(m)
    own_copy.wait()
    load_mlp()
    moves.wait(got_cot)
    take_o(0)
    mlp_rows(0)
    send_do(0)
    take_o(1)
    mlp_rows(1)
    send_do(1)
    take_o(2)
    moves.start(o_rows, rows_out)
    mlp_rows(2)
    moves.start(a2, a2_out)
    moves.start(dattn, dattn_out)
    moves.start(do_rows.at[2], do_last)
    for b in range(2):
        for step in (1, 2, 3):
            m = p.peer(step)
            dst = do_head.at[b, block(m), :]
            remote(do_rows.at[b, m], dst, s_do.at[b, 0], r_do.at[b, m], (d, m)).wait_recv()
            do_copy(b, step).wait_send()
        moves.start(do_head.at[b], do_out.at[b])
    act_copy(2, 2, 0).wait()
    act_copy(2, 3, 1).wait()
    sent_qkv(0)
    sent_qkv(1)
    sent_qkv(2)
    for b in range(3):
        for i in range(4):

            @pl.when(z != i)
            def _():
                o_copy(b, i).wait_send()

    g1.finish()
    g2.finish()
    moves.rest()


def run_forward(*args):
    vmem = pl.BlockSpec(memory_space=pltpu.VMEM)
    hbm = pl.BlockSpec(memory_space=pl.ANY)
    dma = pltpu.SemaphoreType.DMA
    shape = jax.ShapeDtypeStruct
    return pl.pallas_call(
        forward_kernel,
        out_shape=(
            shape((4, 8, PIECE, 128), BF),
            shape((3, 4, 768, FFC), BF),
            shape((4, 8, QROWS, CHUNK), BF),
            shape((3, 3, 1024, CHUNK), BF),
            shape((3, 1024, CHUNK), BF),
            shape((3, 1024, 128), F32),
            shape((3, 4, CHUNK, CHUNK), BF),
            shape((1024, 768), BF),
            shape((768, 1024), BF),
            shape((768, 1024), BF),
            shape((3, CHUNK, 1024), F32),
            shape((3, CHUNK, 1024), BF),
            shape((2, 1024, CHUNK), BF),
            shape((4, CHUNK, CHUNK), BF),
            shape((8, 1024), F32),
        ),
        in_specs=[pl.BlockSpec(memory_space=pltpu.SMEM)] + [vmem] * 11 + [hbm] * 3,
        out_specs=(hbm,) * 14 + (vmem,),
        scratch_shapes=[
            pltpu.VMEM((3, CHUNK, 1024), BF),
            pltpu.VMEM((3, CHUNK, 1024), BF),
            pltpu.VMEM((3, CHUNK, 1024), BF),
            pltpu.VMEM((4, 8, QROWS, CHUNK), BF),
            pltpu.VMEM((3, 3, 1024, CHUNK), BF),
            pltpu.VMEM((3, 1024, CHUNK), BF),
            pltpu.VMEM((3, 1024, 128), F32),
            pltpu.VMEM((3, 4, CHUNK, CHUNK), BF),
            pltpu.VMEM((1024, 768), BF),
            pltpu.VMEM((768, 1024), BF),
            pltpu.VMEM((3, 4, 3, CHUNK, CHUNK), BF),
            pltpu.VMEM((PIECE, 128), BF),
            pltpu.VMEM((2, 3 * FFC, 1024), BF),
            pltpu.VMEM((4, CHUNK, 1024), BF),
            pltpu.VMEM((768, 1024), BF),
            pltpu.VMEM((3, CHUNK, 1024), F32),
            pltpu.VMEM((3, CHUNK, 1024), BF),
            pltpu.VMEM((CHUNK, 1024), F32),
            pltpu.VMEM((CHUNK, 1024), F32),
            pltpu.VMEM((2, 3, CHUNK, FFC), BF),
            pltpu.VMEM((768, 1024), BF),
            pltpu.VMEM((3, 4, CHUNK, CHUNK), BF),
            pltpu.VMEM((2, 1024, CHUNK), BF),
        ]
        + gather_sems()
        + gather_sems()
        + [dma((3, 3)), dma((3, 4)), dma((3, 4)), dma((3, 4)), dma, dma((3, 3)), dma((3, 4))]
        + [dma((2, 8)), dma((4, 8)), dma((2,)), dma((32,))],
        compiler_params=pltpu.CompilerParams(
            collective_id=1, has_side_effects=True, vmem_limit_bytes=62 * 2**20
        ),
        cost_estimate=pl.CostEstimate(flops=5 * 10**10, bytes_accessed=6 * 10**7, transcendentals=8 * 10**6),
        name="gather_forward",
    )(*args)


def backward_kernel(
    seq, cos_t, sin_t, do_last, do_in, qkv_in, o_in, lse_in, rows_in, a2_in, dattn_in, cot_in, acts,
    d_rows, summed,
    do_mine, do_head, qkv, o_head, lse, o_rows, a2, dattn, cot, act, part, total, dk, dv, stage, *rest,
):
    p = Place()
    s_do, r_do, s_d, r_d, act_sems, move_sems = rest[:6]
    z, d = p.z, p.d
    moves = Moves(move_sems)
    got = []
    for b in range(3):
        got.append(
            [moves.start(qkv_in.at[b], qkv.at[b]), moves.start(o_in.at[b], o_head.at[b]), moves.start(lse_in.at[b], lse.at[b])]
            + ([moves.start(do_in.at[b], do_head.at[b])] if b < 2 else [])
        )
        if b == 0:
            got_do = moves.start(do_last, do_mine)
            got_w = [
                moves.start(a2_in, a2), moves.start(dattn_in, dattn), moves.start(cot_in, cot),
                moves.start(rows_in, o_rows),
            ]
    p.greet()

    def act_copy(m, slot):
        return pltpu.make_async_copy(acts.at[:, m], act.at[slot], act_sems.at[slot])

    act_copy(ORDER[0], 0).start()
    moves.wait(got_do)

    def do_copy(step):
        m = p.peer(step)
        return remote(do_mine.at[m], do_head.at[2, block(z), :], s_do.at[step - 1], r_do.at[z], (d, m))

    for step in (1, 2, 3):
        do_copy(step).start()
    do_head[2, block(z), :] = do_mine[z]

    def take_do():
        for step in (1, 2, 3):
            m = p.peer(step)
            dst = do_head.at[2, block(m), :]
            remote(do_mine.at[m], dst, s_do.at[0], r_do.at[m], (d, m)).wait_recv()

    def d_copy(b, i):
        return remote(stage.at[b, i], d_rows.at[b, z], s_d.at[b, i], r_d.at[b, z], (d, i))

    def own_copy(b, i):
        return pltpu.make_async_copy(stage.at[b, i], d_rows.at[b, i], s_d.at[b, i])

    def back(b, i):
        n = (i + 1) * CHUNK
        rows = slice(i * CHUNK, n)
        packed = seq[b]
        head_of = lanes((CHUNK, CHUNK), 64)
        lane = lax.broadcasted_iota(jnp.int32, (CHUNK, 128), 1)
        q = qkv[b, 0, rows, :]
        keys = qkv[b, 1, 0:n, :]
        values = qkv[b, 2, 0:n, :]
        grad = do_head[b, rows, :]
        spread = grad.astype(F32) * o_head[b, rows, :].astype(F32)
        stats = lse[b, rows, :]

        def head(h, dq):
            here = head_of == h
            q_h = jnp.where(here, q, jnp.zeros_like(q))
            g_h = jnp.where(here, grad, jnp.zeros_like(grad))
            delta = jnp.sum(jnp.where(here, spread, 0.0), axis=1, keepdims=True)
            level = jnp.sum(jnp.where(lane == h, stats, 0.0), axis=1, keepdims=True)
            prob = jnp.exp(tile_scores(q_h, keys, i, packed) - level)
            dp = dot_nt(g_h, values)
            ds = (prob * (dp - delta)).astype(BF)
            dv_part = dot_tn(prob.astype(BF), g_h)
            dk_part = dot_tn(ds, q_h)
            dv[0:n, :] += dv_part
            dk[0:n, :] += dk_part
            return jnp.where(here, dot(ds, keys), dq)

        dq = lax.fori_loop(0, 4, head, jnp.zeros((CHUNK, CHUNK), F32))
        cosine, sine = cos_t[rows, :], sin_t[rows, :]
        if i >= 2:
            early = slice((i - 2) * CHUNK, (i - 1) * CHUNK)
            cosine = jnp.where(packed == 2, cos_t[early, :], cosine)
            sine = jnp.where(packed == 2, sin_t[early, :], sine)
        cosine, sine = wide(cosine), -wide(sine)
        stage[b, i, :, 0:256] = turned(dq * 0.125, cosine, sine).astype(BF)
        stage[b, i, :, 256:512] = turned(dk[rows, :] * 0.125, cosine, sine).astype(BF)
        stage[b, i, :, 512:768] = (dv[rows, :] * 0.5).astype(BF)

        @pl.when(z == i)
        def _():
            own_copy(b, i).start()

        @pl.when(z != i)
        def _():
            d_copy(b, i).start()

    def back_all(b):
        for i in got[b]:
            moves.wait(i)
        dk[...] = jnp.zeros_like(dk)
        dv[...] = jnp.zeros_like(dv)
        for i in (3, 2, 1, 0):
            back(b, i)

    crossing = Crossing(p, lambda m, e: part.at[ORDER.index(m) % 2, e], rest[6:10], rest[10:], total, 592)

    def weight_grad(k):
        m, slot = ORDER[k], k % 2
        act_copy(m, slot).wait()
        if k < 3:
            act_copy(ORDER[k + 1], 1 - slot).start()
        if k >= 2:
            crossing.core_sent(ORDER[k - 2])

        for i in range(3):
            right = cot[...].reshape(768, 1024) if i == 2 else a2[...]
            for at, size in spans(FFC, 256):
                out = dot_tn(act[slot, i, :, at : at + size], right).astype(BF)
                for e in range(8):
                    part[slot, e, i * FFC + at : i * FFC + at + size, :] = out[:, e * 128 : (e + 1) * 128]
        own = jnp.concatenate([o_rows[b, m] for b in range(3)], axis=0)
        out = dot_tn(own, dattn[...]).astype(BF)
        for e in range(8):
            part[slot, e, 3 * FFC :, :] = out[:, e * 128 : (e + 1) * 128]
        crossing.begin(m)

    a, b_, c, e_ = ORDER
    back_all(0)
    for i in got_w:
        moves.wait(i)
    weight_grad(0)
    weight_grad(1)
    crossing.join(a)
    crossing.join(b_)
    back_all(1)
    weight_grad(2)
    weight_grad(3)
    crossing.relay(a)
    crossing.relay(b_)
    take_do()
    back_all(2)
    crossing.join(c)
    crossing.join(e_)
    crossing.total(a)
    crossing.total(b_)
    crossing.relay(c)
    crossing.relay(e_)
    crossing.total(c)
    crossing.total(e_)
    moves.start(total, summed)
    crossing.core_sent(c)
    crossing.core_sent(e_)
    crossing.finish()
    for step in (1, 2, 3):
        do_copy(step).wait_send()
    for b in range(3):
        for step in (1, 2, 3):
            m = p.peer(step)
            remote(stage.at[b, m], d_rows.at[b, m], s_d.at[b, 0], r_d.at[b, m], (d, m)).wait_recv()
        for i in range(4):

            @pl.when(z == i)
            def _():
                own_copy(b, i).wait()

            @pl.when(z != i)
            def _():
                d_copy(b, i).wait_send()

    moves.rest()


def run_backward(*args):
    vmem = pl.BlockSpec(memory_space=pltpu.VMEM)
    hbm = pl.BlockSpec(memory_space=pl.ANY)
    dma = pltpu.SemaphoreType.DMA
    shape = jax.ShapeDtypeStruct
    return pl.pallas_call(
        backward_kernel,
        out_shape=(shape((3, 4, CHUNK, 768), BF), shape((4, PIECE, 128), BF)),
        in_specs=[pl.BlockSpec(memory_space=pltpu.SMEM)] + [vmem] * 2 + [hbm] * (len(args) - 3),
        out_specs=(hbm, hbm),
        scratch_shapes=[
            pltpu.VMEM((4, CHUNK, CHUNK), BF),
            pltpu.VMEM((3, 1024, CHUNK), BF),
            pltpu.VMEM((3, 3, 1024, CHUNK), BF),
            pltpu.VMEM((3, 1024, CHUNK), BF),
            pltpu.VMEM((3, 1024, 128), F32),
            pltpu.VMEM((3, 4, CHUNK, CHUNK), BF),
            pltpu.VMEM((768, 1024), BF),
            pltpu.VMEM((768, 1024), BF),
            pltpu.VMEM((3, CHUNK, 1024), BF),
            pltpu.VMEM((2, 3, 768, FFC), BF),
            pltpu.VMEM((2, 8, PIECE, 128), BF),
            pltpu.VMEM((4, PIECE, 128), BF),
            pltpu.VMEM((1024, CHUNK), F32),
            pltpu.VMEM((1024, CHUNK), F32),
            pltpu.VMEM((3, 4, CHUNK, 768), BF),
            dma((3,)),
            dma((4,)),
            dma((3, 4)),
            dma((3, 4)),
            dma((2,)),
            dma((32,)),
        ]
        + crossing_scratch(PIECE, 128),
        compiler_params=pltpu.CompilerParams(
            collective_id=2, has_side_effects=True, vmem_limit_bytes=63 * 2**20
        ),
        cost_estimate=pl.CostEstimate(flops=4 * 10**10, bytes_accessed=4 * 10**7, transcendentals=8 * 10**6),
        name="attend_back",
    )(*args)


def finish_kernel(
    gain_part, tok_in, mid_in, d_rows_in, a1t_in, f1_in, summed,
    grad_tokens, grad_first, dw1, dw2, gain_sum,
    tok, mid, d_rows, a1_t, f1, grad, first, part, acc, total1, total2, gbuf, *rest,
):
    p = Place()
    rest = list(rest)
    cross = Crossing(p, lambda m, e: part.at[m, e], rest[:4], rest[4:12], total1, 16)
    chain1 = Chain(p, total1, rest[12:14], rest[14:18], dw1, 16)
    chain2 = Chain(p, total2, rest[18:20], rest[20:24], dw2, 592)
    s_gain, r_gain, move_sems = rest[24:27]
    moves = Moves(move_sems)
    got_total = moves.start(summed, total2)
    got_d = [moves.start(d_rows_in, d_rows), moves.start(a1t_in, a1_t)]
    got_f1 = moves.start(f1_in, f1)
    got_x = [moves.start(tok_in, tok), moves.start(mid_in, mid)]
    p.greet()

    def weight_grad(m):
        cols = jnp.concatenate([d_rows[b, m] for b in range(3)], axis=0)

        def rows(k, carry):
            at = pl.ds(pl.multiple_of(k * CHUNK, CHUNK), CHUNK)
            part[m, pl.ds(2 * k, 2)] = dot(a1_t[at, :], cols).astype(BF).reshape(2, 128, 768)
            return carry

        lax.fori_loop(0, 4, rows, 0)

    def input_grad(m):
        cols = jnp.concatenate([d_rows[b, m] for b in range(3)], axis=0)

        def tile(k, carry):
            w = jnp.concatenate(
                [f1[m, pl.ds(2 * k, 2), i * 128 : (i + 1) * 128, :].reshape(CHUNK, CHUNK) for i in range(3)],
                axis=1,
            )
            at = pl.ds(pl.multiple_of(k * CHUNK, CHUNK), CHUNK)
            y = dot_nt(cols, w)
            if m == 0:
                acc[:, at] = y
            else:
                acc[:, at] += y
            return carry

        lax.fori_loop(0, 4, tile, 0)

    def leave(b, total):
        x = tok[b].astype(F32)
        factor = lax.rsqrt(jnp.mean(x * x, axis=1, keepdims=True) + EPSILON)
        n1 = x * factor
        da1 = acc[pl.ds(pl.multiple_of(b * CHUNK, CHUNK), CHUNK), :]
        total = total + jnp.sum(da1 * n1, axis=0, keepdims=True)
        gain = jnp.concatenate([f1[0, e, 384:400, 0:128].astype(F32)[0:1] for e in range(8)], axis=1)
        dn1 = da1 * gain
        grad[b] = mid[b] + factor * (dn1 - n1 * jnp.mean(dn1 * n1, axis=1, keepdims=True))
        for m in range(4):
            first[b, :, m * CHUNK : (m + 1) * CHUNK] = d_rows[b, m, :, 512:768].astype(F32)
        return total

    def gain_copy(i, device):
        return remote(gbuf.at[0] if i == 0 else gbuf.at[4 + i], gbuf.at[1 + i], s_gain.at[i], r_gain.at[i], device)

    a, b, c, e = ORDER
    moves.wait(got_total)
    chain2.level(0)
    for i in got_d:
        moves.wait(i)
    for m in ORDER:
        weight_grad(m)
        cross.begin(m)
    cross.join(a)
    cross.join(b)
    cross.join(c)
    cross.join(e)
    chain2.level(1)
    cross.relay(a)
    cross.relay(b)
    moves.wait(got_f1)
    input_grad(0)
    cross.relay(c)
    cross.relay(e)
    input_grad(1)
    cross.total(a)
    cross.total(b)
    input_grad(2)
    chain2.level(2)
    input_grad(3)
    cross.total(c)
    cross.total(e)
    chain1.level(0)
    for i in got_x:
        moves.wait(i)
    total = lax.fori_loop(0, 3, leave, jnp.zeros((1, 1024), F32))
    moves.start(grad, grad_tokens)
    moves.start(first, grad_first)
    row = lax.broadcasted_iota(jnp.int32, (8, 1024), 0)
    gbuf[0] = jnp.where(row == 0, total, gain_part[...])
    gain_copy(0, p.core).start()
    chain1.level(1)
    gain_copy(0, p.core).wait_recv()
    gbuf[5] = gbuf[0] + gbuf[1]
    gain_copy(1, p.x).start()
    chain2.last()
    gain_copy(1, p.x).wait_recv()
    gbuf[6] = gbuf[5] + gbuf[2]
    gain_copy(2, p.y).start()
    chain1.level(2)
    gain_copy(2, p.y).wait_recv()
    gbuf[7] = gbuf[6] + gbuf[3]
    for step in (1, 2, 3):
        m = p.peer(step)
        remote(gbuf.at[7], gbuf.at[8 + p.z], s_gain.at[2 + step], r_gain.at[3 + p.z], (p.d, m)).start()
    gbuf[8 + p.z] = gbuf[7]
    chain1.last()
    for step in (1, 2, 3):
        m = p.peer(step)
        remote(gbuf.at[7], gbuf.at[8 + m], s_gain.at[2 + step], r_gain.at[3 + m], (p.d, m)).wait_recv()
    gain_sum[...] = (gbuf[8] + gbuf[9]) + (gbuf[10] + gbuf[11])
    for i, device in enumerate((p.core, p.x, p.y)):
        gain_copy(i, device).wait_send()
    for step in (1, 2, 3):
        m = p.peer(step)
        remote(gbuf.at[7], gbuf.at[8 + m], s_gain.at[2 + step], r_gain.at[3 + m], (p.d, m)).wait_send()
    for m in range(4):
        cross.core_sent(m)
    cross.finish()
    chain1.finish()
    chain2.finish()
    moves.rest()


def run_finish(*args):
    vmem = pl.BlockSpec(memory_space=pltpu.VMEM)
    hbm = pl.BlockSpec(memory_space=pl.ANY)
    dma = pltpu.SemaphoreType.DMA
    shape = jax.ShapeDtypeStruct
    return pl.pallas_call(
        finish_kernel,
        out_shape=(
            shape((3, CHUNK, 1024), F32),
            shape((3, CHUNK, 1024), F32),
            shape((128, 768), F32),
            shape((PIECE, 128), F32),
            shape((8, 1024), F32),
        ),
        in_specs=[vmem] + [hbm] * (len(args) - 1),
        out_specs=(hbm, hbm, vmem, vmem, vmem),
        scratch_shapes=[
            pltpu.VMEM((3, CHUNK, 1024), BF),
            pltpu.VMEM((3, CHUNK, 1024), F32),
            pltpu.VMEM((3, 4, CHUNK, 768), BF),
            pltpu.VMEM((1024, 768), BF),
            pltpu.VMEM((4, 8, QROWS, CHUNK), BF),
            pltpu.VMEM((3, CHUNK, 1024), F32),
            pltpu.VMEM((3, CHUNK, 1024), F32),
            pltpu.VMEM((4, 8, 128, 768), BF),
            pltpu.VMEM((768, 1024), F32),
            pltpu.VMEM((4, 128, 768), BF),
            pltpu.VMEM((4, PIECE, 128), BF),
            pltpu.VMEM((12, 8, 1024), F32),
        ]
        + crossing_scratch(128, 768)
        + chain_scratch(128, 768)
        + chain_scratch(PIECE, 128)
        + [dma((6,)), dma((7,)), dma((8,))],
        compiler_params=pltpu.CompilerParams(
            collective_id=3, has_side_effects=True, vmem_limit_bytes=62 * 2**20
        ),
        cost_estimate=pl.CostEstimate(flops=10**10, bytes_accessed=5 * 10**7, transcendentals=0),
        name="sum_grads",
    )(*args)


def fast_body(
    tokens, first_values, sequences, w_query, w_key, w_value, w_out, w_gate, w_up, w_down,
    gain_attn, gain_mlp, cotangent,
):
    seq = sequences[:, 0]
    cos_t, sin_t = rope_tables()
    (_, acts, f1, qkv, o_head, lse, o_rows, a1_t, a2, dattn, mid, layer_out, do_head, do_last, gain_part) = run_forward(
        seq, w_query, w_key, w_value, w_out, w_gate.T, w_up.T, w_down.T,
        gain_attn[None, :], gain_mlp[None, :], cos_t, sin_t, tokens, first_values, cotangent,
    )
    d_rows, summed = run_backward(
        seq, cos_t, sin_t, do_last, do_head, qkv, o_head, lse, o_rows, a2, dattn, cotangent, acts
    )
    grad_tokens, grad_first, dw1, dw2, gain_sum = run_finish(gain_part, tokens, mid, d_rows, a1_t, f1, summed)
    place = (lax.axis_index("dp") * 4 + lax.axis_index("mp")) * 32
    gain_mine = lax.dynamic_slice(gain_sum, (0, place), (2, 32))
    return (
        layer_out,
        grad_tokens,
        grad_first,
        dw1[:, 0:256],
        dw1[:, 256:512],
        dw1[:, 512:768],
        dw2[3 * FFC :].T,
        dw2[0:FFC].T,
        dw2[FFC : 2 * FFC].T,
        dw2[2 * FFC : 3 * FFC].T,
        gain_mine[0],
        gain_mine[1],
    )


def is_small(mesh):
    return mesh.axis_names == ("dp", "mp") and tuple(mesh.devices.shape) == (8, 4)


def solution(mesh):
    return jax.shard_map(
        fast_body if is_small(mesh) else body,
        mesh=mesh,
        in_specs=(
            P(None, ("dp", "mp"), None),
            P(None, ("dp", "mp"), None),
            P(None, "dp"),
            P("dp", "mp"),
            P("dp", "mp"),
            P("dp", "mp"),
            P("dp", "mp"),
            P("dp", "mp"),
            P("dp", "mp"),
            P("dp", "mp"),
            P("dp"),
            P("dp"),
            P(None, ("dp", "mp"), None),
        ),
        out_specs=(
            P(None, ("dp", "mp"), None),
            P(None, ("dp", "mp"), None),
            P(None, ("dp", "mp"), None),
            P("dp", "mp"),
            P("dp", "mp"),
            P("dp", "mp"),
            P("dp", "mp"),
            P("dp", "mp"),
            P("dp", "mp"),
            P("dp", "mp"),
            P(("dp", "mp")),
            P(("dp", "mp")),
        ),
        check_vma=False,
    )
```

```python
import jax
import jax.numpy as jnp
import numpy as np
from jax import lax
from jax.experimental import pallas as pl
from jax.experimental.pallas import tpu as pltpu
from jax.sharding import PartitionSpec as P

HEAD_DIM = 64


EPSILON = 1e-06
THETA = 10000.0


def normalize(rows):
    factor = lax.rsqrt(jnp.mean(rows * rows, axis=-1, keepdims=True) + EPSILON)
    return (rows * factor, factor)


def norm_back(grad_normed, normed, factor):
    return factor * (grad_normed - normed * jnp.mean(grad_normed * normed, axis=-1, keepdims=True))


def rotary_tables(position, head_size):
    halfway = head_size // 2
    inverse = THETA ** (-2.0 * jnp.arange(halfway, dtype=jnp.float32) / head_size)
    angles = position.astype(jnp.float32)[:, None] * inverse[None, :]
    return (jnp.cos(angles), jnp.sin(angles))


def rotate(values, cosine, sine, direction):
    halfway = values.shape[-1] // 2
    former = values[..., :halfway]
    latter = values[..., halfway:]
    cos_rows = cosine[:, None, :]
    sin_rows = direction * sine[:, None, :]
    return jnp.concatenate(
        [former * cos_rows - latter * sin_rows, latter * cos_rows + former * sin_rows], axis=-1
    )


def layout(packed, length):
    index_rows = jnp.arange(length, dtype=jnp.int32)
    second = jnp.where((packed == 2) & (index_rows >= length // 2), 1, 0).astype(jnp.int32)
    return (second, index_rows - second * (length // 2))


def block_scores(query, key_rows, second, offset, block_rows, key_end, scale):
    raw = (
        jnp.einsum(
            "qhd,khd->hqk",
            query[offset : offset + block_rows],
            key_rows,
            preferred_element_type=jnp.float32,
        )
        * scale
    )
    row_ids = offset + jnp.arange(block_rows, dtype=jnp.int32)
    col_ids = jnp.arange(key_end, dtype=jnp.int32)
    allowed = (col_ids[None, :] <= row_ids[:, None]) & (
        second[offset : offset + block_rows][:, None] == second[None, :]
    )
    return jnp.where(allowed[None], raw, -1e30)


def whole_rows(part):
    return lax.all_gather(part, "mp", axis=0, tiled=True)


def summed_rows(term, local_rows):
    return lax.psum_scatter(
        term(jnp.int32(0), local_rows * lax.axis_size("mp")).astype(jnp.bfloat16),
        "mp",
        scatter_dimension=0,
        tiled=True,
    ).astype(jnp.float32)


def fetch(w_query, w_key, w_value, w_out, w_gate, w_up, w_down, gain_attn, gain_mlp):
    return (
        lax.all_gather(w_query, "dp", axis=0, tiled=True),
        lax.all_gather(w_key, "dp", axis=0, tiled=True),
        lax.all_gather(w_value, "dp", axis=0, tiled=True),
        lax.all_gather(w_out, "dp", axis=0, tiled=True),
        lax.all_gather(w_gate, "dp", axis=0, tiled=True),
        lax.all_gather(w_up, "dp", axis=0, tiled=True),
        lax.all_gather(w_down, "dp", axis=0, tiled=True),
        lax.all_gather(gain_attn, "dp", axis=0, tiled=True),
        lax.all_gather(gain_mlp, "dp", axis=0, tiled=True),
    )


def project_back(left, right):
    return jnp.einsum("rc,dc->rd", left, right, preferred_element_type=jnp.float32)


def outer_sum(left, right):
    return jnp.einsum("td,tc->dc", left, right, preferred_element_type=jnp.float32)


def body(
    tokens,
    first_values,
    sequences,
    w_query,
    w_key,
    w_value,
    w_out,
    w_gate,
    w_up,
    w_down,
    gain_attn,
    gain_mlp,
    cotangent,
):
    micro = tokens.shape[0]
    local_rows = tokens.shape[1]
    length = local_rows * lax.axis_size("mp")
    heads_here = w_query.shape[1] // HEAD_DIM
    block_rows = min(512, length)
    scale = HEAD_DIM ** (-0.5)
    saved = []
    outputs = []
    for batch in range(micro):
        full = fetch(w_query, w_key, w_value, w_out, w_gate, w_up, w_down, gain_attn, gain_mlp)
        q_full, k_full, v_full, o_full, gate_full, up_full, down_full, gain_one, gain_two = full
        gain_one = gain_one.astype(jnp.float32)
        gain_two = gain_two.astype(jnp.float32)
        x_rows = tokens[batch].astype(jnp.float32)
        normed_one, factor_one = normalize(x_rows)
        input_one = whole_rows((normed_one * gain_one[None, :]).astype(jnp.bfloat16))
        second, position = layout(sequences[batch, 0], length)
        cosine, sine = rotary_tables(position, HEAD_DIM)
        query = jnp.dot(input_one, q_full, preferred_element_type=jnp.float32).reshape(
            length, heads_here, HEAD_DIM
        )
        query = rotate(query, cosine, sine, 1.0).astype(jnp.bfloat16)
        key_rows = jnp.dot(input_one, k_full, preferred_element_type=jnp.float32).reshape(
            length, heads_here, HEAD_DIM
        )
        key_rows = rotate(key_rows, cosine, sine, 1.0).astype(jnp.bfloat16)
        first_here = lax.all_to_all(
            first_values[batch], "mp", split_axis=1, concat_axis=0, tiled=True
        )
        mixed = 0.5 * (
            jnp.dot(input_one, v_full, preferred_element_type=jnp.float32)
            + first_here.astype(jnp.float32)
        )
        mixed = mixed.astype(jnp.bfloat16).reshape(length, heads_here, HEAD_DIM)
        pieces = []
        logsums = []
        for offset in range(0, length, block_rows):
            key_end = length
            scores = block_scores(query, key_rows, second, offset, block_rows, key_end, scale)
            highest = jnp.max(scores, axis=-1, keepdims=True)
            powers = jnp.exp(scores - highest)
            denominator = jnp.sum(powers, axis=-1, keepdims=True)
            probs_low = (powers / denominator).astype(jnp.bfloat16)
            logsums.append(highest + jnp.log(denominator))
            pieces.append(
                jnp.einsum("hqk,khd->qhd", probs_low, mixed, preferred_element_type=jnp.float32)
            )
        attended = (
            jnp.concatenate(pieces, axis=0)
            .reshape(length, heads_here * HEAD_DIM)
            .astype(jnp.bfloat16)
        )

        def attn_term(offset, amount):
            return project_back(attended, o_full)

        mid_rows = x_rows + summed_rows(attn_term, local_rows)
        normed_two, factor_two = normalize(mid_rows)
        input_two = whole_rows((normed_two * gain_two[None, :]).astype(jnp.bfloat16))
        gate = jnp.dot(input_two, gate_full, preferred_element_type=jnp.float32)
        upward = jnp.dot(input_two, up_full, preferred_element_type=jnp.float32)
        sigma = jax.nn.sigmoid(gate)
        hidden = (gate * sigma * upward).astype(jnp.bfloat16)

        def mlp_term(offset, amount):
            return project_back(hidden, down_full)

        mlp_rows = summed_rows(mlp_term, local_rows)
        outputs.append((mid_rows + mlp_rows).astype(jnp.bfloat16))
        saved.append(
            (
                normed_one,
                factor_one,
                input_one,
                second,
                cosine,
                sine,
                query,
                key_rows,
                mixed,
                logsums,
                attended,
                normed_two,
                factor_two,
                input_two,
                gate,
                sigma,
                upward,
                hidden,
            )
        )
    grad_sum = None
    gain_grad_one = jnp.zeros((tokens.shape[2],), jnp.float32)
    gain_grad_two = jnp.zeros((tokens.shape[2],), jnp.float32)
    grad_tokens = []
    grad_first = []
    for batch in range(micro):
        (
            normed_one,
            factor_one,
            input_one,
            second,
            cosine,
            sine,
            query,
            key_rows,
            mixed,
            logsums,
            attended,
            normed_two,
            factor_two,
            input_two,
            gate,
            sigma,
            upward,
            hidden,
        ) = saved[batch]
        full = fetch(w_query, w_key, w_value, w_out, w_gate, w_up, w_down, gain_attn, gain_mlp)
        q_full, k_full, v_full, o_full, gate_full, up_full, down_full, gain_one, gain_two = full
        gain_one = gain_one.astype(jnp.float32)
        gain_two = gain_two.astype(jnp.float32)
        grad_rows = cotangent[batch]
        grad_full = whole_rows(grad_rows)
        grad_down = outer_sum(grad_full, hidden)
        grad_hidden = jnp.dot(grad_full, down_full, preferred_element_type=jnp.float32)
        grad_gate = (grad_hidden * upward * sigma * (1.0 + gate * (1.0 - sigma))).astype(
            jnp.bfloat16
        )
        grad_up = (grad_hidden * gate * sigma).astype(jnp.bfloat16)
        grad_gate_w = outer_sum(input_two, grad_gate)
        grad_up_w = outer_sum(input_two, grad_up)

        def mlp_back(offset, amount):
            return project_back(grad_gate, gate_full) + project_back(grad_up, up_full)

        grad_input_two = summed_rows(mlp_back, local_rows)
        gain_grad_two = gain_grad_two + jnp.sum(grad_input_two * normed_two, axis=0)
        grad_mid = grad_rows.astype(jnp.float32) + norm_back(
            grad_input_two * gain_two[None, :], normed_two, factor_two
        )
        grad_attn = whole_rows(grad_mid.astype(jnp.bfloat16))
        grad_out_w = outer_sum(grad_attn, attended)
        grad_attended = jnp.dot(grad_attn, o_full, preferred_element_type=jnp.float32)
        grad_attended = grad_attended.astype(jnp.bfloat16).reshape(length, heads_here, HEAD_DIM)
        grad_mixed = jnp.zeros((length, heads_here, HEAD_DIM), jnp.float32)
        grad_key = jnp.zeros((length, heads_here, HEAD_DIM), jnp.float32)
        query_parts = []
        for turn, offset in enumerate(range(0, length, block_rows)):
            key_end = length
            scores = block_scores(query, key_rows, second, offset, block_rows, key_end, scale)
            probs = jnp.exp(scores - logsums[turn])
            grad_block = grad_attended[offset : offset + block_rows]
            grad_probs = jnp.einsum(
                "qhd,khd->hqk", grad_block, mixed, preferred_element_type=jnp.float32
            )
            grad_mixed = grad_mixed.at[:key_end].add(
                jnp.einsum(
                    "hqk,qhd->khd",
                    probs.astype(jnp.bfloat16),
                    grad_block,
                    preferred_element_type=jnp.float32,
                )
            )
            grad_scores = probs * (grad_probs - jnp.sum(probs * grad_probs, axis=-1, keepdims=True))
            grad_scores = grad_scores.astype(jnp.bfloat16)
            query_parts.append(
                jnp.einsum(
                    "hqk,khd->qhd", grad_scores, key_rows, preferred_element_type=jnp.float32
                )
                * scale
            )
            grad_key = grad_key.at[:key_end].add(
                jnp.einsum(
                    "hqk,qhd->khd",
                    grad_scores,
                    query[offset : offset + block_rows],
                    preferred_element_type=jnp.float32,
                )
                * scale
            )
        grad_mixed_low = grad_mixed.reshape(length, heads_here * HEAD_DIM).astype(jnp.bfloat16)
        grad_value = (0.5 * grad_mixed_low.astype(jnp.float32)).astype(jnp.bfloat16)
        grad_query = rotate(jnp.concatenate(query_parts, axis=0), cosine, sine, -1.0)
        grad_query = grad_query.reshape(length, heads_here * HEAD_DIM).astype(jnp.bfloat16)
        grad_key_low = (
            rotate(grad_key, cosine, sine, -1.0)
            .reshape(length, heads_here * HEAD_DIM)
            .astype(jnp.bfloat16)
        )
        grad_query_w = outer_sum(input_one, grad_query)
        grad_key_w = outer_sum(input_one, grad_key_low)
        grad_value_w = outer_sum(input_one, grad_value)

        def attn_back(offset, amount):
            return (
                project_back(grad_query, q_full)
                + project_back(grad_key_low, k_full)
                + project_back(grad_value, v_full)
            )

        grad_input_one = summed_rows(attn_back, local_rows)
        gain_grad_one = gain_grad_one + jnp.sum(grad_input_one * normed_one, axis=0)
        grad_tokens.append(
            grad_mid + norm_back(grad_input_one * gain_one[None, :], normed_one, factor_one)
        )
        returned = lax.all_to_all(grad_mixed_low, "mp", split_axis=0, concat_axis=1, tiled=True)
        grad_first.append(0.5 * returned.astype(jnp.float32))
        shared = (
            lax.psum_scatter(
                grad_query_w.astype(jnp.bfloat16), "dp", scatter_dimension=0, tiled=True
            ).astype(jnp.float32),
            lax.psum_scatter(
                grad_key_w.astype(jnp.bfloat16), "dp", scatter_dimension=0, tiled=True
            ).astype(jnp.float32),
            lax.psum_scatter(
                grad_value_w.astype(jnp.bfloat16), "dp", scatter_dimension=0, tiled=True
            ).astype(jnp.float32),
            lax.psum_scatter(
                grad_out_w.astype(jnp.bfloat16), "dp", scatter_dimension=0, tiled=True
            ).astype(jnp.float32),
            lax.psum_scatter(
                grad_gate_w.astype(jnp.bfloat16), "dp", scatter_dimension=0, tiled=True
            ).astype(jnp.float32),
            lax.psum_scatter(
                grad_up_w.astype(jnp.bfloat16), "dp", scatter_dimension=0, tiled=True
            ).astype(jnp.float32),
            lax.psum_scatter(
                grad_down.astype(jnp.bfloat16), "dp", scatter_dimension=0, tiled=True
            ).astype(jnp.float32),
        )
        grad_sum = shared if grad_sum is None else jax.tree.map(jnp.add, grad_sum, shared)
    gain_parts = (
        lax.psum_scatter(gain_grad_one, ("dp", "mp"), scatter_dimension=0, tiled=True),
        lax.psum_scatter(gain_grad_two, ("dp", "mp"), scatter_dimension=0, tiled=True),
    )
    return (
        jnp.stack(outputs),
        jnp.stack(grad_tokens),
        jnp.stack(grad_first),
        grad_sum[0],
        grad_sum[1],
        grad_sum[2],
        grad_sum[3],
        grad_sum[4],
        grad_sum[5],
        grad_sum[6],
        gain_parts[0],
        gain_parts[1],
    )


def rope_tables():
    half = HEAD_DIM // 2
    inverse = (THETA ** (-2.0 * np.arange(half) / HEAD_DIM)).astype(np.float32)
    angles = np.arange(1024, dtype=np.float32)[:, None] * inverse[None, :]
    cosine, sine = np.cos(angles), np.sin(angles)
    return (
        jnp.asarray(np.concatenate([cosine] * 4, axis=1), jnp.float32),
        jnp.asarray(np.concatenate([-sine, sine, -sine, sine], axis=1), jnp.float32),
    )


BF = jnp.bfloat16
F32 = jnp.float32
MESH = pl.DeviceIdType.MESH
CHUNK = 256
FFC = 704
PIECE = 3 * FFC + 256
QROWS = 400


def remote(src, dst, send, recv, device):
    return pltpu.make_async_remote_copy(
        src_ref=src, dst_ref=dst, send_sem=send, recv_sem=recv, device_id=device, device_id_type=MESH
    )


class Place:
    def __init__(self):
        self.d = d = lax.axis_index("dp")
        self.z = z = lax.axis_index("mp")
        core = lax.rem(d, 2)
        along_x = lax.rem(lax.div(d, 2), 2)
        along_y = lax.div(d, 4)
        self.dc = d + 1 - 2 * core
        self.dx = d + 2 - 4 * along_x
        self.dy = d + 4 - 8 * along_y
        self.dxy = self.dx + 4 - 8 * along_y
        self.core = (self.dc, z)
        self.x = (self.dx, z)
        self.y = (self.dy, z)
        self.quads = (d, self.dx, self.dy, self.dxy)
        self.core_quads = tuple(q + 1 - 2 * core for q in self.quads)

    def peer(self, step):
        return lax.rem(self.z + step, 4)

    def greet(self):
        barrier = pltpu.get_barrier_semaphore()
        others = [self.core, self.x, self.y, (self.dxy, self.z)] + [(self.d, self.peer(s)) for s in (1, 2, 3)]
        for other in others:
            pl.semaphore_signal(barrier, inc=1, device_id=other, device_id_type=MESH)
        pl.semaphore_wait(barrier, len(others))

    def hop(self, step, visit):
        for sign in (1, -1):
            m = self.z + sign * step

            @pl.when((m >= 0) & (m <= 3))
            def _():
                visit(m)


class Gather:
    def __init__(self, place, at, own, sems):
        self.p, self.at, self.own = place, at, own
        self.right, self.left, self.sx, self.sy, self.sc, self.arrived = sems

    def send(self, src, m, d, sem, device):
        remote(src, self.at(m, d), sem, self.arrived.at[m, d], device).start()

    def along_z(self, m, src=None):
        p = self.p
        src = self.at(m, p.d) if src is None else src

        @pl.when((m <= p.z) & (p.z < 3))
        def _():
            self.send(src, m, p.d, self.right.at[m], (p.d, p.z + 1))

        @pl.when((m >= p.z) & (p.z > 0))
        def _():
            self.send(src, m, p.d, self.left.at[m], (p.d, p.z - 1))

    def spread(self, m, src=None):
        p = self.p
        src = self.at(m, p.d) if src is None else src
        self.send(src, m, p.d, self.sx.at[m], p.x)
        self.send(src, m, p.d, self.sy.at[m], p.y)
        self.send(src, m, p.d, self.sc.at[m], p.core)

    def take(self, m, d):
        remote(self.at(m, d), self.at(m, d), self.sc.at[0], self.arrived.at[m, d], self.p.core).wait_recv()

    def z_in(self, m):
        self.take(m, self.p.d)
        self.along_z(m)

    def x_in(self, m):
        p = self.p
        self.take(m, p.dx)
        src = self.at(m, p.dx)

        @pl.when(lax.rem(m, 2) == 0)
        def _():
            self.send(src, m, p.dx, self.sy.at[4 + m], p.y)

        self.send(src, m, p.dx, self.sc.at[4 + m], p.core)

    def y_in(self, m):
        p = self.p
        self.take(m, p.dy)
        src = self.at(m, p.dy)

        @pl.when(lax.rem(m, 2) == 1)
        def _():
            self.send(src, m, p.dy, self.sx.at[4 + m], p.x)

        self.send(src, m, p.dy, self.sc.at[8 + m], p.core)

    def diag_in(self, m):
        p = self.p
        self.take(m, p.dxy)
        self.send(self.at(m, p.dxy), m, p.dxy, self.sc.at[12 + m], p.core)

    def core_in(self, m):
        for d in self.p.core_quads:
            self.take(m, d)

    def second(self, m):
        return (self.sx if m % 2 else self.sy).at[4 + m]

    def finish(self):
        p = self.p

        def sent(sem, device):
            remote(self.own, self.own, sem, self.arrived.at[0, 0], device).wait_send()

        for m in range(4):

            @pl.when((m <= p.z) & (p.z < 3))
            def _():
                sent(self.right.at[m], p.core)

            @pl.when((m >= p.z) & (p.z > 0))
            def _():
                sent(self.left.at[m], p.core)

            sent(self.sx.at[m], p.core)
            sent(self.sy.at[m], p.core)
            sent(self.second(m), p.core)
            for q in range(4):
                sent(self.sc.at[4 * q + m], p.core)


class Direct(Gather):
    def spread(self, m, src=None):
        p = self.p
        src = self.at(m, p.d) if src is None else src
        super().spread(m, src)
        self.send(src, m, p.d, self.sx.at[4 + m], (p.dxy, p.z))

    def x_in(self, m):
        self.take(m, self.p.dx)
        self.send(self.at(m, self.p.dx), m, self.p.dx, self.sc.at[4 + m], self.p.core)

    def y_in(self, m):
        self.take(m, self.p.dy)
        self.send(self.at(m, self.p.dy), m, self.p.dy, self.sc.at[8 + m], self.p.core)

    def second(self, m):
        return self.sx.at[4 + m]


def gather_sems():
    dma = pltpu.SemaphoreType.DMA
    return [dma((4,)), dma((4,)), dma((8,)), dma((8,)), dma((16,)), dma((4, 8))]


def lanes(shape, width):
    return lax.div(lax.broadcasted_iota(jnp.int32, shape, 1), width)


def turned(x, cosine, sine):
    first = lax.rem(lanes(x.shape, 32), 2) == 0
    width = x.shape[1]
    other = jnp.where(first, pltpu.roll(x, width - 32, 1), pltpu.roll(x, 32, 1))
    return x * cosine + other * sine


def wide(table):
    return jnp.concatenate([table, table], axis=1)


def dot(a, b):
    return lax.dot_general(a, b, (((1,), (0,)), ((), ())), preferred_element_type=F32)


def dot_nt(a, b):
    return lax.dot_general(a, b, (((1,), (1,)), ((), ())), preferred_element_type=F32)


def dot_tn(a, b):
    return lax.dot_general(a, b, (((0,), (0,)), ((), ())), preferred_element_type=F32)


def tile_scores(q_head, keys, tile, packed):
    n = (tile + 1) * CHUNK
    s = dot_nt(q_head, keys) * 0.125
    rows = lax.broadcasted_iota(jnp.int32, (CHUNK, n), 0) + tile * CHUNK
    cols = lax.broadcasted_iota(jnp.int32, (CHUNK, n), 1)
    allowed = cols <= rows
    if tile >= 2:
        allowed = allowed & ((packed != 2) | (cols >= 2 * CHUNK))
    return jnp.where(allowed, s, -1e30)


ORDER = (3, 0, 1, 2)


def add_rows(dst, terms, step):
    def rows(r, carry):
        at = pl.ds(pl.multiple_of(r * step, step), step)
        total = terms[0][at, :].astype(F32)
        for term in terms[1:]:
            total = total + term[at, :].astype(F32)
        dst[at, :] = total.astype(dst.dtype)
        return carry

    lax.fori_loop(0, dst.shape[0] // step, rows, 0)


def spans(n, step):
    return [(at, min(step, n - at)) for at in range(0, n, step)]


def block(i):
    return pl.ds(pl.multiple_of(i * CHUNK, CHUNK), CHUNK)


class Moves:
    def __init__(self, sems):
        self.sems, self.made = sems, []

    def start(self, src, dst):
        copy = pltpu.make_async_copy(src, dst, self.sems.at[len(self.made)])
        copy.start()
        self.made.append(copy)
        return len(self.made) - 1

    def wait(self, i):
        self.made[i].wait()
        self.made[i] = self.made[i], True

    def rest(self):
        for copy in self.made:
            if not isinstance(copy, tuple):
                copy.wait()


class Crossing:
    def __init__(self, place, part, bufs, sems, out, step):
        self.p, self.part, self.out, self.step = place, part, out, step
        self.acc, self.corner, self.bx, self.by = bufs
        (self.s_core, self.r_core, self.s_corner, self.r_corner,
         self.s_x, self.r_x, self.s_y, self.r_y) = sems

    def core_copy(self, m, q):
        p = self.p
        return remote(
            self.part(m, p.core_quads[q]), self.acc.at[m, q],
            self.s_core.at[m, q], self.r_core.at[m, q], p.core,
        )

    def begin(self, m):
        for q in (3, 1, 2, 0):
            self.core_copy(m, q).start()

    def corner_copy(self, m):
        to = self.p.x if m % 2 == 0 else self.p.y
        return remote(self.acc.at[m, 3], self.corner.at[m], self.s_corner.at[m], self.r_corner.at[m], to)

    def x_copy(self, m):
        return remote(self.acc.at[m, 1], self.bx.at[m], self.s_x.at[m], self.r_x.at[m], self.p.x)

    def y_copy(self, m):
        return remote(self.acc.at[m, 2], self.by.at[m], self.s_y.at[m], self.r_y.at[m], self.p.y)

    def join(self, m):
        first = 1 if m % 2 == 0 else 2
        for q in (3, first, 3 - first, 0):
            self.core_copy(m, q).wait_recv()
            add_rows(self.acc.at[m, q], [self.acc.at[m, q], self.part(m, self.p.quads[q])], self.step)
            if q == 3:
                self.corner_copy(m).start()
            if q == first:
                (self.x_copy if m % 2 == 0 else self.y_copy)(m).start()

    def relay(self, m):
        q = 2 if m % 2 == 0 else 1
        self.corner_copy(m).wait_recv()
        add_rows(self.acc.at[m, q], [self.acc.at[m, q], self.corner.at[m]], self.step)
        (self.y_copy if m % 2 == 0 else self.x_copy)(m).start()

    def total(self, m):
        self.x_copy(m).wait_recv()
        self.y_copy(m).wait_recv()
        add_rows(self.out.at[m], [self.acc.at[m, 0], self.bx.at[m], self.by.at[m]], self.step)

    def core_sent(self, m):
        for q in range(4):
            self.core_copy(m, q).wait_send()

    def finish(self):
        for m in range(4):
            self.corner_copy(m).wait_send()
            self.x_copy(m).wait_send()
            self.y_copy(m).wait_send()


def crossing_scratch(rows, width):
    def buf(*lead):
        return pltpu.VMEM((*lead, rows, width), BF)

    dma = pltpu.SemaphoreType.DMA
    return [buf(4, 4), buf(4), buf(4), buf(4), dma((4, 4)), dma((4, 4))] + [dma((4,))] * 6


class Chain:
    def __init__(self, place, part, bufs, sems, out, step):
        self.p, self.part, self.out, self.step = place, part, out, step
        self.br, self.bl = bufs
        self.s_r, self.r_r, self.s_l, self.r_l = sems

    def r_copy(self, m):
        p = self.p
        return remote(self.part.at[m], self.br.at[m], self.s_r.at[m], self.r_r.at[m], (p.d, p.z + 1))

    def l_copy(self, m):
        p = self.p
        return remote(self.part.at[m], self.bl.at[m], self.s_l.at[m], self.r_l.at[m], (p.d, p.z - 1))

    def level(self, k):
        @pl.when(self.p.z == k)
        def _():
            for m in range(3, k, -1):
                if k > 0:
                    self.r_copy(m).wait_recv()
                    add_rows(self.part.at[m], [self.part.at[m], self.br.at[m]], self.step)
                self.r_copy(m).start()

        @pl.when(self.p.z == 3 - k)
        def _():
            for m in range(0, 3 - k):
                if k > 0:
                    self.l_copy(m).wait_recv()
                    add_rows(self.part.at[m], [self.part.at[m], self.bl.at[m]], self.step)
                self.l_copy(m).start()

    def last(self):
        for m in range(4):

            @pl.when(self.p.z == m)
            def _():
                terms = [self.part.at[m]]
                if m > 0:
                    self.r_copy(m).wait_recv()
                    terms.append(self.br.at[m])
                if m < 3:
                    self.l_copy(m).wait_recv()
                    terms.append(self.bl.at[m])
                add_rows(self.out, terms, self.step)

    def finish(self):
        for m in range(4):
            if m > 0:

                @pl.when(self.p.z < m)
                def _():
                    self.r_copy(m).wait_send()

            if m < 3:

                @pl.when(self.p.z > m)
                def _():
                    self.l_copy(m).wait_send()


def chain_scratch(rows, width):
    dma = pltpu.SemaphoreType.DMA
    return [pltpu.VMEM((4, rows, width), BF)] * 2 + [dma((4,))] * 4


def forward_kernel(
    seq, wq, wk, wv, wo_own, wg_t, wu_t, wd_t, gain_attn, gain_mlp, cos_t, sin_t, tok_in, fv_in, cot_in,
    f2, acts, f1_out, qkv_out, o_out, lse_out, rows_out, a1t_out, a2_out, dattn_out, mid_out, layer_out, do_out, do_last, gain_part,
    tok, fv, cot, f1, qkv, o_head, lse, o_rows, a1_t, a1, stage, p2, w, wo, a2, mid, y_out, acc, back, act, dattn, do_rows, do_head, *sems,
):
    p = Place()
    sems = list(sems)
    g1s, g2s = sems[:6], sems[6:12]
    s_qkv, r_qkv, s_o, r_o, s_local, s_do, r_do, w_sems, wo_sems, act_sems, move_sems = sems[12:]
    moves = Moves(move_sems)
    z, d = p.z, p.d
    got_tok = moves.start(tok_in, tok)
    got_fv = moves.start(fv_in, fv)
    got_cot = moves.start(cot_in, cot)
    p.greet()

    f1[z, d, 0:128] = wq[...]
    f1[z, d, 128:256] = wk[...]
    f1[z, d, 256:384] = wv[...]
    f1[z, d, 384:400, 0:128] = jnp.broadcast_to(gain_attn[...], (16, 128))
    f1[z, d, 384:400, 128:256] = jnp.broadcast_to(gain_mlp[...], (16, 128))
    g1 = Gather(p, lambda m, e: f1.at[m, e], f1.at[0, 0], g1s)
    g2 = Direct(p, lambda m, e: f2.at[m, e], p2, g2s)
    g1.along_z(z)
    g1.spread(z)
    for i, source in enumerate((wg_t, wu_t, wd_t)):
        p2[i * FFC : (i + 1) * FFC, :] = source[...]
    p2[3 * FFC :, :] = wo_own[...].T
    own_copy = pltpu.make_async_copy(p2, f2.at[z, d], s_local)
    own_copy.start()

    def arrive(g):
        def visit(m):
            g.z_in(m)
            g.spread(m)
        return visit

    def side(g):
        def visit(m):
            g.x_in(m)
            g.y_in(m)
        return visit

    p.hop(1, arrive(g1))
    side(g1)(z)
    p.hop(2, arrive(g1))
    g2.along_z(z, p2)
    p.hop(1, side(g1))
    g1.diag_in(z)
    p.hop(3, arrive(g1))
    g1.core_in(z)

    gain_row = jnp.concatenate([f1[z, e, 384:400, :].astype(F32)[0:8] for e in range(8)], axis=1)
    gain_two = jnp.concatenate([gain_row[0:1, e * 256 + 128 : e * 256 + 256] for e in range(8)], axis=1)
    moves.wait(got_tok)

    def norm_body(b, carry):
        x = tok[b].astype(F32)
        factor = lax.rsqrt(jnp.mean(x * x, axis=1, keepdims=True) + EPSILON)
        for e in range(8):
            cols = slice(e * 128, (e + 1) * 128)
            a1[pl.ds(pl.multiple_of(b * CHUNK, CHUNK), CHUNK), cols] = (
                x[:, cols] * factor * gain_row[0:1, e * 256 : e * 256 + 128]
            ).astype(BF)
        return carry

    lax.fori_loop(0, 3, norm_body, 0)

    p.hop(2, side(g1))
    p.hop(1, g1.diag_in)
    p.hop(3, side(g1))
    g2.spread(z, p2)
    p.hop(2, g1.diag_in)
    p.hop(1, g2.z_in)
    p.hop(1, g1.core_in)
    p.hop(3, g1.diag_in)
    p.hop(2, g1.core_in)
    p.hop(3, g1.core_in)
    p.hop(1, g2.spread)
    moves.start(f1, f1_out)
    moves.wait(got_fv)

    def project(b):
        pos_full = pl.ds(pl.multiple_of(z * CHUNK, CHUNK), CHUNK)
        low = jnp.where(z >= 2, z - 2, z)
        pos_half = pl.ds(pl.multiple_of(low * CHUNK, CHUNK), CHUNK)
        second = seq[b] == 2
        cosine = wide(jnp.where(second, cos_t[pos_half, :], cos_t[pos_full, :]))
        sine = wide(jnp.where(second, sin_t[pos_half, :], sin_t[pos_full, :]))
        rows = a1[b * CHUNK : (b + 1) * CHUNK, :]

        def one(step, carry):
            m = lax.rem(z + step, 4)
            w = lambda i: f1[m, :, i * 128 : (i + 1) * 128, :].reshape(1024, CHUNK)
            stage[b, m, 0] = turned(dot(rows, w(0)), cosine, sine).astype(BF)
            stage[b, m, 1] = turned(dot(rows, w(1)), cosine, sine).astype(BF)
            first = fv[b, :, pl.ds(pl.multiple_of(m * CHUNK, CHUNK), CHUNK)].astype(F32)
            stage[b, m, 2] = (0.5 * (dot(rows, w(2)) + first)).astype(BF)
            return carry

        lax.fori_loop(0, 4, one, 0)
        for i in range(3):
            qkv[b, i, block(z), :] = stage[b, z, i]

    def qkv_copy(b, step):
        m = p.peer(step)
        dst = qkv.at[b, :, pl.ds(pl.multiple_of(z * CHUNK, CHUNK), CHUNK), :]
        return remote(stage.at[b, m], dst, s_qkv.at[b, step - 1], r_qkv.at[b, z], (d, m))

    def send_qkv(b):
        for step in (1, 2, 3):
            qkv_copy(b, step).start()

    def sent_qkv(b):
        for step in (1, 2, 3):
            qkv_copy(b, step).wait_send()

    def take_qkv(b):
        for step in (1, 2, 3):
            m = p.peer(step)
            dst = qkv.at[b, :, pl.ds(pl.multiple_of(m * CHUNK, CHUNK), CHUNK), :]
            remote(stage.at[b, m], dst, s_qkv.at[b, 0], r_qkv.at[b, m], (d, m)).wait_recv()

    def o_copy(b, i):
        rows = slice(i * CHUNK, (i + 1) * CHUNK)
        return remote(o_head.at[b, rows, :], o_rows.at[b, z], s_o.at[b, i], r_o.at[b, z], (d, i))

    def attend(b, i):
        n = (i + 1) * CHUNK
        rows = slice(i * CHUNK, n)
        packed = seq[b]
        q = qkv[b, 0, rows, :]
        keys = qkv[b, 1, 0:n, :]
        values = qkv[b, 2, 0:n, :]
        head_of = lanes((CHUNK, CHUNK), 64)
        lane = lax.broadcasted_iota(jnp.int32, (CHUNK, 128), 1)

        def head(h, carry):
            out, stats = carry
            s = tile_scores(jnp.where(head_of == h, q, jnp.zeros_like(q)), keys, i, packed)
            top = jnp.max(s, axis=1, keepdims=True)
            e = jnp.exp(s - top)
            total = jnp.sum(e, axis=1, keepdims=True)
            part = dot(e.astype(BF), values) * (1.0 / total)
            return (
                jnp.where(head_of == h, part, out),
                jnp.where(lane == h, top + jnp.log(total), stats),
            )

        out, stats = lax.fori_loop(
            0, 4, head, (jnp.zeros((CHUNK, CHUNK), F32), jnp.zeros((CHUNK, 128), F32))
        )
        o_head[b, rows, :] = out.astype(BF)
        lse[b, rows, :] = stats

        @pl.when(z == i)
        def _():
            o_rows[b, z] = out.astype(BF)

        @pl.when(z != i)
        def _():
            o_copy(b, i).start()

    def take_o(b):
        for step in (1, 2, 3):
            m = p.peer(step)
            remote(o_rows.at[b, m], o_rows.at[b, m], s_o.at[b, 0], r_o.at[b, m], (d, m)).wait_recv()

    def w_copy(t, e):
        m, slot = lax.rem(t, 4), lax.rem(t, 2)
        return pltpu.make_async_copy(
            f2.at[m, e, 0 : 3 * FFC, :], w.at[slot, :, e * 128 : (e + 1) * 128], w_sems.at[slot, e]
        )

    def wo_copy(m, e):
        return pltpu.make_async_copy(
            f2.at[m, e, 3 * FFC :, :], wo.at[m, :, e * 128 : (e + 1) * 128], wo_sems.at[m, e]
        )

    def act_copy(b, m, slot):
        return pltpu.make_async_copy(
            act.at[slot], acts.at[:, m, b * CHUNK : (b + 1) * CHUNK, :], act_sems.at[slot]
        )

    def load_mlp():
        for m in range(4):
            for e in range(8):
                wo_copy(m, e).start()
        for e in range(8):
            w_copy(0, e).start()
        for m in range(4):
            for e in range(8):
                wo_copy(m, e).wait()

    def do_copy(b, step):
        m = p.peer(step)
        return remote(
            do_rows.at[b, m], do_head.at[b, block(z), :], s_do.at[b, step - 1], r_do.at[b, z], (d, m)
        )

    def send_do(b):
        for step in (1, 2, 3):
            do_copy(b, step).start()
        do_head[b, block(z), :] = do_rows[b, z]

    def mlp_rows(b):
        rows = slice(b * CHUNK, (b + 1) * CHUNK)
        x2 = tok[b].astype(F32)
        for m in range(4):
            x2 = x2 + dot(o_rows[b, m], wo[m])
        factor = lax.rsqrt(jnp.mean(x2 * x2, axis=1, keepdims=True) + EPSILON)
        mid[b] = x2
        a2[rows, :] = (x2 * factor * gain_two).astype(BF)

        def chunk(m, carry):
            t = b * 4 + m
            slot = lax.rem(m, 2)
            for e in range(8):
                w_copy(t, e).wait()

            @pl.when(t < 11)
            def _():
                for e in range(8):
                    w_copy(t + 1, e).start()

            @pl.when(t >= 2)
            def _():
                act_copy(b, m, slot).wait()

            for at, size in spans(FFC, 256):
                cols = slice(at, at + size)
                gate = dot_nt(a2[rows, :], w[slot, at : at + size, :])
                up = dot_nt(a2[rows, :], w[slot, FFC + at : FFC + at + size, :])
                dh = dot_nt(cot[b], w[slot, 2 * FFC + at : 2 * FFC + at + size, :])
                sg = jax.nn.sigmoid(gate)
                silu = gate * sg
                act[slot, 0, :, cols] = (dh * up * (sg + silu * (1.0 - sg))).astype(BF)
                act[slot, 1, :, cols] = (dh * silu).astype(BF)
                act[slot, 2, :, cols] = (silu * up).astype(BF)
            for at, size in spans(1024, 256):
                cols = slice(at, at + size)
                y = dot(act[slot, 2], w[slot, 2 * FFC : 3 * FFC, cols])
                u = dot(act[slot, 0], w[slot, 0:FFC, cols]) + dot(act[slot, 1], w[slot, FFC : 2 * FFC, cols])
                acc[:, cols] = jnp.where(m == 0, y, acc[:, cols] + y)
                back[:, cols] = jnp.where(m == 0, u, back[:, cols] + u)
            act_copy(b, m, slot).start()
            return carry

        lax.fori_loop(0, 4, chunk, 0)
        x2 = mid[b]
        y_out[b] = (x2 + acc[...]).astype(BF)
        factor = lax.rsqrt(jnp.mean(x2 * x2, axis=1, keepdims=True) + EPSILON)
        n2 = x2 * factor
        da2 = back[...]
        sums = jnp.broadcast_to(jnp.sum(da2 * n2, axis=0, keepdims=True), (8, 1024))
        gain_part[...] = sums if b == 0 else gain_part[...] + sums
        dn2 = da2 * gain_two
        grad_mid = cot[b].astype(F32) + factor * (dn2 - n2 * jnp.mean(dn2 * n2, axis=1, keepdims=True))
        mid[b] = grad_mid
        dattn[rows, :] = grad_mid.astype(BF)

        def heads(m, carry):
            do_rows[b, m] = dot_nt(dattn[rows, :], wo[m]).astype(BF)
            return carry

        lax.fori_loop(0, 4, heads, 0)
        moves.start(mid.at[b], mid_out.at[b])
        moves.start(y_out.at[b], layer_out.at[b])

    def attend_all(b):
        for i in range(4):
            attend(b, i)
        moves.start(o_head.at[b], o_out.at[b])
        moves.start(lse.at[b], lse_out.at[b])

    project(0)
    send_qkv(0)
    p.hop(2, arrive(g2))
    project(1)
    project(2)
    a1_t[...] = a1[...].T
    moves.start(a1_t, a1t_out)
    p.hop(3, arrive(g2))
    send_qkv(1)
    side(g2)(z)
    take_qkv(0)
    moves.start(qkv.at[0], qkv_out.at[0])
    send_qkv(2)
    p.hop(1, side(g2))
    attend(0, 0)
    attend(0, 1)
    attend(0, 2)
    attend(0, 3)
    moves.start(o_head.at[0], o_out.at[0])
    moves.start(lse.at[0], lse_out.at[0])
    take_qkv(1)
    moves.start(qkv.at[1], qkv_out.at[1])
    attend(1, 0)
    attend(1, 1)
    g2.diag_in(z)
    attend(1, 2)
    attend(1, 3)
    p.hop(2, side(g2))
    moves.start(o_head.at[1], o_out.at[1])
    moves.start(lse.at[1], lse_out.at[1])
    p.hop(1, g2.diag_in)
    take_qkv(2)
    moves.start(qkv.at[2], qkv_out.at[2])
    attend(2, 0)
    attend(2, 1)
    p.hop(2, g2.diag_in)
    attend(2, 2)
    attend(2, 3)
    p.hop(3, side(g2))
    moves.start(o_head.at[2], o_out.at[2])
    moves.start(lse.at[2], lse_out.at[2])
    p.hop(3, g2.diag_in)
    for m in range(4):
        g2.core_in(m)
    own_copy.wait()
    load_mlp()
    moves.wait(got_cot)
    take_o(0)
    mlp_rows(0)
    send_do(0)
    take_o(1)
    mlp_rows(1)
    send_do(1)
    take_o(2)
    moves.start(o_rows, rows_out)
    mlp_rows(2)
    moves.start(a2, a2_out)
    moves.start(dattn, dattn_out)
    moves.start(do_rows.at[2], do_last)
    for b in range(2):
        for step in (1, 2, 3):
            m = p.peer(step)
            dst = do_head.at[b, block(m), :]
            remote(do_rows.at[b, m], dst, s_do.at[b, 0], r_do.at[b, m], (d, m)).wait_recv()
            do_copy(b, step).wait_send()
        moves.start(do_head.at[b], do_out.at[b])
    act_copy(2, 2, 0).wait()
    act_copy(2, 3, 1).wait()
    sent_qkv(0)
    sent_qkv(1)
    sent_qkv(2)
    for b in range(3):
        for i in range(4):

            @pl.when(z != i)
            def _():
                o_copy(b, i).wait_send()

    g1.finish()
    g2.finish()
    moves.rest()


def run_forward(*args):
    vmem = pl.BlockSpec(memory_space=pltpu.VMEM)
    hbm = pl.BlockSpec(memory_space=pl.ANY)
    dma = pltpu.SemaphoreType.DMA
    shape = jax.ShapeDtypeStruct
    return pl.pallas_call(
        forward_kernel,
        out_shape=(
            shape((4, 8, PIECE, 128), BF),
            shape((3, 4, 768, FFC), BF),
            shape((4, 8, QROWS, CHUNK), BF),
            shape((3, 3, 1024, CHUNK), BF),
            shape((3, 1024, CHUNK), BF),
            shape((3, 1024, 128), F32),
            shape((3, 4, CHUNK, CHUNK), BF),
            shape((1024, 768), BF),
            shape((768, 1024), BF),
            shape((768, 1024), BF),
            shape((3, CHUNK, 1024), F32),
            shape((3, CHUNK, 1024), BF),
            shape((2, 1024, CHUNK), BF),
            shape((4, CHUNK, CHUNK), BF),
            shape((8, 1024), F32),
        ),
        in_specs=[pl.BlockSpec(memory_space=pltpu.SMEM)] + [vmem] * 11 + [hbm] * 3,
        out_specs=(hbm,) * 14 + (vmem,),
        scratch_shapes=[
            pltpu.VMEM((3, CHUNK, 1024), BF),
            pltpu.VMEM((3, CHUNK, 1024), BF),
            pltpu.VMEM((3, CHUNK, 1024), BF),
            pltpu.VMEM((4, 8, QROWS, CHUNK), BF),
            pltpu.VMEM((3, 3, 1024, CHUNK), BF),
            pltpu.VMEM((3, 1024, CHUNK), BF),
            pltpu.VMEM((3, 1024, 128), F32),
            pltpu.VMEM((3, 4, CHUNK, CHUNK), BF),
            pltpu.VMEM((1024, 768), BF),
            pltpu.VMEM((768, 1024), BF),
            pltpu.VMEM((3, 4, 3, CHUNK, CHUNK), BF),
            pltpu.VMEM((PIECE, 128), BF),
            pltpu.VMEM((2, 3 * FFC, 1024), BF),
            pltpu.VMEM((4, CHUNK, 1024), BF),
            pltpu.VMEM((768, 1024), BF),
            pltpu.VMEM((3, CHUNK, 1024), F32),
            pltpu.VMEM((3, CHUNK, 1024), BF),
            pltpu.VMEM((CHUNK, 1024), F32),
            pltpu.VMEM((CHUNK, 1024), F32),
            pltpu.VMEM((2, 3, CHUNK, FFC), BF),
            pltpu.VMEM((768, 1024), BF),
            pltpu.VMEM((3, 4, CHUNK, CHUNK), BF),
            pltpu.VMEM((2, 1024, CHUNK), BF),
        ]
        + gather_sems()
        + gather_sems()
        + [dma((3, 3)), dma((3, 4)), dma((3, 4)), dma((3, 4)), dma, dma((3, 3)), dma((3, 4))]
        + [dma((2, 8)), dma((4, 8)), dma((2,)), dma((32,))],
        compiler_params=pltpu.CompilerParams(
            collective_id=1, has_side_effects=True, vmem_limit_bytes=62 * 2**20
        ),
        cost_estimate=pl.CostEstimate(flops=5 * 10**10, bytes_accessed=6 * 10**7, transcendentals=8 * 10**6),
        name="gather_forward",
    )(*args)


def backward_kernel(
    seq, cos_t, sin_t, do_last, do_in, qkv_in, o_in, lse_in, rows_in, a2_in, dattn_in, cot_in, acts,
    d_rows, summed,
    do_mine, do_head, qkv, o_head, lse, o_rows, a2, dattn, cot, act, part, total, dk, dv, stage, *rest,
):
    p = Place()
    s_do, r_do, s_d, r_d, act_sems, move_sems = rest[:6]
    z, d = p.z, p.d
    moves = Moves(move_sems)
    got = []
    for b in range(3):
        got.append(
            [moves.start(qkv_in.at[b], qkv.at[b]), moves.start(o_in.at[b], o_head.at[b]), moves.start(lse_in.at[b], lse.at[b])]
            + ([moves.start(do_in.at[b], do_head.at[b])] if b < 2 else [])
        )
        if b == 0:
            got_do = moves.start(do_last, do_mine)
            got_w = [
                moves.start(a2_in, a2), moves.start(dattn_in, dattn), moves.start(cot_in, cot),
                moves.start(rows_in, o_rows),
            ]
    p.greet()

    def act_copy(m, slot):
        return pltpu.make_async_copy(acts.at[:, m], act.at[slot], act_sems.at[slot])

    act_copy(ORDER[0], 0).start()
    moves.wait(got_do)

    def do_copy(step):
        m = p.peer(step)
        return remote(do_mine.at[m], do_head.at[2, block(z), :], s_do.at[step - 1], r_do.at[z], (d, m))

    for step in (1, 2, 3):
        do_copy(step).start()
    do_head[2, block(z), :] = do_mine[z]

    def take_do():
        for step in (1, 2, 3):
            m = p.peer(step)
            dst = do_head.at[2, block(m), :]
            remote(do_mine.at[m], dst, s_do.at[0], r_do.at[m], (d, m)).wait_recv()

    def d_copy(b, i):
        return remote(stage.at[b, i], d_rows.at[b, z], s_d.at[b, i], r_d.at[b, z], (d, i))

    def own_copy(b, i):
        return pltpu.make_async_copy(stage.at[b, i], d_rows.at[b, i], s_d.at[b, i])

    def back(b, i):
        n = (i + 1) * CHUNK
        rows = slice(i * CHUNK, n)
        packed = seq[b]
        head_of = lanes((CHUNK, CHUNK), 64)
        lane = lax.broadcasted_iota(jnp.int32, (CHUNK, 128), 1)
        q = qkv[b, 0, rows, :]
        keys = qkv[b, 1, 0:n, :]
        values = qkv[b, 2, 0:n, :]
        grad = do_head[b, rows, :]
        spread = grad.astype(F32) * o_head[b, rows, :].astype(F32)
        stats = lse[b, rows, :]

        def head(h, dq):
            here = head_of == h
            q_h = jnp.where(here, q, jnp.zeros_like(q))
            g_h = jnp.where(here, grad, jnp.zeros_like(grad))
            delta = jnp.sum(jnp.where(here, spread, 0.0), axis=1, keepdims=True)
            level = jnp.sum(jnp.where(lane == h, stats, 0.0), axis=1, keepdims=True)
            prob = jnp.exp(tile_scores(q_h, keys, i, packed) - level)
            dp = dot_nt(g_h, values)
            ds = (prob * (dp - delta)).astype(BF)
            dv_part = dot_tn(prob.astype(BF), g_h)
            dk_part = dot_tn(ds, q_h)
            dv[0:n, :] += dv_part
            dk[0:n, :] += dk_part
            return jnp.where(here, dot(ds, keys), dq)

        dq = lax.fori_loop(0, 4, head, jnp.zeros((CHUNK, CHUNK), F32))
        cosine, sine = cos_t[rows, :], sin_t[rows, :]
        if i >= 2:
            early = slice((i - 2) * CHUNK, (i - 1) * CHUNK)
            cosine = jnp.where(packed == 2, cos_t[early, :], cosine)
            sine = jnp.where(packed == 2, sin_t[early, :], sine)
        cosine, sine = wide(cosine), -wide(sine)
        stage[b, i, :, 0:256] = turned(dq * 0.125, cosine, sine).astype(BF)
        stage[b, i, :, 256:512] = turned(dk[rows, :] * 0.125, cosine, sine).astype(BF)
        stage[b, i, :, 512:768] = (dv[rows, :] * 0.5).astype(BF)

        @pl.when(z == i)
        def _():
            own_copy(b, i).start()

        @pl.when(z != i)
        def _():
            d_copy(b, i).start()

    def back_all(b):
        for i in got[b]:
            moves.wait(i)
        dk[...] = jnp.zeros_like(dk)
        dv[...] = jnp.zeros_like(dv)
        for i in (3, 2, 1, 0):
            back(b, i)

    crossing = Crossing(p, lambda m, e: part.at[ORDER.index(m) % 2, e], rest[6:10], rest[10:], total, 592)

    def weight_grad(k):
        m, slot = ORDER[k], k % 2
        act_copy(m, slot).wait()
        if k < 3:
            act_copy(ORDER[k + 1], 1 - slot).start()
        if k >= 2:
            crossing.core_sent(ORDER[k - 2])

        for i in range(3):
            right = cot[...].reshape(768, 1024) if i == 2 else a2[...]
            for at, size in spans(FFC, 256):
                out = dot_tn(act[slot, i, :, at : at + size], right).astype(BF)
                for e in range(8):
                    part[slot, e, i * FFC + at : i * FFC + at + size, :] = out[:, e * 128 : (e + 1) * 128]
        own = jnp.concatenate([o_rows[b, m] for b in range(3)], axis=0)
        out = dot_tn(own, dattn[...]).astype(BF)
        for e in range(8):
            part[slot, e, 3 * FFC :, :] = out[:, e * 128 : (e + 1) * 128]
        crossing.begin(m)

    a, b_, c, e_ = ORDER
    back_all(0)
    for i in got_w:
        moves.wait(i)
    weight_grad(0)
    weight_grad(1)
    crossing.join(a)
    crossing.join(b_)
    back_all(1)
    weight_grad(2)
    weight_grad(3)
    crossing.relay(a)
    crossing.relay(b_)
    take_do()
    back_all(2)
    crossing.join(c)
    crossing.join(e_)
    crossing.total(a)
    crossing.total(b_)
    crossing.relay(c)
    crossing.relay(e_)
    crossing.total(c)
    crossing.total(e_)
    moves.start(total, summed)
    crossing.core_sent(c)
    crossing.core_sent(e_)
    crossing.finish()
    for step in (1, 2, 3):
        do_copy(step).wait_send()
    for b in range(3):
        for step in (1, 2, 3):
            m = p.peer(step)
            remote(stage.at[b, m], d_rows.at[b, m], s_d.at[b, 0], r_d.at[b, m], (d, m)).wait_recv()
        for i in range(4):

            @pl.when(z == i)
            def _():
                own_copy(b, i).wait()

            @pl.when(z != i)
            def _():
                d_copy(b, i).wait_send()

    moves.rest()


def run_backward(*args):
    vmem = pl.BlockSpec(memory_space=pltpu.VMEM)
    hbm = pl.BlockSpec(memory_space=pl.ANY)
    dma = pltpu.SemaphoreType.DMA
    shape = jax.ShapeDtypeStruct
    return pl.pallas_call(
        backward_kernel,
        out_shape=(shape((3, 4, CHUNK, 768), BF), shape((4, PIECE, 128), BF)),
        in_specs=[pl.BlockSpec(memory_space=pltpu.SMEM)] + [vmem] * 2 + [hbm] * (len(args) - 3),
        out_specs=(hbm, hbm),
        scratch_shapes=[
            pltpu.VMEM((4, CHUNK, CHUNK), BF),
            pltpu.VMEM((3, 1024, CHUNK), BF),
            pltpu.VMEM((3, 3, 1024, CHUNK), BF),
            pltpu.VMEM((3, 1024, CHUNK), BF),
            pltpu.VMEM((3, 1024, 128), F32),
            pltpu.VMEM((3, 4, CHUNK, CHUNK), BF),
            pltpu.VMEM((768, 1024), BF),
            pltpu.VMEM((768, 1024), BF),
            pltpu.VMEM((3, CHUNK, 1024), BF),
            pltpu.VMEM((2, 3, 768, FFC), BF),
            pltpu.VMEM((2, 8, PIECE, 128), BF),
            pltpu.VMEM((4, PIECE, 128), BF),
            pltpu.VMEM((1024, CHUNK), F32),
            pltpu.VMEM((1024, CHUNK), F32),
            pltpu.VMEM((3, 4, CHUNK, 768), BF),
            dma((3,)),
            dma((4,)),
            dma((3, 4)),
            dma((3, 4)),
            dma((2,)),
            dma((32,)),
        ]
        + crossing_scratch(PIECE, 128),
        compiler_params=pltpu.CompilerParams(
            collective_id=2, has_side_effects=True, vmem_limit_bytes=63 * 2**20
        ),
        cost_estimate=pl.CostEstimate(flops=4 * 10**10, bytes_accessed=4 * 10**7, transcendentals=8 * 10**6),
        name="attend_back",
    )(*args)


def finish_kernel(
    gain_part, tok_in, mid_in, d_rows_in, a1t_in, f1_in, summed,
    grad_tokens, grad_first, dw1, dw2, gain_sum,
    tok, mid, d_rows, a1_t, f1, grad, first, part, acc, total1, total2, gbuf, *rest,
):
    p = Place()
    rest = list(rest)
    cross = Crossing(p, lambda m, e: part.at[m, e], rest[:4], rest[4:12], total1, 16)
    chain1 = Chain(p, total1, rest[12:14], rest[14:18], dw1, 16)
    chain2 = Chain(p, total2, rest[18:20], rest[20:24], dw2, 592)
    s_gain, r_gain, move_sems = rest[24:27]
    moves = Moves(move_sems)
    got_total = moves.start(summed, total2)
    got_d = [moves.start(d_rows_in, d_rows), moves.start(a1t_in, a1_t)]
    got_f1 = moves.start(f1_in, f1)
    got_x = [moves.start(tok_in, tok), moves.start(mid_in, mid)]
    p.greet()

    def weight_grad(m):
        cols = jnp.concatenate([d_rows[b, m] for b in range(3)], axis=0)

        def rows(k, carry):
            at = pl.ds(pl.multiple_of(k * CHUNK, CHUNK), CHUNK)
            part[m, pl.ds(2 * k, 2)] = dot(a1_t[at, :], cols).astype(BF).reshape(2, 128, 768)
            return carry

        lax.fori_loop(0, 4, rows, 0)

    def input_grad(m):
        cols = jnp.concatenate([d_rows[b, m] for b in range(3)], axis=0)

        def tile(k, carry):
            w = jnp.concatenate(
                [f1[m, pl.ds(2 * k, 2), i * 128 : (i + 1) * 128, :].reshape(CHUNK, CHUNK) for i in range(3)],
                axis=1,
            )
            at = pl.ds(pl.multiple_of(k * CHUNK, CHUNK), CHUNK)
            y = dot_nt(cols, w)
            if m == 0:
                acc[:, at] = y
            else:
                acc[:, at] += y
            return carry

        lax.fori_loop(0, 4, tile, 0)

    def leave(b, total):
        x = tok[b].astype(F32)
        factor = lax.rsqrt(jnp.mean(x * x, axis=1, keepdims=True) + EPSILON)
        n1 = x * factor
        da1 = acc[pl.ds(pl.multiple_of(b * CHUNK, CHUNK), CHUNK), :]
        total = total + jnp.sum(da1 * n1, axis=0, keepdims=True)
        gain = jnp.concatenate([f1[0, e, 384:400, 0:128].astype(F32)[0:1] for e in range(8)], axis=1)
        dn1 = da1 * gain
        grad[b] = mid[b] + factor * (dn1 - n1 * jnp.mean(dn1 * n1, axis=1, keepdims=True))
        for m in range(4):
            first[b, :, m * CHUNK : (m + 1) * CHUNK] = d_rows[b, m, :, 512:768].astype(F32)
        return total

    def gain_copy(i, device):
        return remote(gbuf.at[0] if i == 0 else gbuf.at[4 + i], gbuf.at[1 + i], s_gain.at[i], r_gain.at[i], device)

    a, b, c, e = ORDER
    moves.wait(got_total)
    chain2.level(0)
    for i in got_d:
        moves.wait(i)
    for m in ORDER:
        weight_grad(m)
        cross.begin(m)
    cross.join(a)
    cross.join(b)
    cross.join(c)
    cross.join(e)
    chain2.level(1)
    cross.relay(a)
    cross.relay(b)
    moves.wait(got_f1)
    input_grad(0)
    cross.relay(c)
    cross.relay(e)
    input_grad(1)
    cross.total(a)
    cross.total(b)
    input_grad(2)
    chain2.level(2)
    input_grad(3)
    cross.total(c)
    cross.total(e)
    chain1.level(0)
    for i in got_x:
        moves.wait(i)
    total = lax.fori_loop(0, 3, leave, jnp.zeros((1, 1024), F32))
    moves.start(grad, grad_tokens)
    moves.start(first, grad_first)
    row = lax.broadcasted_iota(jnp.int32, (8, 1024), 0)
    gbuf[0] = jnp.where(row == 0, total, gain_part[...])
    gain_copy(0, p.core).start()
    chain1.level(1)
    gain_copy(0, p.core).wait_recv()
    gbuf[5] = gbuf[0] + gbuf[1]
    gain_copy(1, p.x).start()
    chain2.last()
    gain_copy(1, p.x).wait_recv()
    gbuf[6] = gbuf[5] + gbuf[2]
    gain_copy(2, p.y).start()
    chain1.level(2)
    gain_copy(2, p.y).wait_recv()
    gbuf[7] = gbuf[6] + gbuf[3]
    for step in (1, 2, 3):
        m = p.peer(step)
        remote(gbuf.at[7], gbuf.at[8 + p.z], s_gain.at[2 + step], r_gain.at[3 + p.z], (p.d, m)).start()
    gbuf[8 + p.z] = gbuf[7]
    chain1.last()
    for step in (1, 2, 3):
        m = p.peer(step)
        remote(gbuf.at[7], gbuf.at[8 + m], s_gain.at[2 + step], r_gain.at[3 + m], (p.d, m)).wait_recv()
    gain_sum[...] = (gbuf[8] + gbuf[9]) + (gbuf[10] + gbuf[11])
    for i, device in enumerate((p.core, p.x, p.y)):
        gain_copy(i, device).wait_send()
    for step in (1, 2, 3):
        m = p.peer(step)
        remote(gbuf.at[7], gbuf.at[8 + m], s_gain.at[2 + step], r_gain.at[3 + m], (p.d, m)).wait_send()
    for m in range(4):
        cross.core_sent(m)
    cross.finish()
    chain1.finish()
    chain2.finish()
    moves.rest()


def run_finish(*args):
    vmem = pl.BlockSpec(memory_space=pltpu.VMEM)
    hbm = pl.BlockSpec(memory_space=pl.ANY)
    dma = pltpu.SemaphoreType.DMA
    shape = jax.ShapeDtypeStruct
    return pl.pallas_call(
        finish_kernel,
        out_shape=(
            shape((3, CHUNK, 1024), F32),
            shape((3, CHUNK, 1024), F32),
            shape((128, 768), F32),
            shape((PIECE, 128), F32),
            shape((8, 1024), F32),
        ),
        in_specs=[vmem] + [hbm] * (len(args) - 1),
        out_specs=(hbm, hbm, vmem, vmem, vmem),
        scratch_shapes=[
            pltpu.VMEM((3, CHUNK, 1024), BF),
            pltpu.VMEM((3, CHUNK, 1024), F32),
            pltpu.VMEM((3, 4, CHUNK, 768), BF),
            pltpu.VMEM((1024, 768), BF),
            pltpu.VMEM((4, 8, QROWS, CHUNK), BF),
            pltpu.VMEM((3, CHUNK, 1024), F32),
            pltpu.VMEM((3, CHUNK, 1024), F32),
            pltpu.VMEM((4, 8, 128, 768), BF),
            pltpu.VMEM((768, 1024), F32),
            pltpu.VMEM((4, 128, 768), BF),
            pltpu.VMEM((4, PIECE, 128), BF),
            pltpu.VMEM((12, 8, 1024), F32),
        ]
        + crossing_scratch(128, 768)
        + chain_scratch(128, 768)
        + chain_scratch(PIECE, 128)
        + [dma((6,)), dma((7,)), dma((8,))],
        compiler_params=pltpu.CompilerParams(
            collective_id=3, has_side_effects=True, vmem_limit_bytes=62 * 2**20
        ),
        cost_estimate=pl.CostEstimate(flops=10**10, bytes_accessed=5 * 10**7, transcendentals=0),
        name="sum_grads",
    )(*args)


def fast_body(
    tokens, first_values, sequences, w_query, w_key, w_value, w_out, w_gate, w_up, w_down,
    gain_attn, gain_mlp, cotangent,
):
    seq = sequences[:, 0]
    cos_t, sin_t = rope_tables()
    (_, acts, f1, qkv, o_head, lse, o_rows, a1_t, a2, dattn, mid, layer_out, do_head, do_last, gain_part) = run_forward(
        seq, w_query, w_key, w_value, w_out, w_gate.T, w_up.T, w_down.T,
        gain_attn[None, :], gain_mlp[None, :], cos_t, sin_t, tokens, first_values, cotangent,
    )
    d_rows, summed = run_backward(
        seq, cos_t, sin_t, do_last, do_head, qkv, o_head, lse, o_rows, a2, dattn, cotangent, acts
    )
    grad_tokens, grad_first, dw1, dw2, gain_sum = run_finish(gain_part, tokens, mid, d_rows, a1_t, f1, summed)
    place = (lax.axis_index("dp") * 4 + lax.axis_index("mp")) * 32
    gain_mine = lax.dynamic_slice(gain_sum, (0, place), (2, 32))
    return (
        layer_out,
        grad_tokens,
        grad_first,
        dw1[:, 0:256],
        dw1[:, 256:512],
        dw1[:, 512:768],
        dw2[3 * FFC :].T,
        dw2[0:FFC].T,
        dw2[FFC : 2 * FFC].T,
        dw2[2 * FFC : 3 * FFC].T,
        gain_mine[0],
        gain_mine[1],
    )


def is_small(mesh):
    return mesh.axis_names == ("dp", "mp") and tuple(mesh.devices.shape) == (8, 4)


def solution(mesh):
    return jax.shard_map(
        fast_body if is_small(mesh) else body,
        mesh=mesh,
        in_specs=(
            P(None, ("dp", "mp"), None),
            P(None, ("dp", "mp"), None),
            P(None, "dp"),
            P("dp", "mp"),
            P("dp", "mp"),
            P("dp", "mp"),
            P("dp", "mp"),
            P("dp", "mp"),
            P("dp", "mp"),
            P("dp", "mp"),
            P("dp"),
            P("dp"),
            P(None, ("dp", "mp"), None),
        ),
        out_specs=(
            P(None, ("dp", "mp"), None),
            P(None, ("dp", "mp"), None),
            P(None, ("dp", "mp"), None),
            P("dp", "mp"),
            P("dp", "mp"),
            P("dp", "mp"),
            P("dp", "mp"),
            P("dp", "mp"),
            P("dp", "mp"),
            P("dp", "mp"),
            P(("dp", "mp")),
            P(("dp", "mp")),
        ),
        check_vma=False,
    )
```
